32 devices in a mesh: tile: 8 (over z, y), col: 4 (over x, core).
Axes of the slice: x: 2, y: 2, z: 4, core: 2. Of those that a mesh axis runs over, the one named last changes fastest.
Arguments:
- positions: float32 [3, 4096], P(None, 'tile'), may hold values from 0 to 640, as said below
- trial_block: float32 [3, 16, 4096], P(None, None, 'tile')
- pair_tiles: int32 [2, 8, 4, 8], P(None, 'tile'), may hold values from 0 to 31, as said below
- pair_count: int32 [8, 4], P('tile'), may hold values from 0 to 8, as said below
Outputs:
- next_block: float32 [3, 16, 4096], P(None, None, 'tile')
- rayleigh: float32 [16, 16], replicated
- correlation_norm: float32 [16, 16], replicated
- residual_norms: float32 [16], replicated
The draws below stay inside these ranges and needn't reach their ends.
Inputs may be any that keep to these rules, and one draw needn't show every extreme that they name: `positions`: tiles follow one another along the first component, in order of their numbers. `pair_tiles`: entry 1 lies between the row tile and two tiles past it, never below it, within the tiles of the same index along tile or of the next one. Each unordered pair of tiles is listed at most once among live slots; every pair of beads closer than 15 is covered by a live slot. Slots at or past the count hold valid numbers too. `pair_count`: for every index along tile but the last, one of its 4 devices along col has all 8 slots live.
All inputs are finite; a program needn't handle non-finite values.
Results may differ from the reference program's by a relative error of at most 0.0003.
Values sent between devices are 32-bit elements; how exact they have to be, the bound alone decides.
No kernel may reach another device: no remote copies, remote signals or barrier semaphores. Data moves between devices by JAX's collectives and lax.ppermute only.
A program may use at most 64 MiB of HBM per device.

```python
import jax
import jax.numpy as jnp
from jax import lax

TILE_B = 128
COLS = 16
R_DEV = 4
P_DEV = 8
ITERS = 2
TILES = 32
BEADS = 4096
N_TILE = 8
N_COL = 4


def tile_layout(key):
    thick = jax.random.randint(jax.random.fold_in(key, 7), (TILES,), 10, 21).astype(jnp.int32)
    start = (jnp.cumsum(thick) - thick).astype(jnp.int32)
    return (thick, start)


def pair_layout(key):
    thick, start = tile_layout(key)
    finish = start + thick
    tile_range = jnp.arange(TILES, dtype=jnp.int32)
    reach = jnp.arange(3, dtype=jnp.int32)
    partner = tile_range[:, None] + reach[None, :]
    safe_partner = jnp.minimum(partner, TILES - 1)
    spacing = start[safe_partner] - finish[:, None]
    linked = (reach[None, :] == 0) | (partner < TILES) & (spacing < 15)
    linked_group = linked.reshape(N_TILE, R_DEV * 3)
    cand_range = jnp.arange(R_DEV * 3, dtype=jnp.int32)
    score = jnp.where(linked_group, cand_range[None, :], cand_range[None, :] + 3 * R_DEV)
    order = jnp.argsort(score, axis=1, stable=True).astype(jnp.int32)
    length = jnp.sum(linked_group.astype(jnp.int32), axis=1)
    heavy = jax.random.randint(jax.random.fold_in(key, 13), (N_TILE,), 0, N_COL).astype(jnp.int32)
    slot_range = jnp.arange(P_DEV, dtype=jnp.int32)
    dev_range = jnp.arange(N_COL, dtype=jnp.int32)
    rank = jnp.where(dev_range[None, :] < heavy[:, None], dev_range[None, :], dev_range[None, :] - 1)
    is_heavy = dev_range[None, :] == heavy[:, None]
    item = jnp.where(is_heavy[:, :, None], slot_range[None, None, :], P_DEV + slot_range[None, None, :] * (N_COL - 1) + rank[:, :, None])
    live = item < length[:, None, None]
    count = jnp.sum(live.astype(jnp.int32), axis=2)
    item_safe = jnp.minimum(item, 3 * R_DEV - 1)
    order_wide = jnp.broadcast_to(order[:, None, :], (N_TILE, N_COL, 3 * R_DEV))
    chosen = jnp.take_along_axis(order_wide, item_safe, axis=2)
    row_local = chosen // 3
    group_first = jnp.arange(N_TILE, dtype=jnp.int32)[:, None, None] * R_DEV
    col_global = jnp.minimum(group_first + row_local + chosen % 3, TILES - 1)
    return (jnp.stack([row_local, col_global]).astype(jnp.int32), count.astype(jnp.int32))


def draw_positions(key, part):
    thick, start = tile_layout(key)
    key_along, key_across = jax.random.split(jax.random.fold_in(key, 11))
    along = jax.random.uniform(key_along, (TILES, TILE_B), jnp.float32) * thick[:, None].astype(jnp.float32)
    along = along + start[:, None].astype(jnp.float32)
    across = jax.random.uniform(key_across, (2, TILES, TILE_B), jnp.float32, 0.0, 22.0)
    return jnp.concatenate([along[None], across], axis=0).reshape(3, BEADS)


def draw_trial_block(key, part):
    key_base, key_scale = jax.random.split(key, 2)
    values_base = jax.random.normal(key_base, (3, COLS, BEADS), jnp.float32)
    column_scale = 0.3 * jnp.exp(jax.random.uniform(key_scale, (COLS,), jnp.float32, 0.0, jnp.log(10.0)))
    position = jnp.arange(BEADS, dtype=jnp.float32) / BEADS
    growth = 1.0 + 2.0 * position
    return values_base * column_scale[None, :, None] * growth[None, None, :]


def draw_pair_tiles(key, part):
    lists, count = pair_layout(key)
    return lists


def draw_pair_count(key, part):
    lists, count = pair_layout(key)
    return count


def setup_inputs(seed: int = 0) -> dict:
    key_of = jax.random.split(jax.random.key(seed), 5)
    positions = draw_positions(jax.random.fold_in(key_of[4], 71), 0)
    trial_block = draw_trial_block(jax.random.fold_in(key_of[4], 71), 0)
    pair_tiles = draw_pair_tiles(jax.random.fold_in(key_of[4], 71), 0)
    pair_count = draw_pair_count(jax.random.fold_in(key_of[4], 71), 0)
    return dict(positions=positions, trial_block=trial_block, pair_tiles=pair_tiles, pair_count=pair_count)


spring_scale = 1.0 / 64.0
cutoff_sq = 225.0
step_size = 0.2
highest = lax.Precision.HIGHEST

def pair_terms(pos_rows, pos_cols, vec_rows, vec_cols):
    offset = pos_cols[:, :, None, :] - pos_rows[:, :, :, None]
    dist_sq = jnp.sum(offset * offset, axis=0)
    falloff = jnp.where(dist_sq < cutoff_sq, (1.0 - dist_sq / cutoff_sq) ** 2, 0.0)
    weight = spring_scale * falloff / jnp.maximum(dist_sq, 1.0)
    spring = weight[None, None] * offset[:, None] * offset[None, :]
    row_diag = jnp.sum(spring, axis=-1)
    col_diag = jnp.sum(spring, axis=-2)
    row_term = jnp.einsum('cdpa,dkpa->pcka', row_diag, vec_rows, precision=highest) - jnp.einsum('cdpab,dkpb->pcka', spring, vec_cols, precision=highest)
    col_term = jnp.einsum('cdpb,dkpb->pckb', col_diag, vec_cols, precision=highest) - jnp.einsum('cdpab,dkpa->pckb', spring, vec_rows, precision=highest)
    return (row_term, col_term)

def project_out(correlation, gram_sum):
    factor = jnp.linalg.cholesky(correlation)
    middle = lax.linalg.triangular_solve(factor, gram_sum, left_side=True, lower=True)
    return lax.linalg.triangular_solve(factor, middle, left_side=True, lower=True, transpose_a=True)

def reference(positions, trial_block, pair_tiles, pair_count):
    tile_count = N_TILE * R_DEV
    pos_tiles = positions.reshape(3, tile_count, TILE_B)
    slot_range = jnp.arange(P_DEV, dtype=jnp.int32)
    is_live = (slot_range[None, None, :] < pair_count[:, :, None]).astype(jnp.float32)
    row_ids = (jnp.arange(N_TILE, dtype=jnp.int32)[:, None, None] * R_DEV + pair_tiles[0]).astype(jnp.int32)
    col_ids = pair_tiles[1].astype(jnp.int32)
    off_diag = is_live * (col_ids != row_ids).astype(jnp.float32)
    groups = (row_ids.reshape(-1, 8), col_ids.reshape(-1, 8), is_live.reshape(-1, 8), off_diag.reshape(-1, 8))
    current = trial_block
    for iteration in range(ITERS):
        vec_tiles = current.reshape(3, COLS, tile_count, TILE_B)

        def add_group(running, group_now):
            rows_now, cols_now, live_now, far_now = group_now
            row_term, col_term = pair_terms(jnp.take(pos_tiles, rows_now, axis=1), jnp.take(pos_tiles, cols_now, axis=1), jnp.take(vec_tiles, rows_now, axis=2), jnp.take(vec_tiles, cols_now, axis=2))
            row_term = row_term * live_now[:, None, None, None]
            col_term = col_term * far_now[:, None, None, None]
            running = running.at[:, :, rows_now, :].add(jnp.transpose(row_term, (1, 2, 0, 3)))
            running = running.at[:, :, cols_now, :].add(jnp.transpose(col_term, (1, 2, 0, 3)))
            return (running, None)
        product, _ = lax.scan(add_group, jnp.zeros((3, COLS, tile_count, TILE_B), jnp.float32), groups)
        product = product.reshape(3, COLS, BEADS)
        gram_sum = jnp.einsum('dkb,dlb->kl', current, product, precision=highest)
        correlation = jnp.einsum('dkb,dlb->kl', current, current, precision=highest)
        coefficients = project_out(correlation, gram_sum)
        residual = product - jnp.einsum('jk,djb->dkb', coefficients, current, precision=highest)
        current = current - step_size * residual
    bead_scale = 1.0 / (3.0 * BEADS)
    resid_norms = jnp.sum(residual * residual, axis=(0, 2))
    return (current, gram_sum * bead_scale, correlation * bead_scale, resid_norms * bead_scale)
```

```python
import functools

import jax
import jax.numpy as jnp
from jax import lax
from jax.experimental import pallas as pl
from jax.experimental.pallas import tpu as pltpu
from jax.sharding import PartitionSpec as P

TILE_B = 128
REACH = 2
CHUNK = 32

spring_scale = 1.0 / 64.0
cutoff_sq = 225.0
step_size = 0.2
highest = lax.Precision.HIGHEST
f32 = jnp.float32
bf16 = jnp.bfloat16
COMPONENT_PAIRS = ((0, 0), (0, 1), (0, 2), (1, 1), (1, 2), (2, 2))


def parity():
    return lax.rem(lax.axis_index("col"), 2)


def lanes(start, size):
    return pl.ds(pl.multiple_of(start, TILE_B), size)


def pack_kernel(vec_ref, pos_ref, tiles_ref, count_ref, out_ref):
    rows, width = vec_ref.shape
    out_ref[0:rows, :] = vec_ref[...]
    first_tile = lax.axis_index("tile") * (width // TILE_B)
    tile_of = lax.broadcasted_iota(jnp.int32, (8, width), 1) // TILE_B
    reach_of = lax.broadcasted_iota(jnp.int32, (8, width), 0) - 4
    live = jnp.zeros((8, width), f32)
    for c in range(tiles_ref.shape[2]):
        for s in range(tiles_ref.shape[3]):
            row = tiles_ref[0, 0, c, s]
            reach = tiles_ref[1, 0, c, s] - first_tile - row
            row = jnp.where(s < count_ref[0, c], row, -1)
            live += jnp.where((tile_of == row) & (reach_of == reach), 1.0, 0.0)
    out_ref[rows : rows + 8, :] = live * (spring_scale * step_size)
    out_ref[rows : rows + 3, :] = pos_ref[...]


def split(x):
    high = x.astype(bf16)
    return high, (x - high.astype(f32)).astype(bf16)


def store_vectors(lhs, x, base):
    rows, width = x.shape
    high, low = split(x)
    lhs[0:rows, lanes(base, width)] = high
    lhs[rows + 16 : 2 * rows + 16, lanes(base, width)] = low


def store_places(pos, pos_t, block, base):
    width = block.shape[1]
    pos[:, lanes(base, width)] = block
    pos_t[lanes(base, width), :] = jnp.transpose(block)


def fill_springs(pos, pos_t, spring_high, spring_low, row_tiles):
    for j in range(row_tiles[0] - REACH, row_tiles[-1] + REACH + 1):
        near = [w for w in row_tiles if abs(w - j) <= REACH]

        def one_chunk(q, carry):
            start = pl.multiple_of(q * CHUNK, CHUNK)
            col = pos_t[pl.ds(j * TILE_B + start, CHUNK), :]
            down = [jnp.broadcast_to(col[:, c : c + 1], (CHUNK, TILE_B)) for c in range(3)]
            for w in near:
                first, reach = min(j, w), abs(w - j)
                live = pos[4 + reach : 5 + reach, first * TILE_B : (first + 1) * TILE_B]
                offset = [down[c] - pos[c : c + 1, w * TILE_B : (w + 1) * TILE_B] for c in range(3)]
                dist_sq = offset[0] * offset[0] + offset[1] * offset[1] + offset[2] * offset[2]
                falloff = jnp.maximum(1.0 - dist_sq * (1.0 / cutoff_sq), 0.0)
                weight = falloff * falloff * live / jnp.maximum(dist_sq, 1.0)
                pulled = [weight * offset[c] for c in range(3)]
                place = pl.ds((j - w + REACH) * TILE_B + start, CHUNK)
                for n, (c, d) in enumerate(COMPONENT_PAIRS):
                    high, low = split(pulled[c] * offset[d])
                    r = row_tiles.index(w)
                    spring_high[r, place, n * TILE_B : (n + 1) * TILE_B] = high
                    spring_low[r, place, n * TILE_B : (n + 1) * TILE_B] = low
            return carry

        lax.fori_loop(0, TILE_B // CHUNK, one_chunk, 0)


def apply_springs(lhs, spring_high, spring_low, r, w, vec, cols):
    rows = 3 * cols
    near = slice((w - REACH) * TILE_B, (w + REACH + 1) * TILE_B)
    with_high = jnp.dot(lhs[:, near], spring_high[r], preferred_element_type=f32)
    with_low = jnp.dot(lhs[0 : rows + 16, near], spring_low[r], preferred_element_type=f32)
    total = with_high[0 : rows + 16] + with_low
    diag = total[rows : rows + 1]
    total = total[0:rows] + with_high[rows + 16 :]
    out = [None] * 3
    for n, (c, d) in enumerate(COMPONENT_PAIRS):
        part = slice(n * TILE_B, (n + 1) * TILE_B)
        for a, b in dict.fromkeys(((c, d), (d, c))):
            term = diag[:, part] * vec[b] - total[b * cols : (b + 1) * cols, part]
            out[a] = term if out[a] is None else out[a] + term
    return out


def first_kernel(own_ref, got_ref, out_ref, lhs, pos, pos_t, spring_high, spring_low):
    rows, width = out_ref.shape
    cols = rows // 3
    tiles = width // TILE_B
    odd = parity()
    lhs[rows : rows + 16, :] = jnp.ones((16, lhs.shape[1]), bf16)
    for ref, slot in ((own_ref, 1 - odd), (got_ref, odd)):
        store_vectors(lhs, ref[0:rows, :], slot * width)
        store_places(pos, pos_t, ref[rows : rows + 8, :], slot * width)
    row_tiles = list(range(REACH, REACH + tiles))
    fill_springs(pos, pos_t, spring_high, spring_low, row_tiles)
    for r, w in enumerate(row_tiles):
        part = slice(w * TILE_B, (w + 1) * TILE_B)
        vec = [
            lhs[d * cols : (d + 1) * cols, part].astype(f32)
            + lhs[rows + 16 + d * cols : rows + 16 + (d + 1) * cols, part].astype(f32)
            for d in range(3)
        ]
        out = apply_springs(lhs, spring_high, spring_low, r, w, vec, cols)
        for c in range(3):
            out_ref[c * cols : (c + 1) * cols, r * TILE_B : (r + 1) * TILE_B] = out[c]


def second_kernel(
    own_ref, got_ref, prod_ref, prod_got_ref, out_ref, gram_ref, lhs, pos, pos_t, spring_high, spring_low
):
    rows, width = prod_ref.shape
    cols = rows // 3
    half = width // 2
    odd = parity()
    lhs[rows : rows + 16, :] = jnp.ones((16, lhs.shape[1]), bf16)
    store_places(pos, pos_t, own_ref[rows : rows + 8, :], (1 - odd) * half)
    store_places(pos, pos_t, got_ref[rows : rows + 8, lanes((1 - odd) * half, half)], odd * width)
    store_vectors(lhs, prod_ref[...], odd * half)
    store_vectors(lhs, prod_got_ref[:, lanes(odd * half, half)], (1 - odd) * width)
    row_tiles = [REACH, REACH + 1]
    fill_springs(pos, pos_t, spring_high, spring_low, row_tiles)
    for r, w in enumerate(row_tiles):
        here = lanes((1 - odd) * half + r * TILE_B, TILE_B)
        vec = [prod_ref[d * cols : (d + 1) * cols, here] for d in range(3)]
        out = apply_springs(lhs, spring_high, spring_low, r, w, vec, cols)
        for c in range(3):
            out_ref[c * cols : (c + 1) * cols, r * TILE_B : (r + 1) * TILE_B] = out[c]
    gram = jnp.zeros((rows, rows), f32)
    for d in range(3):
        band = slice(d * cols, (d + 1) * cols)
        joint = jnp.concatenate(
            [own_ref[band, lanes(odd * half, half)], prod_ref[band, lanes((1 - odd) * half, half)], out_ref[band, :]],
            axis=0,
        )
        gram += lax.dot_general(joint, joint, (((1,), (1,)), ((), ())), precision=highest, preferred_element_type=f32)
    block = [[gram[a * cols : (a + 1) * cols, b * cols : (b + 1) * cols] for b in range(3)] for a in range(3)]
    gram_ref[...] = jnp.zeros(gram_ref.shape, f32)
    for n, part in enumerate((block[0][0], block[0][1], block[1][1], block[1][2], block[2][2])):
        gram_ref[:, n * cols : (n + 1) * cols] = part


def solve(matrix, rhs):
    n = matrix.shape[0]
    joint = jnp.concatenate([matrix, rhs], axis=1)
    row_of = lax.broadcasted_iota(jnp.int32, joint.shape, 0)
    for k in range(n):
        row = joint[k : k + 1, :] / joint[k : k + 1, k : k + 1]
        joint = jnp.where(row_of == k, row, joint - joint[:, k : k + 1] * row)
    return joint[:, n:]


def mul(a, b):
    return jnp.dot(a, b, precision=highest, preferred_element_type=f32)


def mul_t(a, b):
    return lax.dot_general(a, b, (((0,), (0,)), ((), ())), precision=highest, preferred_element_type=f32)


def last_kernel(
    bead_scale, own_ref, prod_ref, prod_got_ref, quad_ref, quad_got_ref, gram_ref, out_ref, ray_ref, corr_ref, norm_ref
):
    rows, width = prod_ref.shape
    cols = rows // 3
    half = width // 2
    odd = parity()
    xx, xp, pp, pq, qq = [gram_ref[:, n * cols : (n + 1) * cols] for n in range(5)]
    row_of = lax.broadcasted_iota(jnp.int32, (cols, cols), 0)
    col_of = lax.broadcasted_iota(jnp.int32, (cols, cols), 1)
    eye = jnp.where(row_of == col_of, 1.0, 0.0).astype(f32)
    shift = solve(xx, xp)
    turn = eye + shift
    first = mul_t(turn, xp)
    corr = mul_t(turn, mul(xx, turn) - xp) - mul_t(xp, turn) + pp
    gram = mul(first, turn) - mul_t(turn, pp) - mul(pp, turn) + pq
    squares = jnp.sum(eye * (mul_t(turn, mul(pp, turn) - 2.0 * pq) + qq), axis=0, keepdims=True)
    second = solve(corr, gram)
    squares = squares - jnp.sum(gram * second, axis=0, keepdims=True)
    ray_ref[...] = gram * (bead_scale / step_size)
    corr_ref[...] = corr * bead_scale
    norm_ref[...] = squares * (bead_scale / step_size**2)
    both = shift + second
    with_vec = both + mul(shift, second)
    for side in range(2):
        here = slice(side * half, (side + 1) * half)
        away = slice((1 - side) * half, (2 - side) * half)
        mine = odd == side
        for d in range(3):
            band = slice(d * cols, (d + 1) * cols)
            vec = own_ref[band, here]
            prod = jnp.where(mine, prod_ref[band, away], prod_got_ref[band, away])
            quad = jnp.where(mine, quad_ref[band, :], quad_got_ref[band, :])
            out_ref[band, here] = vec + mul_t(with_vec, vec) - 2.0 * prod - mul_t(both, prod) + quad


def per_device(positions, trial_block, pair_tiles, pair_count):
    comps, cols, width = trial_block.shape
    rows = comps * cols
    n_tile, n_col = lax.axis_size("tile"), lax.axis_size("col")
    tiles = width // TILE_B
    half = width // 2
    assert tiles == 2 * REACH and n_col % 2 == 0
    bead_scale = 1.0 / (3.0 * n_tile * width)
    vmem = pl.BlockSpec(memory_space=pltpu.VMEM)
    smem = pl.BlockSpec(memory_space=pltpu.SMEM)
    params = pltpu.CompilerParams(vmem_limit_bytes=40 * 2**20)

    own = pl.pallas_call(
        pack_kernel,
        out_shape=jax.ShapeDtypeStruct((rows + 8, width), f32),
        in_specs=[vmem, vmem, smem, smem],
        out_specs=vmem,
        name="pack",
    )(trial_block.reshape(rows, width), positions, pair_tiles, pair_count)

    halo = []
    for t in range(n_tile):
        for c in range(n_col):
            source = t - 1 if c % 2 == 0 else t + 1
            if 0 <= source < n_tile:
                halo.append((source * n_col + c, t * n_col + c))
    got = lax.ppermute(own, ("tile", "col"), halo)

    def swapped(x):
        return lax.ppermute(x, "col", [(c, c ^ 1) for c in range(n_col)])

    def scratch(window, count):
        deep = (2 * REACH + 1) * TILE_B
        across = len(COMPONENT_PAIRS) * TILE_B
        return [
            pltpu.VMEM((2 * rows + 16, window), bf16),
            pltpu.VMEM((8, window), f32),
            pltpu.VMEM((window, 8), f32),
            pltpu.VMEM((count, deep, across), bf16),
            pltpu.VMEM((count, deep, across), bf16),
        ]

    prod = pl.pallas_call(
        first_kernel,
        out_shape=jax.ShapeDtypeStruct((rows, width), f32),
        in_specs=[vmem] * 2,
        out_specs=vmem,
        scratch_shapes=scratch(2 * width, tiles),
        compiler_params=params,
        name="first",
    )(own, got)
    prod_got = swapped(prod)
    quad, gram = pl.pallas_call(
        second_kernel,
        out_shape=(jax.ShapeDtypeStruct((rows, half), f32), jax.ShapeDtypeStruct((cols, 128), f32)),
        in_specs=[vmem] * 4,
        out_specs=(vmem, vmem),
        scratch_shapes=scratch(width + half, REACH),
        compiler_params=params,
        name="second",
    )(own, got, prod, prod_got)
    gram = gram + swapped(gram)
    quad_got = swapped(quad)
    step = 1
    while step < n_tile:
        gram = gram + lax.ppermute(gram, "tile", [(t, t ^ step) for t in range(n_tile)])
        step *= 2
    block, ray, corr, norms = pl.pallas_call(
        functools.partial(last_kernel, bead_scale),
        out_shape=(
            jax.ShapeDtypeStruct((rows, width), f32),
            jax.ShapeDtypeStruct((cols, cols), f32),
            jax.ShapeDtypeStruct((cols, cols), f32),
            jax.ShapeDtypeStruct((1, cols), f32),
        ),
        in_specs=[vmem] * 6,
        out_specs=(vmem,) * 4,
        compiler_params=params,
        name="last",
    )(own, prod, prod_got, quad, quad_got, gram)
    return block.reshape(comps, cols, width), ray, corr, norms.reshape(cols)


def solution(mesh):
    return jax.shard_map(
        per_device,
        mesh=mesh,
        in_specs=(
            P(None, "tile"),
            P(None, None, "tile"),
            P(None, "tile", None, None),
            P("tile", None),
        ),
        out_specs=(P(None, None, "tile"), P(), P(), P()),
        check_vma=False,
    )
```

```python
import functools

import jax
import jax.numpy as jnp
from jax import lax
from jax.experimental import pallas as pl
from jax.experimental.pallas import tpu as pltpu
from jax.sharding import PartitionSpec as P

TILE_B = 128
REACH = 2
CHUNK = 32

spring_scale = 1.0 / 64.0
cutoff_sq = 225.0
step_size = 0.2
highest = lax.Precision.HIGHEST
f32 = jnp.float32
bf16 = jnp.bfloat16


def parity():
    return lax.rem(lax.axis_index("col"), 2)


def lanes(start, size):
    return pl.ds(pl.multiple_of(start, TILE_B), size)


def pack_kernel(vec_ref, pos_ref, tiles_ref, count_ref, out_ref, tiles, count, pos, sems):
    rows, width = vec_ref.shape
    copies = [
        pltpu.make_async_copy(tiles_ref, tiles, sems.at[0]),
        pltpu.make_async_copy(count_ref, count, sems.at[1]),
        pltpu.make_async_copy(pos_ref, pos, sems.at[2]),
        pltpu.make_async_copy(vec_ref, out_ref.at[0:rows], sems.at[3]),
    ]
    for copy in copies:
        copy.start()
    first_tile = lax.axis_index("tile") * (width // TILE_B)
    tile_of = lax.broadcasted_iota(jnp.int32, (8, width), 1) // TILE_B
    reach_of = lax.broadcasted_iota(jnp.int32, (8, width), 0) - 4
    live = jnp.zeros((8, width), f32)
    copies[0].wait()
    copies[1].wait()
    for c in range(tiles.shape[2]):
        for s in range(tiles.shape[3]):
            row = tiles[0, 0, c, s]
            reach = tiles[1, 0, c, s] - first_tile - row
            row = jnp.where(s < count[0, c], row, -1)
            live += jnp.where((tile_of == row) & (reach_of == reach), cutoff_sq, 0.0)
    out_ref[rows : rows + 8, :] = live
    copies[2].wait()
    out_ref[rows : rows + 3, :] = pos[...]
    copies[3].wait()


def split(x):
    high = x.astype(bf16)
    return high, (x - high.astype(f32)).astype(bf16)


def store_vectors(vec, high, low, x, base):
    place = lanes(base, x.shape[1])
    vec[:, place] = x
    high[:, place], low[:, place] = split(x)


def store_places(pos, pos_t, block, base):
    place = lanes(base, block.shape[1])
    pos[:, place] = block
    if pos_t is not None:
        pos_t[place, :] = jnp.transpose(block)


def tile_slice(w):
    return slice(w * TILE_B, (w + 1) * TILE_B)


def fill_pulls(pos, pos_t, pull_high, pull_low, r, w):
    across = pos[:, tile_slice(w)]
    for j in range(w - REACH, w + REACH + 1):
        first, reach = min(j, w), abs(w - j)
        bound = pos[4 + reach : 5 + reach, tile_slice(first)]
        for q in range(0, TILE_B, CHUNK):
            down = pos_t[j * TILE_B + q : j * TILE_B + q + CHUNK, :]
            offset = [down[:, c : c + 1] - across[c : c + 1, :] for c in range(3)]
            dist_sq = offset[0] * offset[0] + offset[1] * offset[1] + offset[2] * offset[2]
            falloff = jnp.maximum(bound - dist_sq, 0.0)
            weight = falloff * falloff / jnp.maximum(dist_sq, 1.0)
            place = slice((j - w + REACH) * TILE_B + q, (j - w + REACH) * TILE_B + q + CHUNK)
            for c in range(3):
                high, low = split(weight * offset[c])
                pull_high[r, place, tile_slice(c)] = high
                pull_low[r, place, tile_slice(c)] = low


def apply_pulls(vec, high, low, pos, pull_high, pull_low, w):
    rows = vec.shape[0]
    cols = rows // 3
    near = slice((w - REACH) * TILE_B, (w + REACH + 1) * TILE_B)
    here = tile_slice(w)
    middle = jnp.mean(pos[:, here], axis=1, keepdims=True)
    place = pos[:, near] - middle
    row_of = lax.broadcasted_iota(jnp.int32, place.shape, 0)
    extra = jnp.where(row_of < 3, place, jnp.where(row_of == 3, 1.0, 0.0))
    along = sum(place[d : d + 1] * vec[d * cols : (d + 1) * cols, near] for d in range(3))
    more_high, more_low = split(jnp.concatenate([along, extra, jnp.zeros_like(extra)], axis=0))
    left_high = jnp.concatenate([high[:, near], more_high], axis=0)
    left_low = jnp.concatenate([low[:, near], more_low], axis=0)
    left = jnp.concatenate([left_high, left_low], axis=0)
    n = left_high.shape[0]
    with_high = jnp.dot(left, pull_high, preferred_element_type=f32)
    with_low = jnp.dot(left_high, pull_low, preferred_element_type=f32)
    total = with_high[0:n] + (with_high[n:] + with_low)
    mine = [place[d : d + 1, REACH * TILE_B : (REACH + 1) * TILE_B] for d in range(3)]
    out = []
    for c in range(3):
        part = total[:, tile_slice(c)]
        e = rows + cols
        term = -part[rows:e]
        for d in range(3):
            diag = part[e + d : e + d + 1] - mine[d] * part[e + 3 : e + 4]
            term += diag * vec[d * cols : (d + 1) * cols, here] + mine[d] * part[d * cols : (d + 1) * cols]
        out.append(term * (spring_scale * step_size / cutoff_sq**2))
    return jnp.concatenate(out, axis=0)


def first_kernel(own_ref, got_ref, out_ref, pull_high, pull_low, vec, high, low, pos, pos_t):
    rows, width = out_ref.shape
    odd = parity()
    store_vectors(vec, high, low, own_ref[0:rows, :], (1 - odd) * width)
    store_vectors(vec, high, low, got_ref[0:rows, :], odd * width)
    store_places(pos, pos_t, own_ref[rows : rows + 8, :], (1 - odd) * width)
    store_places(pos, pos_t, got_ref[rows : rows + 8, :], odd * width)
    for r in range(width // TILE_B):
        w = REACH + r
        fill_pulls(pos, pos_t, pull_high, pull_low, r, w)
        out_ref[:, tile_slice(r)] = apply_pulls(vec, high, low, pos, pull_high[r], pull_low[r], w)


def second_kernel(
    own_ref, got_ref, prod_ref, prod_got_ref, pull_high, pull_low, out_ref, gram_ref, vec, high, low, pos
):
    rows, width = prod_ref.shape
    cols = rows // 3
    half = width // 2
    odd = parity()
    store_places(pos, None, own_ref[rows : rows + 8, :], (1 - odd) * half)
    store_places(pos, None, got_ref[rows : rows + 8, lanes((1 - odd) * half, half)], odd * width)
    store_vectors(vec, high, low, prod_ref[...], odd * half)
    store_vectors(vec, high, low, prod_got_ref[:, lanes(odd * half, half)], (1 - odd) * width)
    for r in range(REACH):
        from_first = r + (1 - odd) * REACH
        out_ref[:, tile_slice(r)] = apply_pulls(
            vec, high, low, pos, pull_high[from_first], pull_low[from_first], REACH + r
        )
    gram = jnp.zeros((rows, rows), f32)
    for d in range(3):
        band = slice(d * cols, (d + 1) * cols)
        joint = jnp.concatenate(
            [own_ref[band, lanes(odd * half, half)], vec[band, half:width], out_ref[band, :]], axis=0
        )
        gram += lax.dot_general(joint, joint, (((1,), (1,)), ((), ())), precision=highest, preferred_element_type=f32)
    block = [[gram[a * cols : (a + 1) * cols, b * cols : (b + 1) * cols] for b in range(3)] for a in range(3)]
    gram_ref[...] = jnp.zeros(gram_ref.shape, f32)
    for n, part in enumerate((block[0][0], block[0][1], block[1][1], block[1][2], block[2][2])):
        gram_ref[:, n * cols : (n + 1) * cols] = part


def solve(matrix, rhs):
    n = matrix.shape[0]
    joint = jnp.concatenate([matrix, rhs], axis=1)
    row_of = lax.broadcasted_iota(jnp.int32, joint.shape, 0)
    for k in range(n):
        row = joint[k : k + 1, :] / joint[k : k + 1, k : k + 1]
        joint = jnp.where(row_of == k, row, joint - joint[:, k : k + 1] * row)
    return joint[:, n:]


def mul(a, b):
    return jnp.dot(a, b, precision=highest, preferred_element_type=f32)


def mul_t(a, b):
    return lax.dot_general(a, b, (((0,), (0,)), ((), ())), precision=highest, preferred_element_type=f32)


def last_kernel(
    bead_scale, own_ref, prod_ref, prod_got_ref, quad_ref, quad_got_ref, gram_ref, out_ref, ray_ref, corr_ref, norm_ref
):
    rows, width = prod_ref.shape
    cols = rows // 3
    half = width // 2
    odd = parity()
    xx, xp, pp, pq, qq = [gram_ref[:, n * cols : (n + 1) * cols] for n in range(5)]
    row_of = lax.broadcasted_iota(jnp.int32, (cols, cols), 0)
    col_of = lax.broadcasted_iota(jnp.int32, (cols, cols), 1)
    eye = jnp.where(row_of == col_of, 1.0, 0.0).astype(f32)
    shift = solve(xx, xp)
    turn = eye + shift
    first = mul_t(turn, xp)
    corr = mul_t(turn, mul(xx, turn) - xp) - mul_t(xp, turn) + pp
    gram = mul(first, turn) - mul_t(turn, pp) - mul(pp, turn) + pq
    squares = jnp.sum(eye * (mul_t(turn, mul(pp, turn) - 2.0 * pq) + qq), axis=0, keepdims=True)
    second = solve(corr, gram)
    squares = squares - jnp.sum(gram * second, axis=0, keepdims=True)
    ray_ref[...] = gram * (bead_scale / step_size)
    corr_ref[...] = corr * bead_scale
    norm_ref[...] = squares * (bead_scale / step_size**2)
    both = shift + second
    with_vec = both + mul(shift, second)
    for side in range(2):
        here = slice(side * half, (side + 1) * half)
        away = slice((1 - side) * half, (2 - side) * half)
        mine = odd == side
        for d in range(3):
            band = slice(d * cols, (d + 1) * cols)
            vec = own_ref[band, here]
            prod = jnp.where(mine, prod_ref[band, away], prod_got_ref[band, away])
            quad = jnp.where(mine, quad_ref[band, :], quad_got_ref[band, :])
            out_ref[band, here] = vec + mul_t(with_vec, vec) - 2.0 * prod - mul_t(both, prod) + quad


def per_device(positions, trial_block, pair_tiles, pair_count):
    comps, cols, width = trial_block.shape
    rows = comps * cols
    n_tile, n_col = lax.axis_size("tile"), lax.axis_size("col")
    tiles = width // TILE_B
    half = width // 2
    assert tiles == 2 * REACH and n_col % 2 == 0
    bead_scale = 1.0 / (3.0 * n_tile * width)
    vmem = pl.BlockSpec(memory_space=pltpu.VMEM)
    smem = pl.BlockSpec(memory_space=pltpu.SMEM)
    params = pltpu.CompilerParams(vmem_limit_bytes=24 * 2**20)

    hbm = pl.BlockSpec(memory_space=pltpu.HBM)
    own = pl.pallas_call(
        pack_kernel,
        out_shape=jax.ShapeDtypeStruct((rows + 8, width), f32),
        in_specs=[hbm] * 4,
        out_specs=vmem,
        scratch_shapes=[
            pltpu.SMEM(pair_tiles.shape, jnp.int32),
            pltpu.SMEM(pair_count.shape, jnp.int32),
            pltpu.VMEM(positions.shape, f32),
            pltpu.SemaphoreType.DMA((4,)),
        ],
        compiler_params=pltpu.CompilerParams(vmem_limit_bytes=4 * 2**20),
        name="pack",
    )(*[
        pltpu.with_memory_space_constraint(x, pltpu.HBM)
        for x in (trial_block.reshape(rows, width), positions, pair_tiles, pair_count)
    ])

    halo = []
    for t in range(n_tile):
        for c in range(n_col):
            source = t - 1 if c % 2 == 0 else t + 1
            if 0 <= source < n_tile:
                halo.append((source * n_col + c, t * n_col + c))
    got = lax.ppermute(own, ("tile", "col"), halo)

    def swapped(x):
        return lax.ppermute(x, "col", [(c, c ^ 1) for c in range(n_col)])

    def scratch(window):
        return [
            pltpu.VMEM((rows, window), f32),
            pltpu.VMEM((rows, window), bf16),
            pltpu.VMEM((rows, window), bf16),
            pltpu.VMEM((8, window), f32),
        ]

    pulls = jax.ShapeDtypeStruct((tiles, (2 * REACH + 1) * TILE_B, 3 * TILE_B), bf16)
    prod, pull_high, pull_low = pl.pallas_call(
        first_kernel,
        out_shape=(jax.ShapeDtypeStruct((rows, width), f32), pulls, pulls),
        in_specs=[vmem] * 2,
        out_specs=(vmem,) * 3,
        scratch_shapes=scratch(2 * width) + [pltpu.VMEM((2 * width, 8), f32)],
        compiler_params=params,
        name="first",
    )(own, got)
    prod_got = swapped(prod)
    quad, gram = pl.pallas_call(
        second_kernel,
        out_shape=(jax.ShapeDtypeStruct((rows, half), f32), jax.ShapeDtypeStruct((cols, 128), f32)),
        in_specs=[vmem] * 6,
        out_specs=(vmem, vmem),
        scratch_shapes=scratch(width + half),
        compiler_params=params,
        name="second",
    )(own, got, prod, prod_got, pull_high, pull_low)
    gram = gram + swapped(gram)
    quad_got = swapped(quad)
    step = 1
    while step < n_tile:
        gram = gram + lax.ppermute(gram, "tile", [(t, t ^ step) for t in range(n_tile)])
        step *= 2
    block, ray, corr, norms = pl.pallas_call(
        functools.partial(last_kernel, bead_scale),
        out_shape=(
            jax.ShapeDtypeStruct((rows, width), f32),
            jax.ShapeDtypeStruct((cols, cols), f32),
            jax.ShapeDtypeStruct((cols, cols), f32),
            jax.ShapeDtypeStruct((1, cols), f32),
        ),
        in_specs=[vmem] * 6,
        out_specs=(vmem,) * 4,
        compiler_params=params,
        name="last",
    )(own, prod, prod_got, quad, quad_got, gram)
    return block.reshape(comps, cols, width), ray, corr, norms.reshape(cols)


def solution(mesh):
    return jax.shard_map(
        per_device,
        mesh=mesh,
        in_specs=(
            P(None, "tile"),
            P(None, None, "tile"),
            P(None, "tile", None, None),
            P("tile", None),
        ),
        out_specs=(P(None, None, "tile"), P(), P(), P()),
        check_vma=False,
    )
```

```python
import functools

import jax
import jax.numpy as jnp
from jax import lax
from jax.experimental import pallas as pl
from jax.experimental.pallas import tpu as pltpu
from jax.sharding import PartitionSpec as P

TILE_B = 128
REACH = 2
CHUNK = 32

spring_scale = 1.0 / 64.0
cutoff_sq = 225.0
step_size = 0.2
highest = lax.Precision.HIGHEST
f32 = jnp.float32
bf16 = jnp.bfloat16


def parity():
    return lax.rem(lax.axis_index("col"), 2)


def lanes(start, size):
    return pl.ds(pl.multiple_of(start, TILE_B), size)


def pack_kernel(vec_ref, pos_ref, tiles_ref, count_ref, out_ref, tiles, count, pos, sems):
    rows, width = vec_ref.shape
    copies = [
        pltpu.make_async_copy(tiles_ref, tiles, sems.at[0]),
        pltpu.make_async_copy(count_ref, count, sems.at[1]),
        pltpu.make_async_copy(pos_ref, pos, sems.at[2]),
        pltpu.make_async_copy(vec_ref, out_ref.at[0:rows], sems.at[3]),
    ]
    for copy in copies:
        copy.start()
    first_tile = lax.axis_index("tile") * (width // TILE_B)
    tile_of = lax.broadcasted_iota(jnp.int32, (8, width), 1) // TILE_B
    reach_of = lax.broadcasted_iota(jnp.int32, (8, width), 0) - 4
    live = jnp.zeros((8, width), f32)
    copies[0].wait()
    copies[1].wait()
    for c in range(tiles.shape[2]):
        for s in range(tiles.shape[3]):
            row = tiles[0, 0, c, s]
            reach = tiles[1, 0, c, s] - first_tile - row
            row = jnp.where(s < count[0, c], row, -1)
            live += jnp.where((tile_of == row) & (reach_of == reach), cutoff_sq, 0.0)
    out_ref[rows : rows + 8, :] = live
    copies[2].wait()
    out_ref[rows : rows + 3, :] = pos[...]
    copies[3].wait()


def split(x):
    high = x.astype(bf16)
    return high, (x - high.astype(f32)).astype(bf16)


def store_vectors(vec, high, low, x, base):
    place = lanes(base, x.shape[1])
    vec[:, place] = x
    high[:, place], low[:, place] = split(x)


def received_places(block):
    t = lax.axis_index("tile")
    missing = jnp.where(parity() == 0, t == 0, t == lax.axis_size("tile") - 1)
    row_of = lax.broadcasted_iota(jnp.int32, block.shape, 0)
    return jnp.where((row_of > 3) & missing, 0.0, block)


def store_places(pos, pos_t, block, base):
    place = lanes(base, block.shape[1])
    pos[:, place] = block
    if pos_t is not None:
        pos_t[place, :] = jnp.transpose(block)


def tile_slice(w):
    return slice(w * TILE_B, (w + 1) * TILE_B)


def fill_pulls(pos, pos_t, pull_high, pull_low, r, w):
    across = pos[:, tile_slice(w)]
    for j in range(w - REACH, w + REACH + 1):
        first, reach = min(j, w), abs(w - j)
        bound = pos[4 + reach : 5 + reach, tile_slice(first)]
        for q in range(0, TILE_B, CHUNK):
            down = pos_t[j * TILE_B + q : j * TILE_B + q + CHUNK, :]
            offset = [down[:, c : c + 1] - across[c : c + 1, :] for c in range(3)]
            dist_sq = offset[0] * offset[0] + offset[1] * offset[1] + offset[2] * offset[2]
            falloff = jnp.maximum(bound - dist_sq, 0.0)
            weight = falloff * falloff / jnp.maximum(dist_sq, 1.0)
            place = slice((j - w + REACH) * TILE_B + q, (j - w + REACH) * TILE_B + q + CHUNK)
            for c in range(3):
                high, low = split(weight * offset[c])
                pull_high[r, place, tile_slice(c)] = high
                pull_low[r, place, tile_slice(c)] = low


def apply_pulls(vec, high, low, pos, pull_high, pull_low, w):
    rows = vec.shape[0]
    cols = rows // 3
    near = slice((w - REACH) * TILE_B, (w + REACH + 1) * TILE_B)
    here = tile_slice(w)
    middle = jnp.mean(pos[:, here], axis=1, keepdims=True)
    place = pos[:, near] - middle
    row_of = lax.broadcasted_iota(jnp.int32, place.shape, 0)
    extra = jnp.where(row_of < 3, place, jnp.where(row_of == 3, 1.0, 0.0))
    along = sum(place[d : d + 1] * vec[d * cols : (d + 1) * cols, near] for d in range(3))
    more_high, more_low = split(jnp.concatenate([along, extra, jnp.zeros_like(extra)], axis=0))
    left_high = jnp.concatenate([high[:, near], more_high], axis=0)
    left_low = jnp.concatenate([low[:, near], more_low], axis=0)
    left = jnp.concatenate([left_high, left_low], axis=0)
    n = left_high.shape[0]
    with_high = jnp.dot(left, pull_high, preferred_element_type=f32)
    with_low = jnp.dot(left_high, pull_low, preferred_element_type=f32)
    total = with_high[0:n] + (with_high[n:] + with_low)
    mine = [place[d : d + 1, REACH * TILE_B : (REACH + 1) * TILE_B] for d in range(3)]
    out = []
    for c in range(3):
        part = total[:, tile_slice(c)]
        e = rows + cols
        term = -part[rows:e]
        for d in range(3):
            diag = part[e + d : e + d + 1] - mine[d] * part[e + 3 : e + 4]
            term += diag * vec[d * cols : (d + 1) * cols, here] + mine[d] * part[d * cols : (d + 1) * cols]
        out.append(term * (spring_scale * step_size / cutoff_sq**2))
    return jnp.concatenate(out, axis=0)


def first_kernel(own_ref, got_ref, out_ref, pull_high, pull_low, vec, high, low, pos, pos_t):
    rows, width = out_ref.shape
    odd = parity()
    store_vectors(vec, high, low, own_ref[0:rows, :], (1 - odd) * width)
    store_vectors(vec, high, low, got_ref[0:rows, :], odd * width)
    store_places(pos, pos_t, own_ref[rows : rows + 8, :], (1 - odd) * width)
    store_places(pos, pos_t, received_places(got_ref[rows : rows + 8, :]), odd * width)
    for r in range(width // TILE_B):
        w = REACH + r
        fill_pulls(pos, pos_t, pull_high, pull_low, r, w)
        out_ref[:, tile_slice(r)] = apply_pulls(vec, high, low, pos, pull_high[r], pull_low[r], w)


def second_kernel(
    own_ref, got_ref, prod_ref, prod_got_ref, pull_high, pull_low, out_ref, gram_ref, vec, high, low, pos
):
    rows, width = prod_ref.shape
    cols = rows // 3
    half = width // 2
    odd = parity()
    store_places(pos, None, own_ref[rows : rows + 8, :], (1 - odd) * half)
    store_places(pos, None, got_ref[rows : rows + 8, lanes((1 - odd) * half, half)], odd * width)
    store_vectors(vec, high, low, prod_ref[...], odd * half)
    store_vectors(vec, high, low, prod_got_ref[:, lanes(odd * half, half)], (1 - odd) * width)
    for r in range(REACH):
        from_first = r + (1 - odd) * REACH
        out_ref[:, tile_slice(r)] = apply_pulls(
            vec, high, low, pos, pull_high[from_first], pull_low[from_first], REACH + r
        )
    gram = jnp.zeros((rows, rows), f32)
    for d in range(3):
        band = slice(d * cols, (d + 1) * cols)
        joint = jnp.concatenate(
            [own_ref[band, lanes(odd * half, half)], vec[band, half:width], out_ref[band, :]], axis=0
        )
        gram += lax.dot_general(joint, joint, (((1,), (1,)), ((), ())), precision=highest, preferred_element_type=f32)
    block = [[gram[a * cols : (a + 1) * cols, b * cols : (b + 1) * cols] for b in range(3)] for a in range(3)]
    gram_ref[...] = jnp.zeros(gram_ref.shape, f32)
    for n, part in enumerate((block[0][0], block[0][1], block[1][1], block[1][2], block[2][2])):
        gram_ref[:, n * cols : (n + 1) * cols] = part


def solve(matrix, rhs):
    n = matrix.shape[0]
    joint = jnp.concatenate([matrix, rhs], axis=1)
    row_of = lax.broadcasted_iota(jnp.int32, joint.shape, 0)
    for k in range(0, n, 2):
        col = [jnp.broadcast_to(joint[:, k + i : k + i + 1], joint.shape) for i in range(2)]
        row = [joint[k + i : k + i + 1, :] for i in range(2)]
        inverse = 1.0 / col[0][k : k + 1]
        ratio = col[0][k + 1 : k + 2] * inverse
        lower = (row[1] - ratio * row[0]) / (col[1][k + 1 : k + 2] - ratio * col[1][k : k + 1])
        upper = (row[0] - col[1][k : k + 1] * lower) * inverse
        joint = joint - col[0] * upper - col[1] * lower
        joint = jnp.where(row_of == k, upper, jnp.where(row_of == k + 1, lower, joint))
    return joint[:, n:]


def mul(a, b):
    return jnp.dot(a, b, precision=highest, preferred_element_type=f32)


def mul_t(a, b):
    return lax.dot_general(a, b, (((0,), (0,)), ((), ())), precision=highest, preferred_element_type=f32)


def last_kernel(
    bead_scale,
    own_ref,
    prod_ref,
    prod_got_ref,
    quad_ref,
    quad_got_ref,
    gram_ref,
    out_ref,
    ray_ref,
    corr_ref,
    norm_ref,
    out,
    ray,
    small,
    norm,
    sems,
):
    rows, width = prod_ref.shape
    cols = rows // 3
    half = width // 2
    odd = parity()
    xx, xp, pp, pq, qq = [gram_ref[:, n * cols : (n + 1) * cols] for n in range(5)]
    row_of = lax.broadcasted_iota(jnp.int32, (cols, cols), 0)
    col_of = lax.broadcasted_iota(jnp.int32, (cols, cols), 1)
    eye = jnp.where(row_of == col_of, 1.0, 0.0).astype(f32)
    shift = solve(xx, xp)
    rest = pp - mul_t(xp, shift)
    corr = xx + rest
    gram = xp - 2.0 * rest + pq - mul_t(shift, pp) - mul(rest, shift)
    second = solve(corr, gram)
    both = shift + second
    turn = eye + shift
    squares = turn * (mul(pp, turn) - 2.0 * pq) + eye * qq - gram * second
    ray[...] = gram * (bead_scale / step_size)
    small[...] = corr * bead_scale
    norm[...] = jnp.sum(squares, axis=0, keepdims=True) * (bead_scale / step_size**2)
    copies = [
        pltpu.make_async_copy(ray, ray_ref, sems.at[0]),
        pltpu.make_async_copy(small, corr_ref, sems.at[1]),
        pltpu.make_async_copy(norm, norm_ref, sems.at[2]),
    ]
    factor = jnp.concatenate([both + mul(shift, second), -both], axis=0)
    factor_high, factor_low = split(factor)
    factor = jnp.concatenate([factor_high, factor_low], axis=1)
    for d in range(3):
        band = slice(d * cols, (d + 1) * cols)
        prod, quad = [], []
        for side in range(2):
            away = slice((1 - side) * half, (2 - side) * half)
            mine = odd == side
            prod.append(jnp.where(mine, prod_ref[band, away], prod_got_ref[band, away]))
            quad.append(jnp.where(mine, quad_ref[band, :], quad_got_ref[band, :]))
        vec = own_ref[band, :]
        prod = jnp.concatenate(prod, axis=1)
        quad = jnp.concatenate(quad, axis=1)
        high, low = split(jnp.concatenate([vec, prod], axis=0))
        turned = lax.dot_general(factor, high, (((0,), (0,)), ((), ())), preferred_element_type=f32)
        small_turned = lax.dot_general(factor_high, low, (((0,), (0,)), ((), ())), preferred_element_type=f32)
        out[band, :] = vec - 2.0 * prod + quad + (turned[0:cols] + (turned[cols:] + small_turned))
        copies.append(pltpu.make_async_copy(out.at[band], out_ref.at[band], sems.at[3 + d]))
        if d == 0:
            for copy in copies:
                copy.start()
        else:
            copies[-1].start()
    for copy in copies:
        copy.wait()


def per_device(positions, trial_block, pair_tiles, pair_count):
    comps, cols, width = trial_block.shape
    rows = comps * cols
    n_tile, n_col = lax.axis_size("tile"), lax.axis_size("col")
    tiles = width // TILE_B
    half = width // 2
    assert tiles == 2 * REACH and n_col % 2 == 0
    bead_scale = 1.0 / (3.0 * n_tile * width)
    vmem = pl.BlockSpec(memory_space=pltpu.VMEM)
    smem = pl.BlockSpec(memory_space=pltpu.SMEM)
    params = pltpu.CompilerParams(vmem_limit_bytes=24 * 2**20)

    hbm = pl.BlockSpec(memory_space=pltpu.HBM)
    own = pl.pallas_call(
        pack_kernel,
        out_shape=jax.ShapeDtypeStruct((rows + 8, width), f32),
        in_specs=[hbm] * 4,
        out_specs=vmem,
        scratch_shapes=[
            pltpu.SMEM(pair_tiles.shape, jnp.int32),
            pltpu.SMEM(pair_count.shape, jnp.int32),
            pltpu.VMEM(positions.shape, f32),
            pltpu.SemaphoreType.DMA((4,)),
        ],
        compiler_params=pltpu.CompilerParams(vmem_limit_bytes=4 * 2**20),
        name="pack",
    )(*[
        pltpu.with_memory_space_constraint(x, pltpu.HBM)
        for x in (trial_block.reshape(rows, width), positions, pair_tiles, pair_count)
    ])

    halo = []
    for t in range(n_tile):
        for c in range(n_col):
            source = t - 1 if c % 2 == 0 else t + 1
            if 0 <= source < n_tile:
                halo.append((source * n_col + c, t * n_col + c))
            else:
                halo.append((t * n_col + (c ^ 1), t * n_col + c))
    got = lax.ppermute(own, ("tile", "col"), halo)

    def swapped(x):
        return lax.ppermute(x, "col", [(c, c ^ 1) for c in range(n_col)])

    def scratch(window):
        return [
            pltpu.VMEM((rows, window), f32),
            pltpu.VMEM((rows, window), bf16),
            pltpu.VMEM((rows, window), bf16),
            pltpu.VMEM((8, window), f32),
        ]

    pulls = jax.ShapeDtypeStruct((tiles, (2 * REACH + 1) * TILE_B, 3 * TILE_B), bf16)
    prod, pull_high, pull_low = pl.pallas_call(
        first_kernel,
        out_shape=(jax.ShapeDtypeStruct((rows, width), f32), pulls, pulls),
        in_specs=[vmem] * 2,
        out_specs=(vmem,) * 3,
        scratch_shapes=scratch(2 * width) + [pltpu.VMEM((2 * width, 8), f32)],
        compiler_params=params,
        name="first",
    )(own, got)
    prod_got = swapped(prod)
    quad, gram = pl.pallas_call(
        second_kernel,
        out_shape=(jax.ShapeDtypeStruct((rows, half), f32), jax.ShapeDtypeStruct((cols, 128), f32)),
        in_specs=[vmem] * 6,
        out_specs=(vmem, vmem),
        scratch_shapes=scratch(width + half),
        compiler_params=params,
        name="second",
    )(own, got, prod, prod_got, pull_high, pull_low)
    gram = gram + swapped(gram)
    quad_got = swapped(quad)

    def crossed(x, step):
        route = [
            (t * n_col + c, (t ^ step) * n_col + (c ^ 1)) for t in range(n_tile) for c in range(n_col)
        ]
        return lax.ppermute(x, ("tile", "col"), route)

    step = 1
    while step < n_tile:
        if 2 * step < n_tile:
            near, far, both = [crossed(gram, s) for s in (step, 2 * step, 3 * step)]
            gram = (gram + near) + (far + both)
        else:
            gram = gram + crossed(gram, step)
        step *= 4
    shapes = [(rows, width), (cols, cols), (cols, cols), (1, cols)]
    block, ray, corr, norms = pl.pallas_call(
        functools.partial(last_kernel, bead_scale),
        out_shape=tuple(jax.ShapeDtypeStruct(shape, f32) for shape in shapes),
        in_specs=[vmem] * 6,
        out_specs=(hbm,) * 4,
        scratch_shapes=[pltpu.VMEM(shape, f32) for shape in shapes] + [pltpu.SemaphoreType.DMA((6,))],
        compiler_params=params,
        name="last",
    )(own, prod, prod_got, quad, quad_got, gram)
    return block.reshape(comps, cols, width), ray, corr, norms.reshape(cols)


def solution(mesh):
    return jax.shard_map(
        per_device,
        mesh=mesh,
        in_specs=(
            P(None, "tile"),
            P(None, None, "tile"),
            P(None, "tile", None, None),
            P("tile", None),
        ),
        out_specs=(P(None, None, "tile"), P(), P(), P()),
        check_vma=False,
    )
```

```python
import functools

import jax
import jax.numpy as jnp
from jax import lax
from jax.experimental import pallas as pl
from jax.experimental.pallas import tpu as pltpu
from jax.sharding import PartitionSpec as P

TILE_B = 128
REACH = 2
CHUNK = 32

spring_scale = 1.0 / 64.0
cutoff_sq = 225.0
step_size = 0.2
highest = lax.Precision.HIGHEST
f32 = jnp.float32
bf16 = jnp.bfloat16


def parity():
    return lax.rem(lax.axis_index("col"), 2)


def lanes(start, size):
    return pl.ds(pl.multiple_of(start, TILE_B), size)


def pack_kernel(vec_ref, pos_ref, tiles_ref, count_ref, out_ref, tiles, count, pos, sems):
    rows, width = vec_ref.shape
    copies = [
        pltpu.make_async_copy(tiles_ref, tiles, sems.at[0]),
        pltpu.make_async_copy(count_ref, count, sems.at[1]),
        pltpu.make_async_copy(pos_ref, pos, sems.at[2]),
        pltpu.make_async_copy(vec_ref, out_ref.at[0:rows], sems.at[3]),
    ]
    for copy in copies:
        copy.start()
    first_tile = lax.axis_index("tile") * (width // TILE_B)
    tile_of = lax.broadcasted_iota(jnp.int32, (8, width), 1) // TILE_B
    reach_of = lax.broadcasted_iota(jnp.int32, (8, width), 0) - 4
    live = jnp.zeros((8, width), f32)
    copies[0].wait()
    copies[1].wait()
    for c in range(tiles.shape[2]):
        for s in range(tiles.shape[3]):
            row = tiles[0, 0, c, s]
            reach = tiles[1, 0, c, s] - first_tile - row
            row = jnp.where(s < count[0, c], row, -1)
            live += jnp.where((tile_of == row) & (reach_of == reach), cutoff_sq, 0.0)
    out_ref[rows : rows + 8, :] = live
    copies[2].wait()
    out_ref[rows : rows + 3, :] = pos[...]
    copies[3].wait()


def split(x):
    high = x.astype(bf16)
    return high, (x - high.astype(f32)).astype(bf16)


def store_vectors(vec, high, low, x, base):
    place = lanes(base, x.shape[1])
    vec[:, place] = x
    high[:, place], low[:, place] = split(x)


def received_places(block):
    t = lax.axis_index("tile")
    missing = jnp.where(parity() == 0, t == 0, t == lax.axis_size("tile") - 1)
    row_of = lax.broadcasted_iota(jnp.int32, block.shape, 0)
    return jnp.where((row_of > 3) & missing, 0.0, block)


def spread_places(pos, wide):
    high, middle = split(pos[...])
    low = (pos[...] - high.astype(f32) - middle.astype(f32)).astype(bf16)
    parts = jnp.concatenate([x.astype(f32) for x in (high, middle, low)], axis=0).astype(bf16)
    part_of = lax.broadcasted_iota(jnp.int32, (parts.shape[0], 3 * TILE_B), 0) % 8
    lane_of = lax.broadcasted_iota(jnp.int32, (parts.shape[0], 3 * TILE_B), 1) // TILE_B
    pick = jnp.where(part_of == lane_of, 1.0, 0.0).astype(bf16)
    wide[...] = lax.dot_general(parts, pick, (((0,), (0,)), ((), ())), preferred_element_type=f32)


def tile_slice(w):
    return slice(w * TILE_B, (w + 1) * TILE_B)


def fill_pulls(pos, wide, pull, r, w):
    across = pos[:, tile_slice(w)]
    for j in range(w - REACH, w + REACH + 1):
        first, reach = min(j, w), abs(w - j)
        bound = pos[4 + reach : 5 + reach, tile_slice(first)]
        for q in range(0, TILE_B, CHUNK):
            down = slice(j * TILE_B + q, j * TILE_B + q + CHUNK)
            offset = [wide[down, tile_slice(c)] - across[c : c + 1, :] for c in range(3)]
            dist_sq = offset[0] * offset[0] + offset[1] * offset[1] + offset[2] * offset[2]
            falloff = jnp.maximum(bound - dist_sq, 0.0)
            weight = falloff * falloff / jnp.maximum(dist_sq, 1.0)
            place = slice((j - w + REACH) * TILE_B + q, (j - w + REACH) * TILE_B + q + CHUNK)
            for c in range(3):
                pull[r, place, tile_slice(c)] = (weight * offset[c]).astype(bf16)


def apply_pulls(vec, high, low, pos, pull, w):
    rows = vec.shape[0]
    cols = rows // 3
    near = slice((w - REACH) * TILE_B, (w + REACH + 1) * TILE_B)
    here = tile_slice(w)
    middle = jnp.mean(pos[:, here], axis=1, keepdims=True)
    place = pos[:, near] - middle
    row_of = lax.broadcasted_iota(jnp.int32, place.shape, 0)
    extra = jnp.where(row_of < 3, place, jnp.where(row_of == 3, 1.0, 0.0))
    along = sum(place[d : d + 1] * vec[d * cols : (d + 1) * cols, near] for d in range(3))
    more_high, more_low = split(jnp.concatenate([along, extra, jnp.zeros_like(extra)], axis=0))
    left_high = jnp.concatenate([high[:, near], more_high], axis=0)
    left_low = jnp.concatenate([low[:, near], more_low], axis=0)
    left = jnp.concatenate([left_high, left_low], axis=0)
    n = left_high.shape[0]
    total = jnp.dot(left, pull, preferred_element_type=f32)
    total = total[0:n] + total[n:]
    mine = [place[d : d + 1, REACH * TILE_B : (REACH + 1) * TILE_B] for d in range(3)]
    out = []
    for c in range(3):
        part = total[:, tile_slice(c)]
        e = rows + cols
        term = -part[rows:e]
        for d in range(3):
            diag = part[e + d : e + d + 1] - mine[d] * part[e + 3 : e + 4]
            term += diag * vec[d * cols : (d + 1) * cols, here] + mine[d] * part[d * cols : (d + 1) * cols]
        out.append(term * (spring_scale * step_size / cutoff_sq**2))
    return jnp.concatenate(out, axis=0)


def first_kernel(own_ref, got_ref, out_ref, pull, vec, high, low, pos, wide):
    rows, width = out_ref.shape
    odd = parity()
    store_vectors(vec, high, low, own_ref[0:rows, :], (1 - odd) * width)
    store_vectors(vec, high, low, got_ref[0:rows, :], odd * width)
    pos[:, lanes((1 - odd) * width, width)] = own_ref[rows : rows + 8, :]
    pos[:, lanes(odd * width, width)] = received_places(got_ref[rows : rows + 8, :])
    spread_places(pos, wide)
    for r in range(width // TILE_B):
        w = REACH + r
        fill_pulls(pos, wide, pull, r, w)
        out_ref[:, tile_slice(r)] = apply_pulls(vec, high, low, pos, pull[r], w)


def second_kernel(
    own_ref, got_ref, prod_ref, prod_got_ref, pull, out_ref, gram_ref, vec, high, low, pos
):
    rows, width = prod_ref.shape
    cols = rows // 3
    half = width // 2
    odd = parity()
    pos[:, lanes((1 - odd) * half, width)] = own_ref[rows : rows + 8, :]
    pos[:, lanes(odd * width, half)] = got_ref[rows : rows + 8, lanes((1 - odd) * half, half)]
    store_vectors(vec, high, low, prod_ref[...], odd * half)
    store_vectors(vec, high, low, prod_got_ref[:, lanes(odd * half, half)], (1 - odd) * width)
    for r in range(REACH):
        from_first = r + (1 - odd) * REACH
        out_ref[:, tile_slice(r)] = apply_pulls(vec, high, low, pos, pull[from_first], REACH + r)
    gram = jnp.zeros((rows, rows), f32)
    for d in range(3):
        band = slice(d * cols, (d + 1) * cols)
        joint = jnp.concatenate(
            [own_ref[band, lanes(odd * half, half)], vec[band, half:width], out_ref[band, :]], axis=0
        )
        gram += lax.dot_general(joint, joint, (((1,), (1,)), ((), ())), precision=highest, preferred_element_type=f32)
    gram_ref[...] = jnp.zeros(gram_ref.shape, f32)
    gram_ref[:, 0:rows] = gram[0:cols]
    gram_ref[:, rows : 2 * rows] = gram[cols : 2 * cols]
    gram_ref[:, 2 * rows : 2 * rows + cols] = gram[2 * cols :, 2 * cols :]


def eliminate(joint, n):
    row_of = lax.broadcasted_iota(jnp.int32, joint.shape, 0)
    col = [jnp.broadcast_to(joint[:, j : j + 1], joint.shape) for j in range(n)]
    for k in range(n):
        inverse = 1.0 / col[k][k : k + 1]
        here = row_of == k
        factor = jnp.where(here, -1.0, col[k])
        joint = jnp.where(here, 0.0, joint) - factor * (joint[k : k + 1] * inverse)
        for j in range(k + 1, n):
            col[j] = jnp.where(here, 0.0, col[j]) - factor * (col[j][k : k + 1] * inverse)
    return joint


def mul(a, b):
    return jnp.dot(a, b, precision=highest, preferred_element_type=f32)


def turned(high, both, vec):
    vec_high, vec_low = split(vec)
    n = high.shape[1]
    first = lax.dot_general(both, vec_high, (((0,), (0,)), ((), ())), preferred_element_type=f32)
    return first[0:n] + (first[n:] + lax.dot_general(high, vec_low, (((0,), (0,)), ((), ())), preferred_element_type=f32))


def last_kernel(
    bead_scale,
    own_ref,
    prod_ref,
    prod_got_ref,
    quad_ref,
    quad_got_ref,
    gram_ref,
    out_ref,
    ray_ref,
    corr_ref,
    norm_ref,
    out,
    ray,
    small,
    norm,
    sems,
):
    rows, width = prod_ref.shape
    cols = rows // 3
    half = width // 2
    odd = parity()
    row_of = lax.broadcasted_iota(jnp.int32, (cols, cols), 0)
    col_of = lax.broadcasted_iota(jnp.int32, (cols, cols), 1)
    eye = jnp.where(row_of == col_of, 1.0, 0.0).astype(f32)
    xx, xp = gram_ref[:, 0:cols], gram_ref[:, cols : 2 * cols]
    pp, pq = gram_ref[:, rows + cols : rows + 2 * cols], gram_ref[:, rows + 2 * cols : 2 * rows]
    qq = gram_ref[:, 2 * rows : 2 * rows + cols]
    joint = eliminate(jnp.concatenate([gram_ref[:, 0:rows], gram_ref[:, rows : 2 * rows]], axis=0), cols)
    shift = joint[0:cols, cols : 2 * cols]
    rest = joint[cols:, cols : 2 * cols]
    cross = joint[cols:, 2 * cols :]
    corr = xx + rest
    side = xp - 2.0 * rest + cross
    both = eliminate(jnp.concatenate([corr, side + xp], axis=1), cols)[:, cols:]
    second = both - shift
    gram = side - mul(rest, shift)
    turn = eye + shift
    squares = turn * (mul(pp, turn) - 2.0 * pq) + eye * qq - gram * second
    ray[...] = gram * (bead_scale / step_size)
    small[...] = corr * bead_scale
    norm[...] = jnp.sum(squares, axis=0, keepdims=True) * (bead_scale / step_size**2)
    copies = [
        pltpu.make_async_copy(ray, ray_ref, sems.at[0]),
        pltpu.make_async_copy(small, corr_ref, sems.at[1]),
        pltpu.make_async_copy(norm, norm_ref, sems.at[2]),
    ]
    shift_high, shift_low = split(shift)
    shift_both = jnp.concatenate([shift_high, shift_low], axis=1)
    factor_high, factor_low = split(jnp.concatenate([both, second], axis=0))
    factor_both = jnp.concatenate([factor_high, factor_low], axis=1)
    for d in range(3):
        band = slice(d * cols, (d + 1) * cols)
        prod, quad = [], []
        for part in range(2):
            away = slice((1 - part) * half, (2 - part) * half)
            mine = odd == part
            prod.append(jnp.where(mine, prod_ref[band, away], prod_got_ref[band, away]))
            quad.append(jnp.where(mine, quad_ref[band, :], quad_got_ref[band, :]))
        vec = own_ref[band, :]
        prod = jnp.concatenate(prod, axis=1)
        quad = jnp.concatenate(quad, axis=1)
        moved = turned(shift_high, shift_both, vec)
        base = vec - 2.0 * prod + quad
        out[band, :] = base + turned(factor_high, factor_both, jnp.concatenate([vec - prod, moved], axis=0))
        copies.append(pltpu.make_async_copy(out.at[band], out_ref.at[band], sems.at[3 + d]))
        if d == 0:
            for copy in copies:
                copy.start()
        else:
            copies[-1].start()
    for copy in copies:
        copy.wait()


def per_device(positions, trial_block, pair_tiles, pair_count):
    comps, cols, width = trial_block.shape
    rows = comps * cols
    n_tile, n_col = lax.axis_size("tile"), lax.axis_size("col")
    tiles = width // TILE_B
    half = width // 2
    assert tiles == 2 * REACH and n_col % 2 == 0
    bead_scale = 1.0 / (3.0 * n_tile * width)
    vmem = pl.BlockSpec(memory_space=pltpu.VMEM)
    smem = pl.BlockSpec(memory_space=pltpu.SMEM)
    params = pltpu.CompilerParams(vmem_limit_bytes=24 * 2**20)

    hbm = pl.BlockSpec(memory_space=pltpu.HBM)
    own = pl.pallas_call(
        pack_kernel,
        out_shape=jax.ShapeDtypeStruct((rows + 8, width), f32),
        in_specs=[hbm] * 4,
        out_specs=vmem,
        scratch_shapes=[
            pltpu.SMEM(pair_tiles.shape, jnp.int32),
            pltpu.SMEM(pair_count.shape, jnp.int32),
            pltpu.VMEM(positions.shape, f32),
            pltpu.SemaphoreType.DMA((4,)),
        ],
        compiler_params=pltpu.CompilerParams(vmem_limit_bytes=4 * 2**20),
        name="pack",
    )(*[
        pltpu.with_memory_space_constraint(x, pltpu.HBM)
        for x in (trial_block.reshape(rows, width), positions, pair_tiles, pair_count)
    ])

    halo = []
    for t in range(n_tile):
        for c in range(n_col):
            source = t - 1 if c % 2 == 0 else t + 1
            if 0 <= source < n_tile:
                halo.append((source * n_col + c, t * n_col + c))
            else:
                halo.append((t * n_col + (c ^ 1), t * n_col + c))
    got = lax.ppermute(own, ("tile", "col"), halo)

    def swapped(x):
        return lax.ppermute(x, "col", [(c, c ^ 1) for c in range(n_col)])

    def scratch(window):
        return [
            pltpu.VMEM((rows, window), f32),
            pltpu.VMEM((rows, window), bf16),
            pltpu.VMEM((rows, window), bf16),
            pltpu.VMEM((8, window), f32),
        ]

    pulls = jax.ShapeDtypeStruct((tiles, (2 * REACH + 1) * TILE_B, 3 * TILE_B), bf16)
    prod, pull = pl.pallas_call(
        first_kernel,
        out_shape=(jax.ShapeDtypeStruct((rows, width), f32), pulls),
        in_specs=[vmem] * 2,
        out_specs=(vmem,) * 2,
        scratch_shapes=scratch(2 * width) + [pltpu.VMEM((2 * width, 3 * TILE_B), f32)],
        compiler_params=params,
        name="first",
    )(own, got)
    prod_got = swapped(prod)
    quad, gram = pl.pallas_call(
        second_kernel,
        out_shape=(jax.ShapeDtypeStruct((rows, half), f32), jax.ShapeDtypeStruct((cols, 128), f32)),
        in_specs=[vmem] * 5,
        out_specs=(vmem, vmem),
        scratch_shapes=scratch(width + half),
        compiler_params=params,
        name="second",
    )(own, got, prod, prod_got, pull)
    gram = gram + swapped(gram)
    quad_got = swapped(quad)

    def crossed(x, step):
        route = [
            (t * n_col + c, (t ^ step) * n_col + (c ^ 1)) for t in range(n_tile) for c in range(n_col)
        ]
        return lax.ppermute(x, ("tile", "col"), route)

    step = 1
    while step < n_tile:
        if 2 * step < n_tile:
            near, far, both = [crossed(gram, s) for s in (step, 2 * step, 3 * step)]
            gram = (gram + near) + (far + both)
        else:
            gram = gram + crossed(gram, step)
        step *= 4
    shapes = [(rows, width), (cols, cols), (cols, cols), (1, cols)]
    block, ray, corr, norms = pl.pallas_call(
        functools.partial(last_kernel, bead_scale),
        out_shape=tuple(jax.ShapeDtypeStruct(shape, f32) for shape in shapes),
        in_specs=[vmem] * 6,
        out_specs=(hbm,) * 4,
        scratch_shapes=[pltpu.VMEM(shape, f32) for shape in shapes] + [pltpu.SemaphoreType.DMA((6,))],
        compiler_params=params,
        name="last",
    )(own, prod, prod_got, quad, quad_got, gram)
    return block.reshape(comps, cols, width), ray, corr, norms.reshape(cols)


def solution(mesh):
    return jax.shard_map(
        per_device,
        mesh=mesh,
        in_specs=(
            P(None, "tile"),
            P(None, None, "tile"),
            P(None, "tile", None, None),
            P("tile", None),
        ),
        out_specs=(P(None, None, "tile"), P(), P(), P()),
        check_vma=False,
    )
```

```python
import functools

import jax
import jax.numpy as jnp
from jax import lax
from jax.experimental import pallas as pl
from jax.experimental.pallas import tpu as pltpu
from jax.sharding import PartitionSpec as P

TILE_B = 128
REACH = 2
CHUNK = 32

spring_scale = 1.0 / 64.0
cutoff_sq = 225.0
step_size = 0.2
highest = lax.Precision.HIGHEST
f32 = jnp.float32
bf16 = jnp.bfloat16


def parity():
    return lax.rem(lax.axis_index("col") + lax.axis_index("tile") + 1, 2)


def pack_kernel(vec_ref, pos_ref, tiles_ref, count_ref, out_ref, tiles, count, pos, sems):
    rows, width = vec_ref.shape
    copies = [
        pltpu.make_async_copy(tiles_ref, tiles, sems.at[0]),
        pltpu.make_async_copy(count_ref, count, sems.at[1]),
        pltpu.make_async_copy(pos_ref, pos, sems.at[2]),
        pltpu.make_async_copy(vec_ref, out_ref.at[0:rows], sems.at[3]),
    ]
    for copy in copies:
        copy.start()
    first_tile = lax.axis_index("tile") * (width // TILE_B)
    tile_of = lax.broadcasted_iota(jnp.int32, (8, width), 1) // TILE_B
    reach_of = lax.broadcasted_iota(jnp.int32, (8, width), 0) - 4
    live = jnp.zeros((8, width), f32)
    copies[0].wait()
    copies[1].wait()
    for c in range(tiles.shape[2]):
        for s in range(tiles.shape[3]):
            row = tiles[0, 0, c, s]
            reach = tiles[1, 0, c, s] - first_tile - row
            row = jnp.where(s < count[0, c], row, -1)
            live += jnp.where((tile_of == row) & (reach_of == reach), cutoff_sq, 0.0)
    out_ref[rows : rows + 8, :] = live
    copies[2].wait()
    out_ref[rows : rows + 3, :] = pos[...]
    copies[3].wait()


def split(x):
    high = x.astype(bf16)
    return high, (x - high.astype(f32)).astype(bf16)


def store_vectors(vec, high, low, x, place):
    vec[:, place] = x
    high[:, place], low[:, place] = split(x)


def received_places(block):
    t = lax.axis_index("tile")
    missing = jnp.where(parity() == 0, t == 0, t == lax.axis_size("tile") - 1)
    row_of = lax.broadcasted_iota(jnp.int32, block.shape, 0)
    return jnp.where((row_of > 3) & missing, 0.0, block)


def spread_places(places):
    high, middle = split(places)
    low = (places - high.astype(f32) - middle.astype(f32)).astype(bf16)
    parts = jnp.concatenate([x.astype(f32) for x in (high, middle, low)], axis=0).astype(bf16)
    part_of = lax.broadcasted_iota(jnp.int32, (parts.shape[0], 3 * TILE_B), 0) % 8
    lane_of = lax.broadcasted_iota(jnp.int32, (parts.shape[0], 3 * TILE_B), 1) // TILE_B
    pick = jnp.where(part_of == lane_of, 1.0, 0.0).astype(bf16)
    return lax.dot_general(parts, pick, (((0,), (0,)), ((), ())), preferred_element_type=f32)


def tile_slice(w):
    return slice(w * TILE_B, (w + 1) * TILE_B)


def fill_pull(across, bound, wide, wide_base, pull, row, m):
    for q in range(0, TILE_B, CHUNK):
        down = slice(wide_base + q, wide_base + q + CHUNK)
        offset = [wide[down, tile_slice(c)] - across[c : c + 1, :] for c in range(3)]
        dist_sq = offset[0] * offset[0] + offset[1] * offset[1] + offset[2] * offset[2]
        falloff = jnp.maximum(bound - dist_sq, 0.0)
        weight = falloff * falloff / jnp.maximum(dist_sq, 1.0)
        place = slice(m * TILE_B + q, m * TILE_B + q + CHUNK)
        for c in range(3):
            pull[row, place, tile_slice(c)] = (weight * offset[c]).astype(bf16)


def bound_of(pos, w, j):
    reach = abs(w - j)
    return pos[4 + reach : 5 + reach, tile_slice(min(w, j))]


def by_parity(body):
    odd = parity()
    pl.when(odd == 0)(functools.partial(body, 0))
    pl.when(odd == 1)(functools.partial(body, 1))


def apply_pulls(vec, high, low, pos, pull, w):
    rows = vec.shape[0]
    cols = rows // 3
    near = slice((w - REACH) * TILE_B, (w + REACH + 1) * TILE_B)
    here = tile_slice(w)
    middle = jnp.mean(pos[:, here], axis=1, keepdims=True)
    place = pos[:, near] - middle
    row_of = lax.broadcasted_iota(jnp.int32, place.shape, 0)
    extra = jnp.where(row_of < 3, place, jnp.where(row_of == 3, 1.0, 0.0))
    along = sum(place[d : d + 1] * vec[d * cols : (d + 1) * cols, near] for d in range(3))
    more_high, more_low = split(jnp.concatenate([along, extra, jnp.zeros_like(extra)], axis=0))
    left_high = jnp.concatenate([high[:, near], more_high], axis=0)
    left_low = jnp.concatenate([low[:, near], more_low], axis=0)
    left = jnp.concatenate([left_high, left_low], axis=0)
    n = left_high.shape[0]
    total = jnp.dot(left, pull, preferred_element_type=f32)
    total = total[0:n] + total[n:]
    mine = [place[d : d + 1, REACH * TILE_B : (REACH + 1) * TILE_B] for d in range(3)]
    out = []
    for c in range(3):
        part = total[:, tile_slice(c)]
        e = rows + cols
        term = -part[rows:e]
        for d in range(3):
            diag = part[e + d : e + d + 1] - mine[d] * part[e + 3 : e + 4]
            term += diag * vec[d * cols : (d + 1) * cols, here] + mine[d] * part[d * cols : (d + 1) * cols]
        out.append(term * (spring_scale * step_size / cutoff_sq**2))
    return jnp.concatenate(out, axis=0)


def own_kernel(own_ref, pull, wide):
    rows = own_ref.shape[0] - 8
    tiles = own_ref.shape[1] // TILE_B
    pos = own_ref.at[rows : rows + 8]
    wide[...] = spread_places(pos[...])
    for u in range(tiles):
        for j in range(max(0, u - REACH), min(tiles, u + REACH + 1)):
            fill_pull(pos[:, tile_slice(u)], bound_of(pos, u, j), wide, j * TILE_B, pull, u + REACH, j - u + REACH)


def first_kernel(own_ref, got_ref, wide_own, pull_in, out_ref, pull, vec, high, low, pos, wide_got):
    rows = vec.shape[0]
    width = own_ref.shape[1]
    tiles = width // TILE_B
    places = received_places(got_ref[rows : rows + 8, :])
    out_ref[rows : rows + 8, :] = places
    wide_got[...] = spread_places(places)

    def body(odd):
        ours = slice((1 - odd) * width, (2 - odd) * width)
        others = slice(odd * width, (1 + odd) * width)
        store_vectors(vec, high, low, own_ref[0:rows, :], ours)
        store_vectors(vec, high, low, got_ref[0:rows, :], others)
        pos[:, ours] = own_ref[rows : rows + 8, :]
        pos[:, others] = places
        for r in range(tiles):
            w = r + REACH
            row = r + odd * tiles
            for j in range(w - REACH, w + REACH + 1):
                wide, base = (wide_got, odd) if j // tiles == odd else (wide_own, 1 - odd)
                if wide is wide_got or w // tiles == odd:
                    bound = bound_of(pos, w, j)
                    fill_pull(pos[:, tile_slice(w)], bound, wide, (j - base * tiles) * TILE_B, pull, row, j - w + REACH)
            out_ref[0:rows, tile_slice(r)] = apply_pulls(vec, high, low, pos, pull[row], w)

    by_parity(body)


def second_kernel(own_ref, prod_ref, prod_got_ref, pull_in, out_ref, mid_ref, gram_ref, pull, vec, high, low, pos, wide):
    rows = vec.shape[0]
    cols = rows // 3
    width = own_ref.shape[1]
    tiles = width // TILE_B
    edge = REACH * TILE_B

    def body(odd):
        sides = prod_ref, prod_got_ref
        pos[:, 0:edge] = sides[odd][rows : rows + 8, width - edge :]
        pos[:, edge : edge + width] = own_ref[rows : rows + 8, :]
        pos[:, edge + width :] = sides[1 - odd][rows : rows + 8, 0:edge]
        store_vectors(vec, high, low, prod_ref[0:rows, :], slice(odd * width, (1 + odd) * width))
        store_vectors(vec, high, low, prod_got_ref[0:rows, :], slice((1 - odd) * width, (2 - odd) * width))
        start = (1 - odd) * (tiles + REACH)
        wide[...] = spread_places(pos[:, start * TILE_B : start * TILE_B + edge])
        half = tiles // 2
        for w in range(REACH + (1 - odd) * half, REACH + (2 - odd) * half):
            for j in range(max(start, w - REACH), min(start + REACH, w + REACH + 1)):
                bound = bound_of(pos, w, j)
                fill_pull(pos[:, tile_slice(w)], bound, wide, (j - start) * TILE_B, pull, w, j - w + REACH)

    by_parity(body)
    for u in range(tiles):
        out_ref[:, tile_slice(u)] = apply_pulls(vec, high, low, pos, pull[u + REACH], u + REACH)
    mid_ref[...] = vec[:, edge : edge + width]
    gram = jnp.zeros((rows, rows), f32)
    for d in range(3):
        band = slice(d * cols, (d + 1) * cols)
        joint = jnp.concatenate(
            [own_ref[band, :], mid_ref[band, :], out_ref[band, :]], axis=0
        )
        gram += lax.dot_general(joint, joint, (((1,), (1,)), ((), ())), precision=highest, preferred_element_type=f32)
    gram_ref[...] = jnp.zeros(gram_ref.shape, f32)
    gram_ref[:, 0:rows] = gram[0:cols]
    gram_ref[:, rows : 2 * rows] = gram[cols : 2 * cols]
    gram_ref[:, 2 * rows : 2 * rows + cols] = gram[2 * cols :, 2 * cols :]


def eliminate(joint, n):
    row_of = lax.broadcasted_iota(jnp.int32, joint.shape, 0)
    col = [jnp.broadcast_to(joint[:, j : j + 1], joint.shape) for j in range(n)]
    for k in range(n):
        inverse = 1.0 / col[k][k : k + 1]
        here = row_of == k
        factor = jnp.where(here, -1.0, col[k])
        joint = jnp.where(here, 0.0, joint) - factor * (joint[k : k + 1] * inverse)
        for j in range(k + 1, n):
            col[j] = jnp.where(here, 0.0, col[j]) - factor * (col[j][k : k + 1] * inverse)
    return joint


def mul(a, b):
    return jnp.dot(a, b, precision=highest, preferred_element_type=f32)


def turned(high, both, vec):
    vec_high, vec_low = split(vec)
    n = high.shape[1]
    first = lax.dot_general(both, vec_high, (((0,), (0,)), ((), ())), preferred_element_type=f32)
    return first[0:n] + (first[n:] + lax.dot_general(high, vec_low, (((0,), (0,)), ((), ())), preferred_element_type=f32))


def last_kernel(
    bead_scale,
    own_ref,
    prod_ref,
    quad_ref,
    gram_ref,
    out_ref,
    ray_ref,
    corr_ref,
    norm_ref,
    out,
    ray,
    small,
    norm,
    sems,
):
    rows, width = prod_ref.shape
    cols = rows // 3
    row_of = lax.broadcasted_iota(jnp.int32, (cols, cols), 0)
    col_of = lax.broadcasted_iota(jnp.int32, (cols, cols), 1)
    eye = jnp.where(row_of == col_of, 1.0, 0.0).astype(f32)
    xx, xp = gram_ref[:, 0:cols], gram_ref[:, cols : 2 * cols]
    pp, pq = gram_ref[:, rows + cols : rows + 2 * cols], gram_ref[:, rows + 2 * cols : 2 * rows]
    qq = gram_ref[:, 2 * rows : 2 * rows + cols]
    joint = eliminate(jnp.concatenate([gram_ref[:, 0:rows], gram_ref[:, rows : 2 * rows]], axis=0), cols)
    shift = joint[0:cols, cols : 2 * cols]
    rest = joint[cols:, cols : 2 * cols]
    cross = joint[cols:, 2 * cols :]
    corr = xx + rest
    side = xp - 2.0 * rest + cross
    both = eliminate(jnp.concatenate([corr, side + xp], axis=1), cols)[:, cols:]
    second = both - shift
    gram = side - mul(rest, shift)
    turn = eye + shift
    squares = turn * (mul(pp, turn) - 2.0 * pq) + eye * qq - gram * second
    ray[...] = gram * (bead_scale / step_size)
    small[...] = corr * bead_scale
    norm[...] = jnp.sum(squares, axis=0, keepdims=True) * (bead_scale / step_size**2)
    copies = [
        pltpu.make_async_copy(ray, ray_ref, sems.at[0]),
        pltpu.make_async_copy(small, corr_ref, sems.at[1]),
        pltpu.make_async_copy(norm, norm_ref, sems.at[2]),
    ]
    shift_high, shift_low = split(shift)
    shift_both = jnp.concatenate([shift_high, shift_low], axis=1)
    factor_high, factor_low = split(jnp.concatenate([both, second], axis=0))
    factor_both = jnp.concatenate([factor_high, factor_low], axis=1)
    for d in range(3):
        band = slice(d * cols, (d + 1) * cols)
        vec, prod = own_ref[band, :], prod_ref[band, :]
        moved = turned(shift_high, shift_both, vec)
        base = vec - 2.0 * prod + quad_ref[band, :]
        out[band, :] = base + turned(factor_high, factor_both, jnp.concatenate([vec - prod, moved], axis=0))
        copies.append(pltpu.make_async_copy(out.at[band], out_ref.at[band], sems.at[3 + d]))
        if d == 0:
            for copy in copies:
                copy.start()
        else:
            copies[-1].start()
    for copy in copies:
        copy.wait()


def per_device(positions, trial_block, pair_tiles, pair_count):
    comps, cols, width = trial_block.shape
    rows = comps * cols
    n_tile, n_col = lax.axis_size("tile"), lax.axis_size("col")
    tiles = width // TILE_B
    assert tiles == 2 * REACH and n_col % 2 == 0
    bead_scale = 1.0 / (3.0 * n_tile * width)
    vmem = pl.BlockSpec(memory_space=pltpu.VMEM)
    smem = pl.BlockSpec(memory_space=pltpu.SMEM)
    params = pltpu.CompilerParams(vmem_limit_bytes=24 * 2**20)

    hbm = pl.BlockSpec(memory_space=pltpu.HBM)
    own = pl.pallas_call(
        pack_kernel,
        out_shape=jax.ShapeDtypeStruct((rows + 8, width), f32),
        in_specs=[hbm] * 4,
        out_specs=vmem,
        scratch_shapes=[
            pltpu.SMEM(pair_tiles.shape, jnp.int32),
            pltpu.SMEM(pair_count.shape, jnp.int32),
            pltpu.VMEM(positions.shape, f32),
            pltpu.SemaphoreType.DMA((4,)),
        ],
        compiler_params=pltpu.CompilerParams(vmem_limit_bytes=4 * 2**20),
        name="pack",
    )(*[
        pltpu.with_memory_space_constraint(x, pltpu.HBM)
        for x in (trial_block.reshape(rows, width), positions, pair_tiles, pair_count)
    ])

    halo = []
    for t in range(n_tile):
        for c in range(n_col):
            source = t - 1 if (c + t + 1) % 2 == 0 else t + 1
            if not 0 <= source < n_tile:
                source = t
            halo.append((source * n_col + (c ^ 1), t * n_col + c))
    got = lax.ppermute(own, ("tile", "col"), halo)

    def scratch(window):
        return [
            pltpu.VMEM((rows, window), f32),
            pltpu.VMEM((rows, window), bf16),
            pltpu.VMEM((rows, window), bf16),
            pltpu.VMEM((8, window), f32),
        ]

    pulls = jax.ShapeDtypeStruct((2 * tiles, (2 * REACH + 1) * TILE_B, 3 * TILE_B), bf16)
    pull, wide = pl.pallas_call(
        own_kernel,
        out_shape=(pulls, jax.ShapeDtypeStruct((width, 3 * TILE_B), f32)),
        in_specs=[vmem],
        out_specs=(vmem,) * 2,
        compiler_params=params,
        cost_estimate=pl.CostEstimate(flops=10**8, bytes_accessed=10**6, transcendentals=0),
        name="own_pulls",
    )(own)
    prod, pull = pl.pallas_call(
        first_kernel,
        out_shape=(jax.ShapeDtypeStruct((rows + 8, width), f32), pulls),
        in_specs=[vmem] * 4,
        out_specs=(vmem,) * 2,
        input_output_aliases={3: 1},
        scratch_shapes=scratch(2 * width) + [pltpu.VMEM((width, 3 * TILE_B), f32)],
        compiler_params=params,
        name="first",
    )(own, got, wide, pull)
    prod_got = lax.ppermute(prod, "col", [(c, c ^ 1) for c in range(n_col)])
    block_shape = jax.ShapeDtypeStruct((rows, width), f32)
    quad, prod, gram, pull = pl.pallas_call(
        second_kernel,
        out_shape=(block_shape, block_shape, jax.ShapeDtypeStruct((cols, 128), f32), pulls),
        in_specs=[vmem] * 4,
        out_specs=(vmem,) * 4,
        input_output_aliases={3: 3},
        scratch_shapes=scratch(2 * width) + [pltpu.VMEM((REACH * TILE_B, 3 * TILE_B), f32)],
        compiler_params=params,
        name="second",
    )(own, prod, prod_got, pull)

    def crossed(x, step):
        route = [
            (t * n_col + c, (t ^ step) * n_col + (c ^ 1)) for t in range(n_tile) for c in range(n_col)
        ]
        return lax.ppermute(x, ("tile", "col"), route)

    step = 1
    while step < n_tile:
        if 2 * step < n_tile:
            near, far, both = [crossed(gram, s) for s in (step, 2 * step, 3 * step)]
            gram = (gram + near) + (far + both)
        else:
            gram = gram + crossed(gram, step)
        step *= 4
    shapes = [(rows, width), (cols, cols), (cols, cols), (1, cols)]
    block, ray, corr, norms = pl.pallas_call(
        functools.partial(last_kernel, bead_scale),
        out_shape=tuple(jax.ShapeDtypeStruct(shape, f32) for shape in shapes),
        in_specs=[vmem] * 4,
        out_specs=(hbm,) * 4,
        scratch_shapes=[pltpu.VMEM(shape, f32) for shape in shapes] + [pltpu.SemaphoreType.DMA((6,))],
        compiler_params=params,
        name="last",
    )(own, prod, quad, gram)
    return block.reshape(comps, cols, width), ray, corr, norms.reshape(cols)


def solution(mesh):
    return jax.shard_map(
        per_device,
        mesh=mesh,
        in_specs=(
            P(None, "tile"),
            P(None, None, "tile"),
            P(None, "tile", None, None),
            P("tile", None),
        ),
        out_specs=(P(None, None, "tile"), P(), P(), P()),
        check_vma=False,
    )
```

```python
import functools

import jax
import jax.numpy as jnp
from jax import lax
from jax.experimental import pallas as pl
from jax.experimental.pallas import tpu as pltpu
from jax.sharding import PartitionSpec as P

TILE_B = 128
REACH = 2
CHUNK = 32

spring_scale = 1.0 / 64.0
cutoff_sq = 225.0
step_size = 0.2
highest = lax.Precision.HIGHEST
f32 = jnp.float32
bf16 = jnp.bfloat16


def parity():
    return lax.rem(lax.axis_index("col") + lax.axis_index("tile") + 1, 2)


def pack_kernel(vec_ref, pos_ref, tiles_ref, count_ref, out_ref, tiles, count, pos, sems):
    rows, width = vec_ref.shape
    copies = [
        pltpu.make_async_copy(tiles_ref, tiles, sems.at[0]),
        pltpu.make_async_copy(count_ref, count, sems.at[1]),
        pltpu.make_async_copy(pos_ref, pos, sems.at[2]),
        pltpu.make_async_copy(vec_ref, out_ref.at[0:rows], sems.at[3]),
    ]
    for copy in copies:
        copy.start()
    first_tile = lax.axis_index("tile") * (width // TILE_B)
    tile_of = lax.broadcasted_iota(jnp.int32, (8, width), 1) // TILE_B
    reach_of = lax.broadcasted_iota(jnp.int32, (8, width), 0) - 4
    live = jnp.zeros((8, width), f32)
    copies[0].wait()
    copies[1].wait()
    for c in range(tiles.shape[2]):
        for s in range(tiles.shape[3]):
            row = tiles[0, 0, c, s]
            reach = tiles[1, 0, c, s] - first_tile - row
            row = jnp.where(s < count[0, c], row, -1)
            live += jnp.where((tile_of == row) & (reach_of == reach), cutoff_sq, 0.0)
    out_ref[rows : rows + 8, :] = live
    copies[2].wait()
    out_ref[rows : rows + 3, :] = pos[...]
    copies[3].wait()


def split(x):
    high = x.astype(bf16)
    return high, (x - high.astype(f32)).astype(bf16)


def received_places(block):
    t = lax.axis_index("tile")
    missing = jnp.where(parity() == 0, t == 0, t == lax.axis_size("tile") - 1)
    row_of = lax.broadcasted_iota(jnp.int32, block.shape, 0)
    return jnp.where((row_of > 3) & missing, 0.0, block)


def spread_places(places):
    high, middle = split(places)
    low = (places - high.astype(f32) - middle.astype(f32)).astype(bf16)
    parts = jnp.concatenate([x.astype(f32) for x in (high, middle, low)], axis=0).astype(bf16)
    part_of = lax.broadcasted_iota(jnp.int32, (parts.shape[0], 3 * TILE_B), 0) % 8
    lane_of = lax.broadcasted_iota(jnp.int32, (parts.shape[0], 3 * TILE_B), 1) // TILE_B
    pick = jnp.where(part_of == lane_of, 1.0, 0.0).astype(bf16)
    return lax.dot_general(parts, pick, (((0,), (0,)), ((), ())), preferred_element_type=f32)


def tile_slice(w):
    return slice(w * TILE_B, (w + 1) * TILE_B)


def fill_pull(across, bound, wide, wide_base, pull, row, m):
    for q in range(0, TILE_B, CHUNK):
        down = slice(wide_base + q, wide_base + q + CHUNK)
        offset = [wide[down, tile_slice(c)] - across[c : c + 1, :] for c in range(3)]
        dist_sq = offset[0] * offset[0] + offset[1] * offset[1] + offset[2] * offset[2]
        falloff = jnp.maximum(bound - dist_sq, 0.0)
        weight = falloff * falloff / jnp.maximum(dist_sq, 1.0)
        place = slice(m * TILE_B + q, m * TILE_B + q + CHUNK)
        for c in range(3):
            pull[row, place, tile_slice(c)] = (weight * offset[c]).astype(bf16)


def by_parity(body):
    odd = parity()
    pl.when(odd == 0)(functools.partial(body, 0))
    pl.when(odd == 1)(functools.partial(body, 1))


class Tiles:
    def __init__(self, place):
        self.place = place

    def __call__(self, which, near):
        parts = []
        for w in near:
            refs, tile = self.place(w)
            parts.append(refs[which][:, tile_slice(refs.get("pos_tile", tile) if which == "pos" else tile)])
        return parts[0] if len(parts) == 1 else jnp.concatenate(parts, axis=1)

    def bound(self, w, j):
        reach = abs(w - j)
        return self("pos", [min(w, j)])[4 + reach : 5 + reach]


def sum_pulls(tiles, w, near, pull):
    middle = jnp.mean(tiles("pos", [w]), axis=1, keepdims=True)
    place = tiles("pos", near) - middle
    vec = tiles("vec", near)
    cols = vec.shape[0] // 3
    row_of = lax.broadcasted_iota(jnp.int32, place.shape, 0)
    extra = jnp.where(row_of < 3, place, jnp.where(row_of == 3, 1.0, 0.0))
    along = sum(place[d : d + 1] * vec[d * cols : (d + 1) * cols] for d in range(3))
    more_high, more_low = split(jnp.concatenate([along, extra, jnp.zeros_like(extra)], axis=0))
    left = jnp.concatenate([tiles("high", near), more_high, tiles("low", near), more_low], axis=0)
    n = left.shape[0] // 2
    first = near[0] - w + REACH
    part = slice(first * TILE_B, (first + len(near)) * TILE_B)
    total = jnp.dot(left, pull[part, :], preferred_element_type=f32)
    return total[0:n] + total[n:]


def from_sums(tiles, w, total):
    vec, pos = tiles("vec", [w]), tiles("pos", [w])
    rows = vec.shape[0]
    cols = rows // 3
    mine = pos - jnp.mean(pos, axis=1, keepdims=True)
    out = []
    for c in range(3):
        part = total[:, tile_slice(c)]
        e = rows + cols
        term = -part[rows:e]
        for d in range(3):
            diag = part[e + d : e + d + 1] - mine[d : d + 1] * part[e + 3 : e + 4]
            term += diag * vec[d * cols : (d + 1) * cols] + mine[d : d + 1] * part[d * cols : (d + 1) * cols]
        out.append(term * (spring_scale * step_size / cutoff_sq**2))
    return jnp.concatenate(out, axis=0)


def own_kernel(own_ref, pull, wide, high, low, part_ref):
    rows, width = high.shape
    tiles = width // TILE_B
    half = tiles // 2
    own = dict(vec=own_ref.at[0:rows], pos=own_ref.at[rows : rows + 8], high=high, low=low)
    mine = Tiles(lambda u: (own, u))
    wide[...] = spread_places(own["pos"][...])
    high[...], low[...] = split(own["vec"][...])
    near = [range(max(0, u - REACH), min(tiles, u + REACH + 1)) for u in range(tiles)]
    for u in range(tiles):
        for j in near[u]:
            fill_pull(mine("pos", [u]), mine.bound(u, j), wide, j * TILE_B, pull, u + REACH, j - u + REACH)

    def body(odd):
        for k in range(half):
            u = odd * half + k
            part_ref[k] = sum_pulls(mine, u, near[u], pull.at[u + REACH])

    by_parity(body)


def first_kernel(
    own_ref, got_ref, wide_own, high_own, low_own, part_ref, pull_in, out_ref, pull, places, wide_got, high_got, low_got
):
    rows, width = high_own.shape
    tiles = width // TILE_B
    places[...] = received_places(got_ref[rows : rows + 8, :])
    out_ref[rows : rows + 8, :] = places[...]
    wide_got[...] = spread_places(places[...])
    high_got[...], low_got[...] = split(got_ref[0:rows, :])
    own = dict(vec=own_ref.at[0:rows], pos=own_ref.at[rows : rows + 8], high=high_own, low=low_own, wide=wide_own)
    got = dict(vec=got_ref.at[0:rows], pos=places, high=high_got, low=low_got, wide=wide_got)

    def body(odd):
        window = Tiles(lambda w: (got if w // tiles == odd else own, w % tiles))
        for r in range(tiles):
            w = r + REACH
            row = r + odd * tiles
            inner = w // tiles != odd
            near = [j for j in range(w - REACH, w + REACH + 1) if not inner or j // tiles == odd]
            for j in near:
                refs, tile = window.place(j)
                fill_pull(
                    window("pos", [w]), window.bound(w, j), refs["wide"], tile * TILE_B, pull, row, j - w + REACH
                )
            total = sum_pulls(window, w, near, pull.at[row])
            if inner:
                total = total + part_ref[w % tiles - odd * (tiles // 2)]
            out_ref[0:rows, tile_slice(r)] = from_sums(window, w, total)

    by_parity(body)


def near_tiles(own_ref, ours, theirs, odd):
    rows, width = ours["vec"].shape
    tiles = width // TILE_B
    sides = (ours, theirs) if odd == 0 else (theirs, ours)

    def place(w):
        side = sides[w // tiles]
        if w < REACH:
            pos, tile = sides[0]["got"], w + tiles - REACH
        elif w < tiles + REACH:
            pos, tile = own_ref.at[rows : rows + 8], w - REACH
        else:
            pos, tile = sides[1]["got"], w - tiles - REACH
        return dict(side, pos=pos, pos_tile=tile), w % tiles

    return Tiles(place)


def middle_kernel(own_ref, prod_ref, pull, part_ref, high, low):
    rows, width = high.shape
    tiles = width // TILE_B
    high[...], low[...] = split(prod_ref[0:rows, :])
    ours = dict(vec=prod_ref.at[0:rows], got=prod_ref.at[rows : rows + 8], high=high, low=low)

    def body(odd):
        window = near_tiles(own_ref, ours, ours, odd)
        for u in range(tiles):
            w = u + REACH
            near = [j for j in range(w - REACH, w + REACH + 1) if j // tiles == odd]
            part_ref[u] = sum_pulls(window, w, near, pull.at[w])

    by_parity(body)


def second_kernel(own_ref, prod_ref, prod_got_ref, part_ref, pull_in, out_ref, mid_ref, gram_ref, pull, high, low, wide):
    rows, width = high.shape
    cols = rows // 3
    tiles = width // TILE_B
    edge = REACH * TILE_B
    high[...], low[...] = split(prod_got_ref[0:rows, :])
    ours = dict(vec=prod_ref.at[0:rows], got=prod_ref.at[rows : rows + 8])
    theirs = dict(vec=prod_got_ref.at[0:rows], got=prod_got_ref.at[rows : rows + 8], high=high, low=low)

    def body(odd):
        window = near_tiles(own_ref, ours, theirs, odd)
        start = (1 - odd) * (tiles + REACH)
        wide[...] = spread_places(window("pos", range(start, start + REACH)))
        for u in range(tiles):
            w = u + REACH
            near = [j for j in range(w - REACH, w + REACH + 1) if j // tiles != odd]
            for j in near:
                if start <= j < start + REACH:
                    fill_pull(
                        window("pos", [w]), window.bound(w, j), wide, (j - start) * TILE_B, pull, w, j - w + REACH
                    )
            total = part_ref[u] + sum_pulls(window, w, near, pull.at[w])
            out_ref[:, tile_slice(u)] = from_sums(window, w, total)
            mid_ref[:, tile_slice(u)] = window("vec", [w])

    by_parity(body)
    bands = [slice(d * cols, (d + 1) * cols) for d in range(3)]
    joint = jnp.concatenate(
        [jnp.concatenate([own_ref[band, :], mid_ref[band, :], out_ref[band, :]], axis=0) for band in bands], axis=1
    )
    joint = jnp.concatenate(split(joint), axis=0)
    gram = lax.dot_general(joint, joint, (((1,), (1,)), ((), ())), preferred_element_type=f32)
    gram = gram[0:rows, 0:rows] + (gram[0:rows, rows:] + gram[rows:, 0:rows] + gram[rows:, rows:])
    gram_ref[...] = jnp.zeros(gram_ref.shape, f32)
    gram_ref[:, 0:rows] = gram[0:cols]
    gram_ref[:, rows : 2 * rows] = gram[cols : 2 * cols]
    gram_ref[:, 2 * rows : 2 * rows + cols] = gram[2 * cols :, 2 * cols :]


def eliminate(joint, n):
    row_of = lax.broadcasted_iota(jnp.int32, joint.shape, 0)
    col = [jnp.broadcast_to(joint[:, j : j + 1], joint.shape) for j in range(n)]
    for k in range(n):
        inverse = 1.0 / col[k][k : k + 1]
        here = row_of == k
        factor = jnp.where(here, -1.0, col[k])
        joint = jnp.where(here, 0.0, joint) - factor * (joint[k : k + 1] * inverse)
        for j in range(k + 1, n):
            col[j] = jnp.where(here, 0.0, col[j]) - factor * (col[j][k : k + 1] * inverse)
    return joint


def mul(a, b):
    return jnp.dot(a, b, precision=highest, preferred_element_type=f32)


def turned(high, both, vec):
    vec_high, vec_low = split(vec)
    n = high.shape[1]
    first = lax.dot_general(both, vec_high, (((0,), (0,)), ((), ())), preferred_element_type=f32)
    return first[0:n] + (first[n:] + lax.dot_general(high, vec_low, (((0,), (0,)), ((), ())), preferred_element_type=f32))


def last_kernel(
    bead_scale,
    own_ref,
    prod_ref,
    quad_ref,
    gram_ref,
    out_ref,
    ray_ref,
    corr_ref,
    norm_ref,
    out,
    ray,
    small,
    norm,
    sems,
):
    rows, width = prod_ref.shape
    cols = rows // 3
    row_of = lax.broadcasted_iota(jnp.int32, (cols, cols), 0)
    col_of = lax.broadcasted_iota(jnp.int32, (cols, cols), 1)
    eye = jnp.where(row_of == col_of, 1.0, 0.0).astype(f32)
    xx, xp = gram_ref[:, 0:cols], gram_ref[:, cols : 2 * cols]
    pp, pq = gram_ref[:, rows + cols : rows + 2 * cols], gram_ref[:, rows + 2 * cols : 2 * rows]
    qq = gram_ref[:, 2 * rows : 2 * rows + cols]
    joint = eliminate(jnp.concatenate([gram_ref[:, 0:rows], gram_ref[:, rows : 2 * rows]], axis=0), cols)
    shift = joint[0:cols, cols : 2 * cols]
    rest = joint[cols:, cols : 2 * cols]
    cross = joint[cols:, 2 * cols :]
    corr = xx + rest
    side = xp - 2.0 * rest + cross
    both = eliminate(jnp.concatenate([corr, side + xp], axis=1), cols)[:, cols:]
    second = both - shift
    gram = side - mul(rest, shift)
    turn = eye + shift
    squares = turn * (mul(pp, turn) - 2.0 * pq) + eye * qq - gram * second
    ray[...] = gram * (bead_scale / step_size)
    small[...] = corr * bead_scale
    norm[...] = jnp.sum(squares, axis=0, keepdims=True) * (bead_scale / step_size**2)
    copies = [
        pltpu.make_async_copy(ray, ray_ref, sems.at[0]),
        pltpu.make_async_copy(small, corr_ref, sems.at[1]),
        pltpu.make_async_copy(norm, norm_ref, sems.at[2]),
    ]
    shift_high, shift_low = split(shift)
    shift_both = jnp.concatenate([shift_high, shift_low], axis=1)
    factor_high, factor_low = split(jnp.concatenate([both, second], axis=0))
    factor_both = jnp.concatenate([factor_high, factor_low], axis=1)
    for d in range(3):
        band = slice(d * cols, (d + 1) * cols)
        vec, prod = own_ref[band, :], prod_ref[band, :]
        moved = turned(shift_high, shift_both, vec)
        base = vec - 2.0 * prod + quad_ref[band, :]
        out[band, :] = base + turned(factor_high, factor_both, jnp.concatenate([vec - prod, moved], axis=0))
        copies.append(pltpu.make_async_copy(out.at[band], out_ref.at[band], sems.at[3 + d]))
        if d == 0:
            for copy in copies:
                copy.start()
        else:
            copies[-1].start()
    for copy in copies:
        copy.wait()


def per_device(positions, trial_block, pair_tiles, pair_count):
    comps, cols, width = trial_block.shape
    rows = comps * cols
    n_tile, n_col = lax.axis_size("tile"), lax.axis_size("col")
    tiles = width // TILE_B
    assert tiles == 2 * REACH and n_col % 2 == 0
    bead_scale = 1.0 / (3.0 * n_tile * width)
    vmem = pl.BlockSpec(memory_space=pltpu.VMEM)
    smem = pl.BlockSpec(memory_space=pltpu.SMEM)
    params = pltpu.CompilerParams(vmem_limit_bytes=24 * 2**20)

    hbm = pl.BlockSpec(memory_space=pltpu.HBM)
    own = pl.pallas_call(
        pack_kernel,
        out_shape=jax.ShapeDtypeStruct((rows + 8, width), f32),
        in_specs=[hbm] * 4,
        out_specs=vmem,
        scratch_shapes=[
            pltpu.SMEM(pair_tiles.shape, jnp.int32),
            pltpu.SMEM(pair_count.shape, jnp.int32),
            pltpu.VMEM(positions.shape, f32),
            pltpu.SemaphoreType.DMA((4,)),
        ],
        compiler_params=pltpu.CompilerParams(vmem_limit_bytes=4 * 2**20),
        name="pack",
    )(*[
        pltpu.with_memory_space_constraint(x, pltpu.HBM)
        for x in (trial_block.reshape(rows, width), positions, pair_tiles, pair_count)
    ])

    halo = []
    for t in range(n_tile):
        for c in range(n_col):
            source = t - 1 if (c + t + 1) % 2 == 0 else t + 1
            if not 0 <= source < n_tile:
                source = t
            halo.append((source * n_col + (c ^ 1), t * n_col + c))
    got = lax.ppermute(own, ("tile", "col"), halo)

    def f32_array(*shape):
        return jax.ShapeDtypeStruct(shape, f32)

    def bf16_array(*shape):
        return jax.ShapeDtypeStruct(shape, bf16)

    parts = [pltpu.VMEM((rows, width), bf16)] * 2
    sums = rows + cols + 16
    pulls = bf16_array(2 * tiles, (2 * REACH + 1) * TILE_B, 3 * TILE_B)
    hidden = pl.CostEstimate(flops=10**8, bytes_accessed=10**6, transcendentals=0)
    pull, wide, high, low, part = pl.pallas_call(
        own_kernel,
        out_shape=(
            pulls,
            f32_array(width, 3 * TILE_B),
            bf16_array(rows, width),
            bf16_array(rows, width),
            f32_array(tiles // 2, sums, 3 * TILE_B),
        ),
        in_specs=[vmem],
        out_specs=(vmem,) * 5,
        compiler_params=params,
        cost_estimate=hidden,
        name="own_pulls",
    )(own)
    prod, pull = pl.pallas_call(
        first_kernel,
        out_shape=(f32_array(rows + 8, width), pulls),
        in_specs=[vmem] * 7,
        out_specs=(vmem,) * 2,
        input_output_aliases={6: 1},
        scratch_shapes=[pltpu.VMEM((8, width), f32), pltpu.VMEM((width, 3 * TILE_B), f32)] + parts,
        compiler_params=params,
        name="first",
    )(own, got, wide, high, low, part, pull)
    prod_got = lax.ppermute(prod, "col", [(c, c ^ 1) for c in range(n_col)])
    part = pl.pallas_call(
        middle_kernel,
        out_shape=f32_array(tiles, sums, 3 * TILE_B),
        in_specs=[vmem] * 3,
        out_specs=vmem,
        scratch_shapes=parts,
        compiler_params=params,
        cost_estimate=hidden,
        name="middle",
    )(own, prod, pull)
    quad, prod, gram, pull = pl.pallas_call(
        second_kernel,
        out_shape=(f32_array(rows, width), f32_array(rows, width), f32_array(cols, 128), pulls),
        in_specs=[vmem] * 5,
        out_specs=(vmem,) * 4,
        input_output_aliases={4: 3},
        scratch_shapes=parts + [pltpu.VMEM((REACH * TILE_B, 3 * TILE_B), f32)],
        compiler_params=params,
        name="second",
    )(own, prod, prod_got, part, pull)

    def crossed(x, step):
        route = [
            (t * n_col + c, (t ^ step) * n_col + (c ^ 1)) for t in range(n_tile) for c in range(n_col)
        ]
        return lax.ppermute(x, ("tile", "col"), route)

    step = 1
    while step < n_tile:
        if 2 * step < n_tile:
            near, far, both = [crossed(gram, s) for s in (step, 2 * step, 3 * step)]
            gram = (gram + near) + (far + both)
        else:
            gram = gram + crossed(gram, step)
        step *= 4
    shapes = [(rows, width), (cols, cols), (cols, cols), (1, cols)]
    block, ray, corr, norms = pl.pallas_call(
        functools.partial(last_kernel, bead_scale),
        out_shape=tuple(jax.ShapeDtypeStruct(shape, f32) for shape in shapes),
        in_specs=[vmem] * 4,
        out_specs=(hbm,) * 4,
        scratch_shapes=[pltpu.VMEM(shape, f32) for shape in shapes] + [pltpu.SemaphoreType.DMA((6,))],
        compiler_params=params,
        name="last",
    )(own, prod, quad, gram)
    return block.reshape(comps, cols, width), ray, corr, norms.reshape(cols)


def solution(mesh):
    return jax.shard_map(
        per_device,
        mesh=mesh,
        in_specs=(
            P(None, "tile"),
            P(None, None, "tile"),
            P(None, "tile", None, None),
            P("tile", None),
        ),
        out_specs=(P(None, None, "tile"), P(), P(), P()),
        check_vma=False,
    )
```

```python
import functools

import jax
import jax.numpy as jnp
from jax import lax
from jax.experimental import pallas as pl
from jax.experimental.pallas import tpu as pltpu
from jax.sharding import PartitionSpec as P

TILE_B = 128
REACH = 2
CHUNK = 32

spring_scale = 1.0 / 64.0
cutoff_sq = 225.0
step_size = 0.2
highest = lax.Precision.HIGHEST
f32 = jnp.float32
bf16 = jnp.bfloat16


def parity():
    return lax.rem(lax.axis_index("col") + lax.axis_index("tile") + 1, 2)


def pack_kernel(vec_ref, pos_ref, tiles_ref, count_ref, near_ref, far_ref, tiles, count, pos, sems):
    rows, width = vec_ref.shape
    half = width // 2
    near = pl.ds(pl.multiple_of((1 - parity()) * half, TILE_B), half)
    far = pl.ds(pl.multiple_of(parity() * half, TILE_B), half)
    copies = [
        pltpu.make_async_copy(tiles_ref, tiles, sems.at[0]),
        pltpu.make_async_copy(count_ref, count, sems.at[1]),
        pltpu.make_async_copy(pos_ref, pos, sems.at[2]),
        pltpu.make_async_copy(vec_ref.at[:, near], near_ref.at[0:rows], sems.at[3]),
        pltpu.make_async_copy(vec_ref.at[:, far], far_ref, sems.at[4]),
    ]
    for copy in copies:
        copy.start()
    first_tile = lax.axis_index("tile") * (width // TILE_B)
    tile_of = lax.broadcasted_iota(jnp.int32, (8, width), 1) // TILE_B
    reach_of = lax.broadcasted_iota(jnp.int32, (8, width), 0) - 4
    live = jnp.zeros((8, width), f32)
    copies[0].wait()
    copies[1].wait()
    for c in range(tiles.shape[2]):
        for s in range(tiles.shape[3]):
            row = tiles[0, 0, c, s]
            reach = tiles[1, 0, c, s] - first_tile - row
            row = jnp.where(s < count[0, c], row, -1)
            live += jnp.where((tile_of == row) & (reach_of == reach), cutoff_sq, 0.0)
    copies[2].wait()
    for n in range(2):
        place = slice(rows + 8 * n, rows + 8 * n + 8)
        part = slice(n * half, (n + 1) * half)
        near_ref[place, :] = live[:, part]
        near_ref[rows + 8 * n : rows + 8 * n + 3, :] = pos[:, part]
    copies[3].wait()
    copies[4].wait()


def joined_places(near):
    rows = near.shape[0] - 16
    return jnp.concatenate([near[rows : rows + 8, :], near[rows + 8 :, :]], axis=1)


def split(x):
    high = x.astype(bf16)
    return high, (x - high.astype(f32)).astype(bf16)


def received_places(block):
    t = lax.axis_index("tile")
    missing = jnp.where(parity() == 0, t == 0, t == lax.axis_size("tile") - 1)
    row_of = lax.broadcasted_iota(jnp.int32, block.shape, 0)
    return jnp.where((row_of > 3) & missing, 0.0, block)


def spread_places(places):
    high, middle = split(places)
    low = (places - high.astype(f32) - middle.astype(f32)).astype(bf16)
    parts = jnp.concatenate([x.astype(f32) for x in (high, middle, low)], axis=0).astype(bf16)
    part_of = lax.broadcasted_iota(jnp.int32, (parts.shape[0], 3 * TILE_B), 0) % 8
    lane_of = lax.broadcasted_iota(jnp.int32, (parts.shape[0], 3 * TILE_B), 1) // TILE_B
    pick = jnp.where(part_of == lane_of, 1.0, 0.0).astype(bf16)
    return lax.dot_general(parts, pick, (((0,), (0,)), ((), ())), preferred_element_type=f32)


def tile_slice(w):
    return slice(w * TILE_B, (w + 1) * TILE_B)


def fill_pull(across, bound, wide, wide_base, pull, row, m):
    for q in range(0, TILE_B, CHUNK):
        down = slice(wide_base + q, wide_base + q + CHUNK)
        offset = [wide[down, tile_slice(c)] - across[c : c + 1, :] for c in range(3)]
        dist_sq = offset[0] * offset[0] + offset[1] * offset[1] + offset[2] * offset[2]
        falloff = jnp.maximum(bound - dist_sq, 0.0)
        weight = falloff * falloff / jnp.maximum(dist_sq, 1.0)
        place = slice(m * TILE_B + q, m * TILE_B + q + CHUNK)
        for c in range(3):
            pull[row, place, tile_slice(c)] = (weight * offset[c]).astype(bf16)


def by_parity(body):
    odd = parity()
    pl.when(odd == 0)(functools.partial(body, 0))
    pl.when(odd == 1)(functools.partial(body, 1))


class Tiles:
    def __init__(self, place):
        self.place = place

    def __call__(self, which, near):
        parts = []
        for w in near:
            refs, tile = self.place(w)
            parts.append(refs[which][:, tile_slice(refs.get("pos_tile", tile) if which == "pos" else tile)])
        return parts[0] if len(parts) == 1 else jnp.concatenate(parts, axis=1)

    def bound(self, w, j):
        reach = abs(w - j)
        return self("pos", [min(w, j)])[4 + reach : 5 + reach]


def sum_pulls(tiles, w, near, pull):
    middle = jnp.mean(tiles("pos", [w]), axis=1, keepdims=True)
    place = tiles("pos", near) - middle
    vec = tiles("vec", near)
    cols = vec.shape[0] // 3
    row_of = lax.broadcasted_iota(jnp.int32, place.shape, 0)
    extra = jnp.where(row_of < 3, place, jnp.where(row_of == 3, 1.0, 0.0))
    along = sum(place[d : d + 1] * vec[d * cols : (d + 1) * cols] for d in range(3))
    more_high, more_low = split(jnp.concatenate([along, extra, jnp.zeros_like(extra)], axis=0))
    left = jnp.concatenate([tiles("high", near), more_high, tiles("low", near), more_low], axis=0)
    n = left.shape[0] // 2
    first = near[0] - w + REACH
    part = slice(first * TILE_B, (first + len(near)) * TILE_B)
    total = jnp.dot(left, pull[part, :], preferred_element_type=f32)
    return total[0:n] + total[n:]


def from_sums(tiles, w, total):
    vec, pos = tiles("vec", [w]), tiles("pos", [w])
    rows = vec.shape[0]
    cols = rows // 3
    mine = pos - jnp.mean(pos, axis=1, keepdims=True)
    out = []
    for c in range(3):
        part = total[:, tile_slice(c)]
        e = rows + cols
        term = -part[rows:e]
        for d in range(3):
            diag = part[e + d : e + d + 1] - mine[d : d + 1] * part[e + 3 : e + 4]
            term += diag * vec[d * cols : (d + 1) * cols] + mine[d : d + 1] * part[d * cols : (d + 1) * cols]
        out.append(term * (spring_scale * step_size / cutoff_sq**2))
    return jnp.concatenate(out, axis=0)


def own_kernel(vec_ref, sent_ref, own_ref, pull, wide, high, low, part_ref, sem):
    rows, width = high.shape
    copy = pltpu.make_async_copy(vec_ref, own_ref.at[0:rows], sem)
    copy.start()
    own_ref[rows : rows + 8, :] = joined_places(sent_ref)
    tiles = width // TILE_B
    half = tiles // 2
    own = dict(vec=own_ref.at[0:rows], pos=own_ref.at[rows : rows + 8], high=high, low=low)
    mine = Tiles(lambda u: (own, u))
    wide[...] = spread_places(own["pos"][...])
    near = [range(max(0, u - REACH), min(tiles, u + REACH + 1)) for u in range(tiles)]
    for u in range(tiles):
        for j in near[u]:
            fill_pull(mine("pos", [u]), mine.bound(u, j), wide, j * TILE_B, pull, u + REACH, j - u + REACH)
    copy.wait()
    high[...], low[...] = split(own["vec"][...])

    def body(odd):
        for k in range(half):
            u = odd * half + k
            part_ref[k] = sum_pulls(mine, u, near[u], pull.at[u + REACH])

    by_parity(body)


def outer_kernel(own_ref, got_ref, wide_own, pull_in, pull, places, wide_got):
    width = wide_own.shape[0]
    rows = own_ref.shape[0] - 8
    tiles = width // TILE_B
    places[...] = received_places(joined_places(got_ref))
    wide_got[...] = spread_places(places[...])
    own = dict(pos=own_ref.at[rows : rows + 8], wide=wide_own)
    got = dict(pos=places, wide=wide_got)

    def body(odd):
        window = Tiles(lambda w: (got if w // tiles == odd else own, w % tiles))
        for r in range(tiles):
            w = r + REACH
            for j in range(w - REACH, w + REACH + 1):
                if w // tiles == odd or j // tiles == odd:
                    refs, tile = window.place(j)
                    across, bound = window("pos", [w]), window.bound(w, j)
                    fill_pull(across, bound, refs["wide"], tile * TILE_B, pull, r + odd * tiles, j - w + REACH)

    by_parity(body)


def first_kernel(own_ref, near_ref, far_ref, places, high_own, low_own, part_ref, pull, out_ref, *parts):
    rows, width = high_own.shape
    tiles = width // TILE_B
    half = tiles // 2
    out_ref[rows : rows + 8, :] = places[...]
    own = dict(vec=own_ref.at[0:rows], pos=own_ref.at[rows : rows + 8], high=high_own, low=low_own)
    got = []
    for vec, high, low in zip((near_ref.at[0:rows], far_ref), parts[0::2], parts[1::2]):
        high[...], low[...] = split(vec[...])
        got.append(dict(vec=vec, pos=places, high=high, low=low))

    def body(odd):
        def place(w):
            if w // tiles != odd:
                return own, w % tiles
            tile = w % tiles
            return dict(got[0 if tile // half != odd else 1], pos_tile=tile), tile % half

        window = Tiles(place)
        for r in range(tiles):
            w = r + REACH
            inner = w // tiles != odd
            near = [j for j in range(w - REACH, w + REACH + 1) if not inner or j // tiles == odd]
            total = sum_pulls(window, w, near, pull.at[r + odd * tiles])
            if inner:
                total = total + part_ref[w % tiles - odd * (tiles // 2)]
            out_ref[0:rows, tile_slice(r)] = from_sums(window, w, total)

    by_parity(body)


def near_tiles(own_ref, ours, theirs, odd):
    rows, width = ours["vec"].shape
    tiles = width // TILE_B
    sides = (ours, theirs) if odd == 0 else (theirs, ours)

    def place(w):
        side = sides[w // tiles]
        if w < REACH:
            pos, tile = sides[0]["got"], w + tiles - REACH
        elif w < tiles + REACH:
            pos, tile = own_ref.at[rows : rows + 8], w - REACH
        else:
            pos, tile = sides[1]["got"], w - tiles - REACH
        return dict(side, pos=pos, pos_tile=tile), w % tiles

    return Tiles(place)


def middle_kernel(own_ref, prod_ref, pull, part_ref, high, low):
    rows, width = high.shape
    tiles = width // TILE_B
    high[...], low[...] = split(prod_ref[0:rows, :])
    ours = dict(vec=prod_ref.at[0:rows], got=prod_ref.at[rows : rows + 8], high=high, low=low)

    def body(odd):
        window = near_tiles(own_ref, ours, ours, odd)
        for u in range(tiles):
            w = u + REACH
            near = [j for j in range(w - REACH, w + REACH + 1) if j // tiles == odd]
            part_ref[u] = sum_pulls(window, w, near, pull.at[w])

    by_parity(body)


def second_kernel(own_ref, prod_ref, prod_got_ref, part_ref, pull_in, out_ref, mid_ref, gram_ref, pull, high, low, wide, sums):
    rows, width = high.shape
    cols = rows // 3
    tiles = width // TILE_B
    edge = REACH * TILE_B
    high[...], low[...] = split(prod_got_ref[0:rows, :])
    ours = dict(vec=prod_ref.at[0:rows], got=prod_ref.at[rows : rows + 8])
    theirs = dict(vec=prod_got_ref.at[0:rows], got=prod_got_ref.at[rows : rows + 8], high=high, low=low)

    def body(odd):
        window = near_tiles(own_ref, ours, theirs, odd)
        start = (1 - odd) * (tiles + REACH)
        wide[...] = spread_places(window("pos", range(start, start + REACH)))
        for u in range(tiles):
            w = u + REACH
            near = [j for j in range(w - REACH, w + REACH + 1) if j // tiles != odd]
            for j in near:
                if start <= j < start + REACH:
                    fill_pull(
                        window("pos", [w]), window.bound(w, j), wide, (j - start) * TILE_B, pull, w, j - w + REACH
                    )
            sums[u] = part_ref[u] + sum_pulls(window, w, near, pull.at[w])
            mid_ref[:, tile_slice(u)] = window("vec", [w])

    by_parity(body)
    own = dict(vec=mid_ref, pos=own_ref.at[rows : rows + 8])
    mine = Tiles(lambda u: (own, u))
    for u in range(tiles):
        out_ref[:, tile_slice(u)] = from_sums(mine, u, sums[u])
    bands = [slice(d * cols, (d + 1) * cols) for d in range(3)]
    joint = jnp.concatenate(
        [jnp.concatenate([own_ref[band, :], mid_ref[band, :], out_ref[band, :]], axis=0) for band in bands], axis=1
    )
    joint = jnp.concatenate(split(joint), axis=0)
    gram = lax.dot_general(joint, joint, (((1,), (1,)), ((), ())), preferred_element_type=f32)
    gram = gram[0:rows, 0:rows] + (gram[0:rows, rows:] + gram[rows:, 0:rows] + gram[rows:, rows:])
    gram_ref[...] = jnp.zeros(gram_ref.shape, f32)
    gram_ref[:, 0:rows] = gram[0:cols]
    gram_ref[:, rows : 2 * rows] = gram[cols : 2 * cols]
    gram_ref[:, 2 * rows : 2 * rows + cols] = gram[2 * cols :, 2 * cols :]


def eliminate(joint, n):
    row_of = lax.broadcasted_iota(jnp.int32, joint.shape, 0)
    col = [jnp.broadcast_to(joint[:, j : j + 1], joint.shape) for j in range(n)]
    for k in range(n):
        inverse = 1.0 / col[k][k : k + 1]
        here = row_of == k
        factor = jnp.where(here, -1.0, col[k])
        joint = jnp.where(here, 0.0, joint) - factor * (joint[k : k + 1] * inverse)
        for j in range(k + 1, n):
            col[j] = jnp.where(here, 0.0, col[j]) - factor * (col[j][k : k + 1] * inverse)
    return joint


def mul(a, b):
    return jnp.dot(a, b, precision=highest, preferred_element_type=f32)


def turned(high, both, vec_high, vec_low):
    n = high.shape[1]
    first = lax.dot_general(both, vec_high, (((0,), (0,)), ((), ())), preferred_element_type=f32)
    return first[0:n] + (first[n:] + lax.dot_general(high, vec_low, (((0,), (0,)), ((), ())), preferred_element_type=f32))


def last_kernel(
    bead_scale,
    own_ref,
    prod_ref,
    quad_ref,
    gram_ref,
    out_ref,
    ray_ref,
    corr_ref,
    norm_ref,
    out,
    ray,
    small,
    norm,
    sems,
):
    rows, width = prod_ref.shape
    cols = rows // 3
    row_of = lax.broadcasted_iota(jnp.int32, (cols, cols), 0)
    col_of = lax.broadcasted_iota(jnp.int32, (cols, cols), 1)
    eye = jnp.where(row_of == col_of, 1.0, 0.0).astype(f32)
    xx, xp = gram_ref[:, 0:cols], gram_ref[:, cols : 2 * cols]
    pp, pq = gram_ref[:, rows + cols : rows + 2 * cols], gram_ref[:, rows + 2 * cols : 2 * rows]
    qq = gram_ref[:, 2 * rows : 2 * rows + cols]
    joint = eliminate(jnp.concatenate([gram_ref[:, 0:rows], gram_ref[:, rows : 2 * rows]], axis=0), cols)
    shift = joint[0:cols, cols : 2 * cols]
    rest = joint[cols:, cols : 2 * cols]
    cross = joint[cols:, 2 * cols :]
    corr = xx + rest
    side = xp - 2.0 * rest + cross
    gram = side - mul(rest, shift)
    turn = eye + shift
    squares = turn * (mul(pp, turn) - 2.0 * pq) + eye * qq
    ray[...] = gram * (bead_scale / step_size)
    small[...] = corr * bead_scale
    copies = [
        pltpu.make_async_copy(ray, ray_ref, sems.at[0]),
        pltpu.make_async_copy(small, corr_ref, sems.at[1]),
        pltpu.make_async_copy(norm, norm_ref, sems.at[2]),
    ]
    shift_high, shift_low = split(shift)
    shift_both = jnp.concatenate([shift_high, shift_low], axis=1)
    bands = [slice(d * cols, (d + 1) * cols) for d in range(3)]
    right = []
    for band in bands:
        vec, prod = own_ref[band, :], prod_ref[band, :]
        moved = turned(shift_high, shift_both, *split(vec))
        out[band, :] = vec - 2.0 * prod + quad_ref[band, :]
        right.append(split(jnp.concatenate([vec - prod, moved], axis=0)))
    both = eliminate(jnp.concatenate([corr, side + xp], axis=1), cols)[:, cols:]
    second = both - shift
    norm[...] = jnp.sum(squares - gram * second, axis=0, keepdims=True) * (bead_scale / step_size**2)
    factor_high, factor_low = split(jnp.concatenate([both, second], axis=0))
    factor_both = jnp.concatenate([factor_high, factor_low], axis=1)
    for d, band in enumerate(bands):
        out[band, :] += turned(factor_high, factor_both, *right[d])
        copies.append(pltpu.make_async_copy(out.at[band], out_ref.at[band], sems.at[3 + d]))
        if d == 0:
            for copy in copies:
                copy.start()
        else:
            copies[-1].start()
    for copy in copies:
        copy.wait()


def per_device(positions, trial_block, pair_tiles, pair_count):
    comps, cols, width = trial_block.shape
    rows = comps * cols
    n_tile, n_col = lax.axis_size("tile"), lax.axis_size("col")
    tiles = width // TILE_B
    assert tiles == 2 * REACH and n_col % 2 == 0
    bead_scale = 1.0 / (3.0 * n_tile * width)
    vmem = pl.BlockSpec(memory_space=pltpu.VMEM)
    smem = pl.BlockSpec(memory_space=pltpu.SMEM)
    params = pltpu.CompilerParams(vmem_limit_bytes=24 * 2**20)

    def f32_array(*shape):
        return jax.ShapeDtypeStruct(shape, f32)

    def bf16_array(*shape):
        return jax.ShapeDtypeStruct(shape, bf16)

    hbm = pl.BlockSpec(memory_space=pltpu.HBM)
    vectors, *tables = [
        pltpu.with_memory_space_constraint(x, pltpu.HBM)
        for x in (trial_block.reshape(rows, width), positions, pair_tiles, pair_count)
    ]
    near, far = pl.pallas_call(
        pack_kernel,
        out_shape=(f32_array(rows + 16, width // 2), f32_array(rows, width // 2)),
        in_specs=[hbm] * 4,
        out_specs=(vmem,) * 2,
        scratch_shapes=[
            pltpu.SMEM(pair_tiles.shape, jnp.int32),
            pltpu.SMEM(pair_count.shape, jnp.int32),
            pltpu.VMEM(positions.shape, f32),
            pltpu.SemaphoreType.DMA((5,)),
        ],
        compiler_params=pltpu.CompilerParams(vmem_limit_bytes=4 * 2**20),
        name="pack",
    )(vectors, *tables)

    halo = []
    for t in range(n_tile):
        for c in range(n_col):
            source = t - 1 if (c + t + 1) % 2 == 0 else t + 1
            if not 0 <= source < n_tile:
                source = t
            halo.append((source * n_col + (c ^ 1), t * n_col + c))
    got_near = lax.ppermute(near, ("tile", "col"), halo)
    got_far = lax.ppermute(far, ("tile", "col"), halo)

    parts = [pltpu.VMEM((rows, width), bf16)] * 2
    sums = (rows + cols + 16, 3 * TILE_B)
    pulls = bf16_array(2 * tiles, (2 * REACH + 1) * TILE_B, 3 * TILE_B)
    hidden = pl.CostEstimate(flops=10**8, bytes_accessed=10**6, transcendentals=0)
    own, pull, wide, high, low, part = pl.pallas_call(
        own_kernel,
        out_shape=(
            f32_array(rows + 8, width),
            pulls,
            f32_array(width, 3 * TILE_B),
            bf16_array(rows, width),
            bf16_array(rows, width),
            f32_array(tiles // 2, *sums),
        ),
        in_specs=[hbm, vmem],
        out_specs=(vmem,) * 6,
        scratch_shapes=[pltpu.SemaphoreType.DMA(())],
        compiler_params=params,
        cost_estimate=hidden,
        name="own_pulls",
    )(vectors, near)
    pull, places = pl.pallas_call(
        outer_kernel,
        out_shape=(pulls, f32_array(8, width)),
        in_specs=[vmem] * 4,
        out_specs=(vmem,) * 2,
        input_output_aliases={3: 0},
        scratch_shapes=[pltpu.VMEM((width, 3 * TILE_B), f32)],
        compiler_params=params,
        cost_estimate=hidden,
        name="outer_pulls",
    )(own, got_near, wide, pull)
    prod = pl.pallas_call(
        first_kernel,
        out_shape=f32_array(rows + 8, width),
        in_specs=[vmem] * 8,
        out_specs=vmem,
        scratch_shapes=[pltpu.VMEM((rows, width // 2), bf16)] * 4,
        compiler_params=params,
        name="first",
    )(own, got_near, got_far, places, high, low, part, pull)
    prod_got = lax.ppermute(prod, "col", [(c, c ^ 1) for c in range(n_col)])
    part = pl.pallas_call(
        middle_kernel,
        out_shape=f32_array(tiles, *sums),
        in_specs=[vmem] * 3,
        out_specs=vmem,
        scratch_shapes=parts,
        compiler_params=params,
        cost_estimate=hidden,
        name="middle",
    )(own, prod, pull)
    quad, prod, gram, pull = pl.pallas_call(
        second_kernel,
        out_shape=(f32_array(rows, width), f32_array(rows, width), f32_array(cols, 128), pulls),
        in_specs=[vmem] * 5,
        out_specs=(vmem,) * 4,
        input_output_aliases={4: 3},
        scratch_shapes=parts + [pltpu.VMEM((REACH * TILE_B, 3 * TILE_B), f32), pltpu.VMEM((tiles, *sums), f32)],
        compiler_params=params,
        name="second",
    )(own, prod, prod_got, part, pull)

    def crossed(x, step):
        route = [
            (t * n_col + c, (t ^ step) * n_col + (c ^ 1)) for t in range(n_tile) for c in range(n_col)
        ]
        return lax.ppermute(x, ("tile", "col"), route)

    step = 1
    while step < n_tile:
        if 2 * step < n_tile:
            near, far, both = [crossed(gram, s) for s in (step, 2 * step, 3 * step)]
            gram = (gram + near) + (far + both)
        else:
            gram = gram + crossed(gram, step)
        step *= 4
    shapes = [(rows, width), (cols, cols), (cols, cols), (1, cols)]
    block, ray, corr, norms = pl.pallas_call(
        functools.partial(last_kernel, bead_scale),
        out_shape=tuple(jax.ShapeDtypeStruct(shape, f32) for shape in shapes),
        in_specs=[vmem] * 4,
        out_specs=(hbm,) * 4,
        scratch_shapes=[pltpu.VMEM(shape, f32) for shape in shapes] + [pltpu.SemaphoreType.DMA((6,))],
        compiler_params=params,
        name="last",
    )(own, prod, quad, gram)
    return block.reshape(comps, cols, width), ray, corr, norms.reshape(cols)


def solution(mesh):
    return jax.shard_map(
        per_device,
        mesh=mesh,
        in_specs=(
            P(None, "tile"),
            P(None, None, "tile"),
            P(None, "tile", None, None),
            P("tile", None),
        ),
        out_specs=(P(None, None, "tile"), P(), P(), P()),
        check_vma=False,
    )
```

```python
import functools

import jax
import jax.numpy as jnp
from jax import lax
from jax.experimental import pallas as pl
from jax.experimental.pallas import tpu as pltpu
from jax.sharding import PartitionSpec as P

TILE_B = 128
REACH = 2
CHUNK = 32

spring_scale = 1.0 / 64.0
cutoff_sq = 225.0
step_size = 0.2
highest = lax.Precision.HIGHEST
f32 = jnp.float32
bf16 = jnp.bfloat16


def parity():
    return lax.rem(lax.axis_index("col") + lax.axis_index("tile") + 1, 2)


def pack_kernel(vec_ref, pos_ref, tiles_ref, count_ref, near_ref, far_ref, tiles, count, pos, sems):
    rows, width = vec_ref.shape
    half = width // 2
    near = pl.ds(pl.multiple_of((1 - parity()) * half, TILE_B), half)
    far = pl.ds(pl.multiple_of(parity() * half, TILE_B), half)
    copies = [
        pltpu.make_async_copy(tiles_ref, tiles, sems.at[0]),
        pltpu.make_async_copy(count_ref, count, sems.at[1]),
        pltpu.make_async_copy(pos_ref, pos, sems.at[2]),
        pltpu.make_async_copy(vec_ref.at[:, near], near_ref.at[0:rows], sems.at[3]),
        pltpu.make_async_copy(vec_ref.at[:, far], far_ref, sems.at[4]),
    ]
    for copy in copies:
        copy.start()
    first_tile = lax.axis_index("tile") * (width // TILE_B)
    tile_of = lax.broadcasted_iota(jnp.int32, (8, width), 1) // TILE_B
    reach_of = lax.broadcasted_iota(jnp.int32, (8, width), 0) - 4
    live = jnp.zeros((8, width), f32)
    copies[0].wait()
    copies[1].wait()
    for c in range(tiles.shape[2]):
        for s in range(tiles.shape[3]):
            row = tiles[0, 0, c, s]
            reach = tiles[1, 0, c, s] - first_tile - row
            row = jnp.where(s < count[0, c], row, -1)
            live += jnp.where((tile_of == row) & (reach_of == reach), cutoff_sq, 0.0)
    copies[2].wait()
    for n in range(2):
        place = slice(rows + 8 * n, rows + 8 * n + 8)
        part = slice(n * half, (n + 1) * half)
        near_ref[place, :] = live[:, part]
        near_ref[rows + 8 * n : rows + 8 * n + 3, :] = pos[:, part]
    copies[3].wait()
    copies[4].wait()


def joined_places(near):
    rows = near.shape[0] - 16
    return jnp.concatenate([near[rows : rows + 8, :], near[rows + 8 :, :]], axis=1)


def split(x):
    high = x.astype(bf16)
    return high, (x - high.astype(f32)).astype(bf16)


def received_places(block):
    t = lax.axis_index("tile")
    missing = jnp.where(parity() == 0, t == 0, t == lax.axis_size("tile") - 1)
    row_of = lax.broadcasted_iota(jnp.int32, block.shape, 0)
    return jnp.where((row_of > 3) & missing, 0.0, block)


def spread_places(places):
    high, middle = split(places)
    low = (places - high.astype(f32) - middle.astype(f32)).astype(bf16)
    parts = jnp.concatenate([x.astype(f32) for x in (high, middle, low)], axis=0).astype(bf16)
    part_of = lax.broadcasted_iota(jnp.int32, (parts.shape[0], 3 * TILE_B), 0) % 8
    lane_of = lax.broadcasted_iota(jnp.int32, (parts.shape[0], 3 * TILE_B), 1) // TILE_B
    pick = jnp.where(part_of == lane_of, 1.0, 0.0).astype(bf16)
    return lax.dot_general(parts, pick, (((0,), (0,)), ((), ())), preferred_element_type=f32)


def tile_slice(w):
    return slice(w * TILE_B, (w + 1) * TILE_B)


def fill_pull(across, bound, wide, wide_base, pull, row, m):
    for q in range(0, TILE_B, CHUNK):
        down = slice(wide_base + q, wide_base + q + CHUNK)
        offset = [wide[down, tile_slice(c)] - across[c : c + 1, :] for c in range(3)]
        dist_sq = offset[0] * offset[0] + offset[1] * offset[1] + offset[2] * offset[2]
        falloff = jnp.maximum(bound - dist_sq, 0.0)
        weight = falloff * falloff / jnp.maximum(dist_sq, 1.0)
        place = slice(m * TILE_B + q, m * TILE_B + q + CHUNK)
        for c in range(3):
            pull[row, place, tile_slice(c)] = (weight * offset[c]).astype(bf16)


def by_parity(body):
    odd = parity()
    pl.when(odd == 0)(functools.partial(body, 0))
    pl.when(odd == 1)(functools.partial(body, 1))


class Tiles:
    def __init__(self, place):
        self.place = place

    def __call__(self, which, near):
        parts = []
        for w in near:
            refs, tile = self.place(w)
            parts.append(refs[which][:, tile_slice(refs.get("pos_tile", tile) if which == "pos" else tile)])
        return parts[0] if len(parts) == 1 else jnp.concatenate(parts, axis=1)

    def bound(self, w, j):
        reach = abs(w - j)
        return self("pos", [min(w, j)])[4 + reach : 5 + reach]


def sum_pulls(tiles, w, near, pull):
    middle = jnp.mean(tiles("pos", [w]), axis=1, keepdims=True)
    place = tiles("pos", near) - middle
    vec = tiles("vec", near)
    cols = vec.shape[0] // 3
    row_of = lax.broadcasted_iota(jnp.int32, place.shape, 0)
    extra = jnp.where(row_of < 3, place, jnp.where(row_of == 3, 1.0, 0.0))
    along = sum(place[d : d + 1] * vec[d * cols : (d + 1) * cols] for d in range(3))
    more_high, more_low = split(jnp.concatenate([along, extra, jnp.zeros_like(extra)], axis=0))
    left = jnp.concatenate([tiles("high", near), more_high, tiles("low", near), more_low], axis=0)
    n = left.shape[0] // 2
    first = near[0] - w + REACH
    part = slice(first * TILE_B, (first + len(near)) * TILE_B)
    total = jnp.dot(left, pull[part, :], preferred_element_type=f32)
    return total[0:n] + total[n:]


def from_sums(tiles, w, total):
    vec, pos = tiles("vec", [w]), tiles("pos", [w])
    rows = vec.shape[0]
    cols = rows // 3
    mine = pos - jnp.mean(pos, axis=1, keepdims=True)
    out = []
    for c in range(3):
        part = total[:, tile_slice(c)]
        e = rows + cols
        term = -part[rows:e]
        for d in range(3):
            diag = part[e + d : e + d + 1] - mine[d : d + 1] * part[e + 3 : e + 4]
            term += diag * vec[d * cols : (d + 1) * cols] + mine[d : d + 1] * part[d * cols : (d + 1) * cols]
        out.append(term * (spring_scale * step_size / cutoff_sq**2))
    return jnp.concatenate(out, axis=0)


def own_kernel(vec_ref, sent_ref, own_ref, pull, wide, high, low, part_ref, sem):
    rows, width = high.shape
    copy = pltpu.make_async_copy(vec_ref, own_ref.at[0:rows], sem)
    copy.start()
    own_ref[rows : rows + 8, :] = joined_places(sent_ref)
    tiles = width // TILE_B
    half = tiles // 2
    own = dict(vec=own_ref.at[0:rows], pos=own_ref.at[rows : rows + 8], high=high, low=low)
    mine = Tiles(lambda u: (own, u))
    wide[...] = spread_places(own["pos"][...])
    near = [range(max(0, u - REACH), min(tiles, u + REACH + 1)) for u in range(tiles)]
    for u in range(tiles):
        for j in near[u]:
            fill_pull(mine("pos", [u]), mine.bound(u, j), wide, j * TILE_B, pull, u + REACH, j - u + REACH)
    copy.wait()
    high[...], low[...] = split(own["vec"][...])

    def body(odd):
        for k in range(half):
            u = odd * half + k
            part_ref[k] = sum_pulls(mine, u, near[u], pull.at[u + REACH])

    by_parity(body)


def outer_kernel(own_ref, got_ref, wide_own, pull_in, pull, places, wide_got):
    width = wide_own.shape[0]
    rows = own_ref.shape[0] - 8
    tiles = width // TILE_B
    places[...] = received_places(joined_places(got_ref))
    wide_got[...] = spread_places(places[...])
    own = dict(pos=own_ref.at[rows : rows + 8], wide=wide_own)
    got = dict(pos=places, wide=wide_got)

    def body(odd):
        window = Tiles(lambda w: (got if w // tiles == odd else own, w % tiles))
        for r in range(tiles):
            w = r + REACH
            for j in range(w - REACH, w + REACH + 1):
                if w // tiles == odd or j // tiles == odd:
                    refs, tile = window.place(j)
                    across, bound = window("pos", [w]), window.bound(w, j)
                    fill_pull(across, bound, refs["wide"], tile * TILE_B, pull, r + odd * tiles, j - w + REACH)

    by_parity(body)


def halo_tiles(own, near, far, odd):
    rows, width = own["vec"].shape
    tiles = width // TILE_B
    half = tiles // 2

    def place(w):
        tile = w % tiles
        if w // tiles != odd:
            return own, tile
        return dict(far if tile // half == odd else near, pos_tile=tile), tile % half

    return Tiles(place)


def is_far(w, tiles, odd):
    return w // tiles == odd and w % tiles // (tiles // 2) == odd


def inner_kernel(own_ref, near_ref, places, high_own, low_own, part_ref, pull, out_ref, outer_ref, high, low):
    rows, width = high_own.shape
    tiles = width // TILE_B
    half = tiles // 2
    edge = half * TILE_B
    out_ref[rows : rows + 8, :] = places[:, 0:edge]
    out_ref[rows + 8 :, :] = places[:, edge:]
    high[...], low[...] = split(near_ref[0:rows, :])
    own = dict(vec=own_ref.at[0:rows], pos=own_ref.at[rows : rows + 8], high=high_own, low=low_own)
    got = dict(vec=near_ref.at[0:rows], pos=places, high=high, low=low)

    def body(odd):
        window = halo_tiles(own, got, None, odd)
        for r in range(tiles):
            w = r + REACH
            near = [j for j in range(w - REACH, w + REACH + 1) if not is_far(j, tiles, odd)]
            if w // tiles == odd:
                outer_ref[r % half] = sum_pulls(window, w, near, pull.at[r + odd * tiles])
            else:
                near = [j for j in near if j // tiles == odd]
                total = part_ref[r % half] + sum_pulls(window, w, near, pull.at[r + odd * tiles])
                out_ref[0:rows, tile_slice(r % half)] = from_sums(window, w, total)

    by_parity(body)


def outer_rows_kernel(own_ref, near_ref, far_ref, places, outer_ref, pull, out_ref, high, low):
    rows, width = own_ref.shape[0] - 8, own_ref.shape[1]
    tiles = width // TILE_B
    half = tiles // 2
    high[...], low[...] = split(far_ref[...])
    own = dict(vec=own_ref.at[0:rows])
    near_refs = dict(vec=near_ref.at[0:rows], pos=places)
    far_refs = dict(vec=far_ref, pos=places, high=high, low=low)

    def body(odd):
        window = halo_tiles(own, near_refs, far_refs, odd)
        for r in range(odd * half, (1 + odd) * half):
            w = r + REACH
            far = [j for j in range(w - REACH, w + REACH + 1) if is_far(j, tiles, odd)]
            total = outer_ref[r % half] + sum_pulls(window, w, far, pull.at[r + odd * tiles])
            out_ref[:, tile_slice(r % half)] = from_sums(window, w, total)

    by_parity(body)


def beside_tiles(own_pos, places, vectors, side):
    tiles = own_pos.shape[1] // TILE_B
    beside = dict(vectors, pos=places[1 - side])

    def place(w):
        if REACH <= w < tiles + REACH:
            return dict(pos=own_pos), w - REACH
        return beside, w if side == 0 else w - tiles - REACH

    return Tiles(place)


def beside_rows(tiles, side):
    half = tiles // 2
    there = range(REACH) if side == 0 else range(tiles + REACH, tiles + 2 * REACH)
    for u in range(side * half, (1 + side) * half):
        yield u, [j for j in there if abs(j - u - REACH) <= REACH]


def places_of(ref):
    rows = ref.shape[0] - 16
    return ref.at[rows : rows + 8], ref.at[rows + 8 :]


def own_sums_kernel(own_ref, prod_ref, outer_ref, pull, part_ref, edge_ref, high, low, high_outer, low_outer):
    rows, width = own_ref.shape[0] - 8, own_ref.shape[1]
    tiles = width // TILE_B
    half = tiles // 2
    own_pos = own_ref.at[rows : rows + 8]
    high[...], low[...] = split(prod_ref[0:rows, :])
    high_outer[...], low_outer[...] = split(outer_ref[...])

    def body(odd):
        inner = dict(vec=prod_ref.at[0:rows], high=high, low=low)
        inner_sums(own_pos, inner, odd, pull, part_ref)
        ours = dict(vec=outer_ref, high=high_outer, low=low_outer)
        window = beside_tiles(own_pos, places_of(prod_ref), ours, odd)
        for u, near in beside_rows(tiles, odd):
            edge_ref[u % half] = sum_pulls(window, u + REACH, near, pull.at[u + REACH])

    by_parity(body)


def inner_sums(own_pos, inner, side, pull, part_ref):
    tiles = own_pos.shape[1] // TILE_B
    half = tiles // 2
    window = Tiles(lambda u: (dict(inner, pos=own_pos, pos_tile=u), u % half))
    for u in range(tiles):
        near = [j for j in range(side * half, (1 + side) * half) if abs(j - u) <= REACH]
        part_ref[u] = sum_pulls(window, u, near, pull.at[u + REACH])


def middle_kernel(own_ref, prod_ref, got_ref, ours_ref, edge_ref, pull_in, mid_ref, part_ref, pull, high, low, wide):
    rows, width = mid_ref.shape
    tiles = width // TILE_B
    half = tiles // 2
    edge = width // 2
    own_pos = own_ref.at[rows : rows + 8]
    high[...], low[...] = split(got_ref[0:rows, :])

    def body(odd):
        side = 1 - odd
        mid_ref[:, odd * edge : (1 + odd) * edge] = prod_ref[0:rows, :]
        mid_ref[:, side * edge : (1 + side) * edge] = got_ref[0:rows, :]
        window = beside_tiles(own_pos, places_of(got_ref), {}, side)
        first = side * (tiles + REACH)
        wide[...] = spread_places(window("pos", range(first, first + REACH)))
        for u, near in beside_rows(tiles, side):
            w = u + REACH
            for j in near:
                fill_pull(window("pos", [w]), window.bound(w, j), wide, (j - first) * TILE_B, pull, w, j - w + REACH)
        inner = dict(vec=got_ref.at[0:rows], high=high, low=low)
        inner_sums(own_pos, inner, side, pull, part_ref)
        for u in range(tiles):
            total = ours_ref[u] + part_ref[u]
            part_ref[u] = total + edge_ref[u % half] if u // half == odd else total

    by_parity(body)


def second_kernel(own_ref, mid_ref, got_ref, outer_ref, pull, sums_in, out_ref, gram_ref, sums, high, low):
    rows, width = mid_ref.shape
    cols = rows // 3
    tiles = width // TILE_B
    own_pos = own_ref.at[rows : rows + 8]
    high[...], low[...] = split(outer_ref[...])

    def body(odd):
        theirs = dict(vec=outer_ref, high=high, low=low)
        window = beside_tiles(own_pos, places_of(got_ref), theirs, 1 - odd)
        for u, near in beside_rows(tiles, 1 - odd):
            sums[u] = sums[u] + sum_pulls(window, u + REACH, near, pull.at[u + REACH])

    by_parity(body)
    own = dict(vec=mid_ref, pos=own_pos)
    mine = Tiles(lambda u: (own, u))
    for u in range(tiles):
        out_ref[:, tile_slice(u)] = from_sums(mine, u, sums[u])
    bands = [slice(d * cols, (d + 1) * cols) for d in range(3)]
    joint = jnp.concatenate(
        [jnp.concatenate([own_ref[band, :], mid_ref[band, :], out_ref[band, :]], axis=0) for band in bands], axis=1
    )
    joint = jnp.concatenate(split(joint), axis=0)
    gram = lax.dot_general(joint, joint, (((1,), (1,)), ((), ())), preferred_element_type=f32)
    gram = gram[0:rows, 0:rows] + (gram[0:rows, rows:] + gram[rows:, 0:rows] + gram[rows:, rows:])
    gram_ref[...] = jnp.zeros(gram_ref.shape, f32)
    gram_ref[:, 0:rows] = gram[0:cols]
    gram_ref[:, rows : 2 * rows] = gram[cols : 2 * cols]
    gram_ref[:, 2 * rows : 2 * rows + cols] = gram[2 * cols :, 2 * cols :]


def eliminate(joint, n):
    row_of = lax.broadcasted_iota(jnp.int32, joint.shape, 0)
    col = [jnp.broadcast_to(joint[:, j : j + 1], joint.shape) for j in range(n)]
    for k in range(n):
        inverse = 1.0 / col[k][k : k + 1]
        here = row_of == k
        factor = jnp.where(here, -1.0, col[k])
        joint = jnp.where(here, 0.0, joint) - factor * (joint[k : k + 1] * inverse)
        for j in range(k + 1, n):
            col[j] = jnp.where(here, 0.0, col[j]) - factor * (col[j][k : k + 1] * inverse)
    return joint


def mul(a, b):
    return jnp.dot(a, b, precision=highest, preferred_element_type=f32)


def turned(high, both, vec_high, vec_low):
    n = high.shape[1]
    first = lax.dot_general(both, vec_high, (((0,), (0,)), ((), ())), preferred_element_type=f32)
    return first[0:n] + (first[n:] + lax.dot_general(high, vec_low, (((0,), (0,)), ((), ())), preferred_element_type=f32))


def last_kernel(
    bead_scale,
    own_ref,
    prod_ref,
    quad_ref,
    gram_ref,
    out_ref,
    ray_ref,
    corr_ref,
    norm_ref,
    out,
    ray,
    small,
    norm,
    sems,
):
    rows, width = prod_ref.shape
    cols = rows // 3
    row_of = lax.broadcasted_iota(jnp.int32, (cols, cols), 0)
    col_of = lax.broadcasted_iota(jnp.int32, (cols, cols), 1)
    eye = jnp.where(row_of == col_of, 1.0, 0.0).astype(f32)
    xx, xp = gram_ref[:, 0:cols], gram_ref[:, cols : 2 * cols]
    pp, pq = gram_ref[:, rows + cols : rows + 2 * cols], gram_ref[:, rows + 2 * cols : 2 * rows]
    qq = gram_ref[:, 2 * rows : 2 * rows + cols]
    joint = eliminate(jnp.concatenate([gram_ref[:, 0:rows], gram_ref[:, rows : 2 * rows]], axis=0), cols)
    shift = joint[0:cols, cols : 2 * cols]
    rest = joint[cols:, cols : 2 * cols]
    cross = joint[cols:, 2 * cols :]
    corr = xx + rest
    side = xp - 2.0 * rest + cross
    gram = side - mul(rest, shift)
    turn = eye + shift
    squares = turn * (mul(pp, turn) - 2.0 * pq) + eye * qq
    ray[...] = gram * (bead_scale / step_size)
    small[...] = corr * bead_scale
    copies = [
        pltpu.make_async_copy(ray, ray_ref, sems.at[0]),
        pltpu.make_async_copy(small, corr_ref, sems.at[1]),
        pltpu.make_async_copy(norm, norm_ref, sems.at[2]),
    ]
    shift_high, shift_low = split(shift)
    shift_both = jnp.concatenate([shift_high, shift_low], axis=1)
    bands = [slice(d * cols, (d + 1) * cols) for d in range(3)]
    right = []
    for band in bands:
        vec, prod = own_ref[band, :], prod_ref[band, :]
        moved = turned(shift_high, shift_both, *split(vec))
        out[band, :] = vec - 2.0 * prod + quad_ref[band, :]
        right.append(split(jnp.concatenate([vec - prod, moved], axis=0)))
    both = eliminate(jnp.concatenate([corr, side + xp], axis=1), cols)[:, cols:]
    second = both - shift
    norm[...] = jnp.sum(squares - gram * second, axis=0, keepdims=True) * (bead_scale / step_size**2)
    factor_high, factor_low = split(jnp.concatenate([both, second], axis=0))
    factor_both = jnp.concatenate([factor_high, factor_low], axis=1)
    for d, band in enumerate(bands):
        out[band, :] += turned(factor_high, factor_both, *right[d])
        copies.append(pltpu.make_async_copy(out.at[band], out_ref.at[band], sems.at[3 + d]))
        if d == 0:
            for copy in copies:
                copy.start()
        else:
            copies[-1].start()
    for copy in copies:
        copy.wait()


def per_device(positions, trial_block, pair_tiles, pair_count):
    comps, cols, width = trial_block.shape
    rows = comps * cols
    n_tile, n_col = lax.axis_size("tile"), lax.axis_size("col")
    tiles = width // TILE_B
    assert tiles == 2 * REACH and n_col % 2 == 0
    bead_scale = 1.0 / (3.0 * n_tile * width)
    vmem = pl.BlockSpec(memory_space=pltpu.VMEM)
    smem = pl.BlockSpec(memory_space=pltpu.SMEM)
    params = pltpu.CompilerParams(vmem_limit_bytes=24 * 2**20)

    def swapped(x):
        return lax.ppermute(x, "col", [(c, c ^ 1) for c in range(n_col)])

    def f32_array(*shape):
        return jax.ShapeDtypeStruct(shape, f32)

    def bf16_array(*shape):
        return jax.ShapeDtypeStruct(shape, bf16)

    hbm = pl.BlockSpec(memory_space=pltpu.HBM)
    vectors, *tables = [
        pltpu.with_memory_space_constraint(x, pltpu.HBM)
        for x in (trial_block.reshape(rows, width), positions, pair_tiles, pair_count)
    ]
    near, far = pl.pallas_call(
        pack_kernel,
        out_shape=(f32_array(rows + 16, width // 2), f32_array(rows, width // 2)),
        in_specs=[hbm] * 4,
        out_specs=(vmem,) * 2,
        scratch_shapes=[
            pltpu.SMEM(pair_tiles.shape, jnp.int32),
            pltpu.SMEM(pair_count.shape, jnp.int32),
            pltpu.VMEM(positions.shape, f32),
            pltpu.SemaphoreType.DMA((5,)),
        ],
        compiler_params=pltpu.CompilerParams(vmem_limit_bytes=4 * 2**20),
        name="pack",
    )(vectors, *tables)

    halo = []
    for t in range(n_tile):
        for c in range(n_col):
            source = t - 1 if (c + t + 1) % 2 == 0 else t + 1
            if not 0 <= source < n_tile:
                source = t
            halo.append((source * n_col + (c ^ 1), t * n_col + c))
    got_near = lax.ppermute(near, ("tile", "col"), halo)
    got_far = lax.ppermute(far, ("tile", "col"), halo)

    parts = [pltpu.VMEM((rows, width), bf16)] * 2
    sums = (rows + cols + 16, 3 * TILE_B)
    pulls = bf16_array(2 * tiles, (2 * REACH + 1) * TILE_B, 3 * TILE_B)
    hidden = pl.CostEstimate(flops=10**8, bytes_accessed=10**6, transcendentals=0)
    own, pull, wide, high, low, part = pl.pallas_call(
        own_kernel,
        out_shape=(
            f32_array(rows + 8, width),
            pulls,
            f32_array(width, 3 * TILE_B),
            bf16_array(rows, width),
            bf16_array(rows, width),
            f32_array(tiles // 2, *sums),
        ),
        in_specs=[hbm, vmem],
        out_specs=(vmem,) * 6,
        scratch_shapes=[pltpu.SemaphoreType.DMA(())],
        compiler_params=params,
        cost_estimate=hidden,
        name="own_pulls",
    )(vectors, near)
    pull, places = pl.pallas_call(
        outer_kernel,
        out_shape=(pulls, f32_array(8, width)),
        in_specs=[vmem] * 4,
        out_specs=(vmem,) * 2,
        input_output_aliases={3: 0},
        scratch_shapes=[pltpu.VMEM((width, 3 * TILE_B), f32)],
        compiler_params=params,
        cost_estimate=hidden,
        name="outer_pulls",
    )(own, got_near, wide, pull)
    half_parts = [pltpu.VMEM((rows, width // 2), bf16)] * 2
    prod, outer = pl.pallas_call(
        inner_kernel,
        out_shape=(f32_array(rows + 16, width // 2), f32_array(tiles // 2, *sums)),
        in_specs=[vmem] * 7,
        out_specs=(vmem,) * 2,
        scratch_shapes=half_parts,
        compiler_params=params,
        cost_estimate=hidden,
        name="inner",
    )(own, got_near, places, high, low, part, pull)
    prod_got = swapped(prod)
    outer = pl.pallas_call(
        outer_rows_kernel,
        out_shape=f32_array(rows, width // 2),
        in_specs=[vmem] * 6,
        out_specs=vmem,
        scratch_shapes=half_parts,
        compiler_params=params,
        name="outer_rows",
    )(own, got_near, got_far, places, outer, pull)
    outer_got = swapped(outer)
    part, edge = pl.pallas_call(
        own_sums_kernel,
        out_shape=(f32_array(tiles, *sums), f32_array(tiles // 2, *sums)),
        in_specs=[vmem] * 4,
        out_specs=(vmem,) * 2,
        scratch_shapes=half_parts * 2,
        compiler_params=params,
        cost_estimate=hidden,
        name="own_sums",
    )(own, prod, outer, pull)
    mid, part, pull = pl.pallas_call(
        middle_kernel,
        out_shape=(f32_array(rows, width), f32_array(tiles, *sums), pulls),
        in_specs=[vmem] * 6,
        out_specs=(vmem,) * 3,
        input_output_aliases={5: 2},
        scratch_shapes=half_parts + [pltpu.VMEM((REACH * TILE_B, 3 * TILE_B), f32)],
        compiler_params=params,
        cost_estimate=hidden,
        name="middle",
    )(own, prod, prod_got, part, edge, pull)
    quad, gram, _ = pl.pallas_call(
        second_kernel,
        out_shape=(f32_array(rows, width), f32_array(cols, 128), f32_array(tiles, *sums)),
        in_specs=[vmem] * 6,
        out_specs=(vmem,) * 3,
        input_output_aliases={5: 2},
        scratch_shapes=half_parts,
        compiler_params=params,
        name="second",
    )(own, mid, prod_got, outer_got, pull, part)

    def crossed(x, step):
        route = [
            (t * n_col + c, (t ^ step) * n_col + (c ^ 1)) for t in range(n_tile) for c in range(n_col)
        ]
        return lax.ppermute(x, ("tile", "col"), route)

    step = 1
    while step < n_tile:
        if 2 * step < n_tile:
            near, far, both = [crossed(gram, s) for s in (step, 2 * step, 3 * step)]
            gram = (gram + near) + (far + both)
        else:
            gram = gram + crossed(gram, step)
        step *= 4
    shapes = [(rows, width), (cols, cols), (cols, cols), (1, cols)]
    block, ray, corr, norms = pl.pallas_call(
        functools.partial(last_kernel, bead_scale),
        out_shape=tuple(jax.ShapeDtypeStruct(shape, f32) for shape in shapes),
        in_specs=[vmem] * 4,
        out_specs=(hbm,) * 4,
        scratch_shapes=[pltpu.VMEM(shape, f32) for shape in shapes] + [pltpu.SemaphoreType.DMA((6,))],
        compiler_params=params,
        name="last",
    )(own, mid, quad, gram)
    return block.reshape(comps, cols, width), ray, corr, norms.reshape(cols)


def solution(mesh):
    return jax.shard_map(
        per_device,
        mesh=mesh,
        in_specs=(
            P(None, "tile"),
            P(None, None, "tile"),
            P(None, "tile", None, None),
            P("tile", None),
        ),
        out_specs=(P(None, None, "tile"), P(), P(), P()),
        check_vma=False,
    )
```

```python
import functools

import jax
import jax.numpy as jnp
from jax import lax
from jax.experimental import pallas as pl
from jax.experimental.pallas import tpu as pltpu
from jax.sharding import PartitionSpec as P

TILE_B = 128
REACH = 2
CHUNK = 32

spring_scale = 1.0 / 64.0
cutoff_sq = 225.0
step_size = 0.2
highest = lax.Precision.HIGHEST
f32 = jnp.float32
bf16 = jnp.bfloat16


def parity():
    return lax.rem(lax.axis_index("col") + lax.axis_index("tile") + 1, 2)


def pack_kernel(vec_ref, pos_ref, tiles_ref, count_ref, near_ref, far_ref, tiles, count, pos, sems):
    rows, width = vec_ref.shape
    half = width // 2
    near = pl.ds(pl.multiple_of((1 - parity()) * half, TILE_B), half)
    far = pl.ds(pl.multiple_of(parity() * half, TILE_B), half)
    copies = [
        pltpu.make_async_copy(tiles_ref, tiles, sems.at[0]),
        pltpu.make_async_copy(count_ref, count, sems.at[1]),
        pltpu.make_async_copy(pos_ref, pos, sems.at[2]),
        pltpu.make_async_copy(vec_ref.at[:, near], near_ref.at[0:rows], sems.at[3]),
        pltpu.make_async_copy(vec_ref.at[:, far], far_ref, sems.at[4]),
    ]
    for copy in copies:
        copy.start()
    first_tile = lax.axis_index("tile") * (width // TILE_B)
    tile_of = lax.broadcasted_iota(jnp.int32, (8, width), 1) // TILE_B
    reach_of = lax.broadcasted_iota(jnp.int32, (8, width), 0) - 4
    live = jnp.zeros((8, width), f32)
    copies[0].wait()
    copies[1].wait()
    for c in range(tiles.shape[2]):
        for s in range(tiles.shape[3]):
            row = tiles[0, 0, c, s]
            reach = tiles[1, 0, c, s] - first_tile - row
            row = jnp.where(s < count[0, c], row, -1)
            live += jnp.where((tile_of == row) & (reach_of == reach), cutoff_sq, 0.0)
    copies[2].wait()
    for n in range(2):
        place = slice(rows + 8 * n, rows + 8 * n + 8)
        part = slice(n * half, (n + 1) * half)
        near_ref[place, :] = live[:, part]
        near_ref[rows + 8 * n : rows + 8 * n + 3, :] = pos[:, part]
    copies[3].wait()
    copies[4].wait()


def joined_places(near):
    rows = near.shape[0] - 16
    return jnp.concatenate([near[rows : rows + 8, :], near[rows + 8 :, :]], axis=1)


def split(x):
    high = x.astype(bf16)
    return high, (x - high.astype(f32)).astype(bf16)


def received_places(block):
    t = lax.axis_index("tile")
    missing = jnp.where(parity() == 0, t == 0, t == lax.axis_size("tile") - 1)
    row_of = lax.broadcasted_iota(jnp.int32, block.shape, 0)
    return jnp.where((row_of > 3) & missing, 0.0, block)


def spread_places(places):
    high, middle = split(places)
    low = (places - high.astype(f32) - middle.astype(f32)).astype(bf16)
    parts = jnp.concatenate([x.astype(f32) for x in (high, middle, low)], axis=0).astype(bf16)
    part_of = lax.broadcasted_iota(jnp.int32, (parts.shape[0], 3 * TILE_B), 0) % 8
    lane_of = lax.broadcasted_iota(jnp.int32, (parts.shape[0], 3 * TILE_B), 1) // TILE_B
    pick = jnp.where(part_of == lane_of, 1.0, 0.0).astype(bf16)
    return lax.dot_general(parts, pick, (((0,), (0,)), ((), ())), preferred_element_type=f32)


def tile_slice(w):
    return slice(w * TILE_B, (w + 1) * TILE_B)


def fill_pull(across, bound, wide, wide_base, pull, row, m):
    for q in range(0, TILE_B, CHUNK):
        down = slice(wide_base + q, wide_base + q + CHUNK)
        offset = [wide[down, tile_slice(c)] - across[c : c + 1, :] for c in range(3)]
        dist_sq = offset[0] * offset[0] + offset[1] * offset[1] + offset[2] * offset[2]
        falloff = jnp.maximum(bound - dist_sq, 0.0)
        weight = falloff * falloff / jnp.maximum(dist_sq, 1.0)
        place = slice(m * TILE_B + q, m * TILE_B + q + CHUNK)
        for c in range(3):
            pull[row, place, tile_slice(c)] = (weight * offset[c]).astype(bf16)


def by_parity(body):
    odd = parity()
    pl.when(odd == 0)(functools.partial(body, 0))
    pl.when(odd == 1)(functools.partial(body, 1))


class Tiles:
    def __init__(self, place):
        self.place = place

    def __call__(self, which, near):
        parts = []
        for w in near:
            refs, tile = self.place(w)
            parts.append(refs[which][:, tile_slice(refs.get("pos_tile", tile) if which == "pos" else tile)])
        return parts[0] if len(parts) == 1 else jnp.concatenate(parts, axis=1)

    def bound(self, w, j):
        reach = abs(w - j)
        return self("pos", [min(w, j)])[4 + reach : 5 + reach]


def sum_pulls(tiles, w, near, pull):
    middle = jnp.mean(tiles("pos", [w]), axis=1, keepdims=True)
    place = tiles("pos", near) - middle
    vec = tiles("vec", near)
    cols = vec.shape[0] // 3
    row_of = lax.broadcasted_iota(jnp.int32, place.shape, 0)
    extra = jnp.where(row_of < 3, place, jnp.where(row_of == 3, 1.0, 0.0))
    along = sum(place[d : d + 1] * vec[d * cols : (d + 1) * cols] for d in range(3))
    more_high, more_low = split(jnp.concatenate([along, extra, jnp.zeros_like(extra)], axis=0))
    left = jnp.concatenate([tiles("high", near), more_high, tiles("low", near), more_low], axis=0)
    n = left.shape[0] // 2
    first = near[0] - w + REACH
    part = slice(first * TILE_B, (first + len(near)) * TILE_B)
    total = jnp.dot(left, pull[part, :], preferred_element_type=f32)
    return total[0:n] + total[n:]


def from_sums(tiles, w, total):
    vec, pos = tiles("vec", [w]), tiles("pos", [w])
    rows = vec.shape[0]
    cols = rows // 3
    mine = pos - jnp.mean(pos, axis=1, keepdims=True)
    out = []
    for c in range(3):
        part = total[:, tile_slice(c)]
        e = rows + cols
        term = -part[rows:e]
        for d in range(3):
            diag = part[e + d : e + d + 1] - mine[d : d + 1] * part[e + 3 : e + 4]
            term += diag * vec[d * cols : (d + 1) * cols] + mine[d : d + 1] * part[d * cols : (d + 1) * cols]
        out.append(term * (spring_scale * step_size / cutoff_sq**2))
    return jnp.concatenate(out, axis=0)


def own_kernel(vec_ref, sent_ref, own_ref, pull, wide, high, low, part_ref, sem):
    rows, width = high.shape
    copy = pltpu.make_async_copy(vec_ref, own_ref.at[0:rows], sem)
    copy.start()
    own_ref[rows : rows + 8, :] = joined_places(sent_ref)
    tiles = width // TILE_B
    half = tiles // 2
    own = dict(vec=own_ref.at[0:rows], pos=own_ref.at[rows : rows + 8], high=high, low=low)
    mine = Tiles(lambda u: (own, u))
    wide[...] = spread_places(own["pos"][...])
    near = [range(max(0, u - REACH), min(tiles, u + REACH + 1)) for u in range(tiles)]
    for u in range(tiles):
        for j in near[u]:
            fill_pull(mine("pos", [u]), mine.bound(u, j), wide, j * TILE_B, pull, u + REACH, j - u + REACH)
    copy.wait()
    high[...], low[...] = split(own["vec"][...])

    def body(odd):
        for k in range(half):
            u = odd * half + k
            part_ref[k] = sum_pulls(mine, u, near[u], pull.at[u + REACH])

    by_parity(body)


def outer_kernel(own_ref, got_ref, wide_own, pull_in, pull, places, wide_got):
    width = wide_own.shape[0]
    rows = own_ref.shape[0] - 8
    tiles = width // TILE_B
    places[...] = received_places(joined_places(got_ref))
    wide_got[...] = spread_places(places[...])
    own = dict(pos=own_ref.at[rows : rows + 8], wide=wide_own)
    got = dict(pos=places, wide=wide_got)

    def body(odd):
        window = Tiles(lambda w: (got if w // tiles == odd else own, w % tiles))
        for r in range(tiles):
            w = r + REACH
            for j in range(w - REACH, w + REACH + 1):
                if w // tiles == odd or j // tiles == odd:
                    refs, tile = window.place(j)
                    across, bound = window("pos", [w]), window.bound(w, j)
                    fill_pull(across, bound, refs["wide"], tile * TILE_B, pull, r + odd * tiles, j - w + REACH)

    by_parity(body)


def halo_tiles(own, near, far, odd):
    rows, width = own["vec"].shape
    tiles = width // TILE_B
    half = tiles // 2

    def place(w):
        tile = w % tiles
        if w // tiles != odd:
            return own, tile
        return dict(far if tile // half == odd else near, pos_tile=tile), tile % half

    return Tiles(place)


def is_far(w, tiles, odd):
    return w // tiles == odd and w % tiles // (tiles // 2) == odd


def inner_kernel(own_ref, near_ref, places, high_own, low_own, part_ref, pull, out_ref, outer_ref, high, low):
    rows, width = high_own.shape
    tiles = width // TILE_B
    half = tiles // 2
    edge = half * TILE_B
    out_ref[rows : rows + 8, :] = places[:, 0:edge]
    out_ref[rows + 8 :, :] = places[:, edge:]
    high[...], low[...] = split(near_ref[0:rows, :])
    own = dict(vec=own_ref.at[0:rows], pos=own_ref.at[rows : rows + 8], high=high_own, low=low_own)
    got = dict(vec=near_ref.at[0:rows], pos=places, high=high, low=low)

    def body(odd):
        window = halo_tiles(own, got, None, odd)
        for r in range(tiles):
            w = r + REACH
            near = [j for j in range(w - REACH, w + REACH + 1) if not is_far(j, tiles, odd)]
            if w // tiles == odd:
                outer_ref[r % half] = sum_pulls(window, w, near, pull.at[r + odd * tiles])
            else:
                near = [j for j in near if j // tiles == odd]
                total = part_ref[r % half] + sum_pulls(window, w, near, pull.at[r + odd * tiles])
                out_ref[0:rows, tile_slice(r % half)] = from_sums(window, w, total)

    by_parity(body)


def outer_rows_kernel(own_ref, near_ref, far_ref, places, outer_ref, pull, out_ref, high, low):
    rows, width = own_ref.shape[0] - 8, own_ref.shape[1]
    tiles = width // TILE_B
    half = tiles // 2
    high[...], low[...] = split(far_ref[...])
    own = dict(vec=own_ref.at[0:rows])
    near_refs = dict(vec=near_ref.at[0:rows], pos=places)
    far_refs = dict(vec=far_ref, pos=places, high=high, low=low)

    def body(odd):
        window = halo_tiles(own, near_refs, far_refs, odd)
        for r in range(odd * half, (1 + odd) * half):
            w = r + REACH
            far = [j for j in range(w - REACH, w + REACH + 1) if is_far(j, tiles, odd)]
            total = outer_ref[r % half] + sum_pulls(window, w, far, pull.at[r + odd * tiles])
            out_ref[:, tile_slice(r % half)] = from_sums(window, w, total)

    by_parity(body)


def beside_tiles(own_pos, places, vectors, side):
    tiles = own_pos.shape[1] // TILE_B
    beside = dict(vectors, pos=places[1 - side])

    def place(w):
        if REACH <= w < tiles + REACH:
            return dict(pos=own_pos), w - REACH
        return beside, w if side == 0 else w - tiles - REACH

    return Tiles(place)


def beside_rows(tiles, side):
    half = tiles // 2
    there = range(REACH) if side == 0 else range(tiles + REACH, tiles + 2 * REACH)
    for u in range(side * half, (1 + side) * half):
        yield u, [j for j in there if abs(j - u - REACH) <= REACH]


def places_of(ref):
    rows = ref.shape[0] - 16
    return ref.at[rows : rows + 8], ref.at[rows + 8 :]


def own_sums_kernel(own_ref, prod_ref, outer_ref, pull, part_ref, edge_ref, high, low, high_outer, low_outer):
    rows, width = own_ref.shape[0] - 8, own_ref.shape[1]
    tiles = width // TILE_B
    half = tiles // 2
    own_pos = own_ref.at[rows : rows + 8]
    high[...], low[...] = split(prod_ref[0:rows, :])
    high_outer[...], low_outer[...] = split(outer_ref[...])

    def body(odd):
        inner = dict(vec=prod_ref.at[0:rows], high=high, low=low)
        for u, total in inner_sums(own_pos, inner, odd, pull):
            part_ref[u] = total
        ours = dict(vec=outer_ref, high=high_outer, low=low_outer)
        window = beside_tiles(own_pos, places_of(prod_ref), ours, odd)
        for u, near in beside_rows(tiles, odd):
            edge_ref[u % half] = sum_pulls(window, u + REACH, near, pull.at[u + REACH])

    by_parity(body)


def inner_sums(own_pos, inner, side, pull):
    tiles = own_pos.shape[1] // TILE_B
    half = tiles // 2
    window = Tiles(lambda u: (dict(inner, pos=own_pos, pos_tile=u), u % half))
    for u in range(tiles):
        near = [j for j in range(side * half, (1 + side) * half) if abs(j - u) <= REACH]
        yield u, sum_pulls(window, u, near, pull.at[u + REACH])


def middle_kernel(own_ref, prod_ref, got_ref, ours_ref, edge_ref, pull_in, mid_ref, part_ref, pull, high, low, wide):
    rows, width = mid_ref.shape
    tiles = width // TILE_B
    half = tiles // 2
    edge = width // 2
    own_pos = own_ref.at[rows : rows + 8]
    high[...], low[...] = split(got_ref[0:rows, :])

    def body(odd):
        side = 1 - odd
        mid_ref[:, odd * edge : (1 + odd) * edge] = prod_ref[0:rows, :]
        mid_ref[:, side * edge : (1 + side) * edge] = got_ref[0:rows, :]
        window = beside_tiles(own_pos, places_of(got_ref), {}, side)
        first = side * (tiles + REACH)
        wide[...] = spread_places(window("pos", range(first, first + REACH)))
        for u, near in beside_rows(tiles, side):
            w = u + REACH
            for j in near:
                fill_pull(window("pos", [w]), window.bound(w, j), wide, (j - first) * TILE_B, pull, w, j - w + REACH)
        inner = dict(vec=got_ref.at[0:rows], high=high, low=low)
        for u, total in inner_sums(own_pos, inner, side, pull):
            total = ours_ref[u] + total
            part_ref[u] = total + edge_ref[u % half] if u // half == odd else total

    by_parity(body)


def second_kernel(own_ref, mid_ref, got_ref, outer_ref, pull, sums_in, out_ref, gram_ref, sums, high, low):
    rows, width = mid_ref.shape
    cols = rows // 3
    tiles = width // TILE_B
    own_pos = own_ref.at[rows : rows + 8]
    high[...], low[...] = split(outer_ref[...])

    def body(odd):
        theirs = dict(vec=outer_ref, high=high, low=low)
        window = beside_tiles(own_pos, places_of(got_ref), theirs, 1 - odd)
        for u, near in beside_rows(tiles, 1 - odd):
            sums[u] = sums[u] + sum_pulls(window, u + REACH, near, pull.at[u + REACH])

    by_parity(body)
    own = dict(vec=mid_ref, pos=own_pos)
    mine = Tiles(lambda u: (own, u))
    for u in range(tiles):
        out_ref[:, tile_slice(u)] = from_sums(mine, u, sums[u])
    bands = [slice(d * cols, (d + 1) * cols) for d in range(3)]
    joint = jnp.concatenate(
        [jnp.concatenate([own_ref[band, :], mid_ref[band, :], out_ref[band, :]], axis=0) for band in bands], axis=1
    )
    parts = split(joint)
    both = jnp.concatenate(parts, axis=0)
    by_high, by_low = [
        lax.dot_general(both, part, (((1,), (1,)), ((), ())), preferred_element_type=f32) for part in parts
    ]
    gram = by_high[0:rows] + (by_high[rows:] + by_low[0:rows] + by_low[rows:])
    gram_ref[...] = jnp.zeros(gram_ref.shape, f32)
    gram_ref[:, 0:rows] = gram[0:cols]
    gram_ref[:, rows : 2 * rows] = gram[cols : 2 * cols]
    gram_ref[:, 2 * rows : 2 * rows + cols] = gram[2 * cols :, 2 * cols :]


def eliminate(joint, n):
    row_of = lax.broadcasted_iota(jnp.int32, joint.shape, 0)
    col = [jnp.broadcast_to(joint[:, j : j + 1], joint.shape) for j in range(n)]
    for k in range(n):
        inverse = 1.0 / col[k][k : k + 1]
        here = row_of == k
        factor = jnp.where(here, -1.0, col[k])
        joint = jnp.where(here, 0.0, joint) - factor * (joint[k : k + 1] * inverse)
        for j in range(k + 1, n):
            col[j] = jnp.where(here, 0.0, col[j]) - factor * (col[j][k : k + 1] * inverse)
    return joint


def mul(a, b):
    return jnp.dot(a, b, precision=highest, preferred_element_type=f32)


def turned(high, both, vec_high, vec_low):
    n = high.shape[1]
    first = lax.dot_general(both, vec_high, (((0,), (0,)), ((), ())), preferred_element_type=f32)
    return first[0:n] + (first[n:] + lax.dot_general(high, vec_low, (((0,), (0,)), ((), ())), preferred_element_type=f32))


def last_kernel(
    bead_scale,
    own_ref,
    prod_ref,
    quad_ref,
    gram_ref,
    out_ref,
    ray_ref,
    corr_ref,
    norm_ref,
    out,
    ray,
    small,
    norm,
    sems,
):
    rows, width = prod_ref.shape
    cols = rows // 3
    row_of = lax.broadcasted_iota(jnp.int32, (cols, cols), 0)
    col_of = lax.broadcasted_iota(jnp.int32, (cols, cols), 1)
    eye = jnp.where(row_of == col_of, 1.0, 0.0).astype(f32)
    xx, xp = gram_ref[:, 0:cols], gram_ref[:, cols : 2 * cols]
    pp, pq = gram_ref[:, rows + cols : rows + 2 * cols], gram_ref[:, rows + 2 * cols : 2 * rows]
    qq = gram_ref[:, 2 * rows : 2 * rows + cols]
    joint = eliminate(jnp.concatenate([gram_ref[:, 0:rows], gram_ref[:, rows : 2 * rows]], axis=0), cols)
    shift = joint[0:cols, cols : 2 * cols]
    rest = joint[cols:, cols : 2 * cols]
    cross = joint[cols:, 2 * cols :]
    corr = xx + rest
    side = xp - 2.0 * rest + cross
    gram = side - mul(rest, shift)
    turn = eye + shift
    squares = turn * (mul(pp, turn) - 2.0 * pq) + eye * qq
    ray[...] = gram * (bead_scale / step_size)
    small[...] = corr * bead_scale
    copies = [
        pltpu.make_async_copy(ray, ray_ref, sems.at[0]),
        pltpu.make_async_copy(small, corr_ref, sems.at[1]),
        pltpu.make_async_copy(norm, norm_ref, sems.at[2]),
    ]
    shift_high, shift_low = split(shift)
    shift_both = jnp.concatenate([shift_high, shift_low], axis=1)
    bands = [slice(d * cols, (d + 1) * cols) for d in range(3)]
    right = []
    for band in bands:
        vec, prod = own_ref[band, :], prod_ref[band, :]
        moved = turned(shift_high, shift_both, *split(vec))
        out[band, :] = vec - 2.0 * prod + quad_ref[band, :]
        right.append(split(jnp.concatenate([vec - prod, moved], axis=0)))
    both = eliminate(jnp.concatenate([corr, side + xp], axis=1), cols)[:, cols:]
    second = both - shift
    norm[...] = jnp.sum(squares - gram * second, axis=0, keepdims=True) * (bead_scale / step_size**2)
    factor_high, factor_low = split(jnp.concatenate([both, second], axis=0))
    factor_both = jnp.concatenate([factor_high, factor_low], axis=1)
    for d, band in enumerate(bands):
        out[band, :] += turned(factor_high, factor_both, *right[d])
        copies.append(pltpu.make_async_copy(out.at[band], out_ref.at[band], sems.at[3 + d]))
        if d == 0:
            for copy in copies:
                copy.start()
        else:
            copies[-1].start()
    for copy in copies:
        copy.wait()


def per_device(positions, trial_block, pair_tiles, pair_count):
    comps, cols, width = trial_block.shape
    rows = comps * cols
    n_tile, n_col = lax.axis_size("tile"), lax.axis_size("col")
    tiles = width // TILE_B
    assert tiles == 2 * REACH and n_col % 2 == 0
    bead_scale = 1.0 / (3.0 * n_tile * width)
    vmem = pl.BlockSpec(memory_space=pltpu.VMEM)
    smem = pl.BlockSpec(memory_space=pltpu.SMEM)
    params = pltpu.CompilerParams(vmem_limit_bytes=24 * 2**20)

    def swapped(x):
        return lax.ppermute(x, "col", [(c, c ^ 1) for c in range(n_col)])

    def f32_array(*shape):
        return jax.ShapeDtypeStruct(shape, f32)

    def bf16_array(*shape):
        return jax.ShapeDtypeStruct(shape, bf16)

    hbm = pl.BlockSpec(memory_space=pltpu.HBM)
    vectors, *tables = [
        pltpu.with_memory_space_constraint(x, pltpu.HBM)
        for x in (trial_block.reshape(rows, width), positions, pair_tiles, pair_count)
    ]
    near, far = pl.pallas_call(
        pack_kernel,
        out_shape=(f32_array(rows + 16, width // 2), f32_array(rows, width // 2)),
        in_specs=[hbm] * 4,
        out_specs=(vmem,) * 2,
        scratch_shapes=[
            pltpu.SMEM(pair_tiles.shape, jnp.int32),
            pltpu.SMEM(pair_count.shape, jnp.int32),
            pltpu.VMEM(positions.shape, f32),
            pltpu.SemaphoreType.DMA((5,)),
        ],
        compiler_params=pltpu.CompilerParams(vmem_limit_bytes=4 * 2**20),
        name="pack",
    )(vectors, *tables)

    halo = []
    for t in range(n_tile):
        for c in range(n_col):
            source = t - 1 if (c + t + 1) % 2 == 0 else t + 1
            if not 0 <= source < n_tile:
                source = t
            halo.append((source * n_col + (c ^ 1), t * n_col + c))
    got_near = lax.ppermute(near, ("tile", "col"), halo)
    got_far = lax.ppermute(far, ("tile", "col"), halo)

    parts = [pltpu.VMEM((rows, width), bf16)] * 2
    sums = (rows + cols + 16, 3 * TILE_B)
    pulls = bf16_array(2 * tiles, (2 * REACH + 1) * TILE_B, 3 * TILE_B)
    hidden = pl.CostEstimate(flops=10**8, bytes_accessed=10**6, transcendentals=0)
    own, pull, wide, high, low, part = pl.pallas_call(
        own_kernel,
        out_shape=(
            f32_array(rows + 8, width),
            pulls,
            f32_array(width, 3 * TILE_B),
            bf16_array(rows, width),
            bf16_array(rows, width),
            f32_array(tiles // 2, *sums),
        ),
        in_specs=[hbm, vmem],
        out_specs=(vmem,) * 6,
        scratch_shapes=[pltpu.SemaphoreType.DMA(())],
        compiler_params=params,
        cost_estimate=hidden,
        name="own_pulls",
    )(vectors, near)
    pull, places = pl.pallas_call(
        outer_kernel,
        out_shape=(pulls, f32_array(8, width)),
        in_specs=[vmem] * 4,
        out_specs=(vmem,) * 2,
        input_output_aliases={3: 0},
        scratch_shapes=[pltpu.VMEM((width, 3 * TILE_B), f32)],
        compiler_params=params,
        cost_estimate=hidden,
        name="outer_pulls",
    )(own, got_near, wide, pull)
    half_parts = [pltpu.VMEM((rows, width // 2), bf16)] * 2
    prod, outer = pl.pallas_call(
        inner_kernel,
        out_shape=(f32_array(rows + 16, width // 2), f32_array(tiles // 2, *sums)),
        in_specs=[vmem] * 7,
        out_specs=(vmem,) * 2,
        scratch_shapes=half_parts,
        compiler_params=params,
        cost_estimate=hidden,
        name="inner",
    )(own, got_near, places, high, low, part, pull)
    prod_got = swapped(prod)
    outer = pl.pallas_call(
        outer_rows_kernel,
        out_shape=f32_array(rows, width // 2),
        in_specs=[vmem] * 6,
        out_specs=vmem,
        scratch_shapes=half_parts,
        compiler_params=params,
        name="outer_rows",
    )(own, got_near, got_far, places, outer, pull)
    outer_got = swapped(outer)
    part, edge = pl.pallas_call(
        own_sums_kernel,
        out_shape=(f32_array(tiles, *sums), f32_array(tiles // 2, *sums)),
        in_specs=[vmem] * 4,
        out_specs=(vmem,) * 2,
        scratch_shapes=half_parts * 2,
        compiler_params=params,
        cost_estimate=hidden,
        name="own_sums",
    )(own, prod, outer, pull)
    mid, part, pull = pl.pallas_call(
        middle_kernel,
        out_shape=(f32_array(rows, width), f32_array(tiles, *sums), pulls),
        in_specs=[vmem] * 6,
        out_specs=(vmem,) * 3,
        input_output_aliases={5: 2},
        scratch_shapes=half_parts + [pltpu.VMEM((REACH * TILE_B, 3 * TILE_B), f32)],
        compiler_params=params,
        cost_estimate=hidden,
        name="middle",
    )(own, prod, prod_got, part, edge, pull)
    quad, gram, _ = pl.pallas_call(
        second_kernel,
        out_shape=(f32_array(rows, width), f32_array(cols, 128), f32_array(tiles, *sums)),
        in_specs=[vmem] * 6,
        out_specs=(vmem,) * 3,
        input_output_aliases={5: 2},
        scratch_shapes=half_parts,
        compiler_params=params,
        name="second",
    )(own, mid, prod_got, outer_got, pull, part)

    def crossed(x, step):
        route = [
            (t * n_col + c, (t ^ step) * n_col + (c ^ 1)) for t in range(n_tile) for c in range(n_col)
        ]
        return lax.ppermute(x, ("tile", "col"), route)

    step = 1
    while step < n_tile:
        if 2 * step < n_tile:
            near, far, both = [crossed(gram, s) for s in (step, 2 * step, 3 * step)]
            gram = (gram + near) + (far + both)
        else:
            gram = gram + crossed(gram, step)
        step *= 4
    shapes = [(rows, width), (cols, cols), (cols, cols), (1, cols)]
    block, ray, corr, norms = pl.pallas_call(
        functools.partial(last_kernel, bead_scale),
        out_shape=tuple(jax.ShapeDtypeStruct(shape, f32) for shape in shapes),
        in_specs=[vmem] * 4,
        out_specs=(hbm,) * 4,
        scratch_shapes=[pltpu.VMEM(shape, f32) for shape in shapes] + [pltpu.SemaphoreType.DMA((6,))],
        compiler_params=params,
        name="last",
    )(own, mid, quad, gram)
    return block.reshape(comps, cols, width), ray, corr, norms.reshape(cols)


def solution(mesh):
    return jax.shard_map(
        per_device,
        mesh=mesh,
        in_specs=(
            P(None, "tile"),
            P(None, None, "tile"),
            P(None, "tile", None, None),
            P("tile", None),
        ),
        out_specs=(P(None, None, "tile"), P(), P(), P()),
        check_vma=False,
    )
```

```python
import functools

import jax
import jax.numpy as jnp
from jax import lax
from jax.experimental import pallas as pl
from jax.experimental.pallas import tpu as pltpu
from jax.sharding import PartitionSpec as P

TILE_B = 128
REACH = 2
CHUNK = 16

spring_scale = 1.0 / 64.0
cutoff_sq = 225.0
step_size = 0.2
highest = lax.Precision.HIGHEST
f32 = jnp.float32
bf16 = jnp.bfloat16


def parity():
    return lax.rem(lax.axis_index("col") + lax.axis_index("tile") + 1, 2)


def pack_kernel(vec_ref, pos_ref, tiles_ref, count_ref, near_ref, far_ref, tiles, count, pos, sems):
    rows, width = vec_ref.shape
    half = width // 2
    near = pl.ds(pl.multiple_of((1 - parity()) * half, TILE_B), half)
    far = pl.ds(pl.multiple_of(parity() * half, TILE_B), half)
    copies = [
        pltpu.make_async_copy(tiles_ref, tiles, sems.at[0]),
        pltpu.make_async_copy(count_ref, count, sems.at[1]),
        pltpu.make_async_copy(pos_ref, pos, sems.at[2]),
        pltpu.make_async_copy(vec_ref.at[:, near], near_ref.at[0:rows], sems.at[3]),
        pltpu.make_async_copy(vec_ref.at[:, far], far_ref, sems.at[4]),
    ]
    for copy in copies:
        copy.start()
    first_tile = lax.axis_index("tile") * (width // TILE_B)
    tile_of = lax.broadcasted_iota(jnp.int32, (8, width), 1) // TILE_B
    reach_of = lax.broadcasted_iota(jnp.int32, (8, width), 0) - 4
    live = jnp.zeros((8, width), f32)
    copies[0].wait()
    copies[1].wait()
    for c in range(tiles.shape[2]):
        for s in range(tiles.shape[3]):
            row = tiles[0, 0, c, s]
            reach = tiles[1, 0, c, s] - first_tile - row
            row = jnp.where(s < count[0, c], row, -1)
            live += jnp.where((tile_of == row) & (reach_of == reach), cutoff_sq, 0.0)
    copies[2].wait()
    for n in range(2):
        place = slice(rows + 8 * n, rows + 8 * n + 8)
        part = slice(n * half, (n + 1) * half)
        near_ref[place, :] = live[:, part]
        near_ref[rows + 8 * n : rows + 8 * n + 3, :] = pos[:, part]
    copies[3].wait()
    copies[4].wait()


def joined_places(near):
    rows = near.shape[0] - 16
    return jnp.concatenate([near[rows : rows + 8, :], near[rows + 8 :, :]], axis=1)


def split(x):
    high = x.astype(bf16)
    return high, (x - high.astype(f32)).astype(bf16)


def received_places(block):
    t = lax.axis_index("tile")
    missing = jnp.where(parity() == 0, t == 0, t == lax.axis_size("tile") - 1)
    row_of = lax.broadcasted_iota(jnp.int32, block.shape, 0)
    return jnp.where((row_of > 3) & missing, 0.0, block)


def spread_places(places):
    high, middle = split(places)
    low = (places - high.astype(f32) - middle.astype(f32)).astype(bf16)
    parts = jnp.concatenate([x.astype(f32) for x in (high, middle, low)], axis=0).astype(bf16)
    part_of = lax.broadcasted_iota(jnp.int32, (parts.shape[0], 3 * TILE_B), 0) % 8
    lane_of = lax.broadcasted_iota(jnp.int32, (parts.shape[0], 3 * TILE_B), 1) // TILE_B
    pick = jnp.where(part_of == lane_of, 1.0, 0.0).astype(bf16)
    return lax.dot_general(parts, pick, (((0,), (0,)), ((), ())), preferred_element_type=f32)


def tile_slice(w):
    return slice(w * TILE_B, (w + 1) * TILE_B)


def fill_pull(across, bound, wide, wide_base, pull, row, m):
    for q in range(0, TILE_B, CHUNK):
        down = slice(wide_base + q, wide_base + q + CHUNK)
        offset = [wide[down, tile_slice(c)] - across[c : c + 1, :] for c in range(3)]
        dist_sq = offset[0] * offset[0] + offset[1] * offset[1] + offset[2] * offset[2]
        falloff = jnp.maximum(bound - dist_sq, 0.0)
        weight = falloff * falloff / jnp.maximum(dist_sq, 1.0)
        place = slice(m * TILE_B + q, m * TILE_B + q + CHUNK)
        for c in range(3):
            pull[row, place, tile_slice(c)] = (weight * offset[c]).astype(bf16)


def by_parity(body):
    odd = parity()
    pl.when(odd == 0)(functools.partial(body, 0))
    pl.when(odd == 1)(functools.partial(body, 1))


class Tiles:
    def __init__(self, place):
        self.place = place

    def __call__(self, which, near):
        parts = []
        for w in near:
            refs, tile = self.place(w)
            parts.append(refs[which][:, tile_slice(refs.get("pos_tile", tile) if which == "pos" else tile)])
        return parts[0] if len(parts) == 1 else jnp.concatenate(parts, axis=1)

    def bound(self, w, j):
        reach = abs(w - j)
        return self("pos", [min(w, j)])[4 + reach : 5 + reach]


def sum_pulls(tiles, w, near, pull):
    middle = jnp.mean(tiles("pos", [w]), axis=1, keepdims=True)
    place = tiles("pos", near) - middle
    vec = tiles("vec", near)
    cols = vec.shape[0] // 3
    row_of = lax.broadcasted_iota(jnp.int32, place.shape, 0)
    extra = jnp.where(row_of < 3, place, jnp.where(row_of == 3, 1.0, 0.0))
    along = sum(place[d : d + 1] * vec[d * cols : (d + 1) * cols] for d in range(3))
    more_high, more_low = split(jnp.concatenate([along, extra, jnp.zeros_like(extra)], axis=0))
    left = jnp.concatenate([tiles("high", near), more_high, tiles("low", near), more_low], axis=0)
    n = left.shape[0] // 2
    first = near[0] - w + REACH
    part = slice(first * TILE_B, (first + len(near)) * TILE_B)
    total = jnp.dot(left, pull[part, :], preferred_element_type=f32)
    return total[0:n] + total[n:]


def from_sums(tiles, w, total):
    vec, pos = tiles("vec", [w]), tiles("pos", [w])
    rows = vec.shape[0]
    cols = rows // 3
    mine = pos - jnp.mean(pos, axis=1, keepdims=True)
    out = []
    for c in range(3):
        part = total[:, tile_slice(c)]
        e = rows + cols
        term = -part[rows:e]
        for d in range(3):
            diag = part[e + d : e + d + 1] - mine[d : d + 1] * part[e + 3 : e + 4]
            term += diag * vec[d * cols : (d + 1) * cols] + mine[d : d + 1] * part[d * cols : (d + 1) * cols]
        out.append(term * (spring_scale * step_size / cutoff_sq**2))
    return jnp.concatenate(out, axis=0)


def own_kernel(vec_ref, sent_ref, own_ref, pull, wide, high, low, part_ref, sem):
    rows, width = high.shape
    copy = pltpu.make_async_copy(vec_ref, own_ref.at[0:rows], sem)
    copy.start()
    own_ref[rows : rows + 8, :] = joined_places(sent_ref)
    tiles = width // TILE_B
    half = tiles // 2
    own = dict(vec=own_ref.at[0:rows], pos=own_ref.at[rows : rows + 8], high=high, low=low)
    mine = Tiles(lambda u: (own, u))
    wide[...] = spread_places(own["pos"][...])
    near = [range(max(0, u - REACH), min(tiles, u + REACH + 1)) for u in range(tiles)]
    for u in range(tiles):
        for j in near[u]:
            fill_pull(mine("pos", [u]), mine.bound(u, j), wide, j * TILE_B, pull, u + REACH, j - u + REACH)
    copy.wait()
    high[...], low[...] = split(own["vec"][...])

    def body(odd):
        for k in range(half):
            u = odd * half + k
            part_ref[k] = sum_pulls(mine, u, near[u], pull.at[u + REACH])

    by_parity(body)


def outer_kernel(own_ref, got_ref, wide_own, pull_in, pull, places, wide_got):
    width = wide_own.shape[0]
    rows = own_ref.shape[0] - 8
    tiles = width // TILE_B
    places[...] = received_places(joined_places(got_ref))
    wide_got[...] = spread_places(places[...])
    own = dict(pos=own_ref.at[rows : rows + 8], wide=wide_own)
    got = dict(pos=places, wide=wide_got)

    def body(odd):
        window = Tiles(lambda w: (got if w // tiles == odd else own, w % tiles))
        for r in range(tiles):
            w = r + REACH
            for j in range(w - REACH, w + REACH + 1):
                if w // tiles == odd or j // tiles == odd:
                    refs, tile = window.place(j)
                    across, bound = window("pos", [w]), window.bound(w, j)
                    fill_pull(across, bound, refs["wide"], tile * TILE_B, pull, r + odd * tiles, j - w + REACH)

    by_parity(body)


def halo_tiles(own, near, far, odd):
    rows, width = own["vec"].shape
    tiles = width // TILE_B
    half = tiles // 2

    def place(w):
        tile = w % tiles
        if w // tiles != odd:
            return own, tile
        return dict(far if tile // half == odd else near, pos_tile=tile), tile % half

    return Tiles(place)


def is_far(w, tiles, odd):
    return w // tiles == odd and w % tiles // (tiles // 2) == odd


def inner_kernel(own_ref, near_ref, places, high_own, low_own, part_ref, pull, out_ref, outer_ref, high, low):
    rows, width = high_own.shape
    tiles = width // TILE_B
    half = tiles // 2
    edge = half * TILE_B
    out_ref[rows : rows + 8, :] = places[:, 0:edge]
    out_ref[rows + 8 :, :] = places[:, edge:]
    high[...], low[...] = split(near_ref[0:rows, :])
    own = dict(vec=own_ref.at[0:rows], pos=own_ref.at[rows : rows + 8], high=high_own, low=low_own)
    got = dict(vec=near_ref.at[0:rows], pos=places, high=high, low=low)

    def body(odd):
        window = halo_tiles(own, got, None, odd)
        for r in range(tiles):
            w = r + REACH
            near = [j for j in range(w - REACH, w + REACH + 1) if not is_far(j, tiles, odd)]
            if w // tiles == odd:
                outer_ref[r % half] = sum_pulls(window, w, near, pull.at[r + odd * tiles])
            else:
                near = [j for j in near if j // tiles == odd]
                total = part_ref[r % half] + sum_pulls(window, w, near, pull.at[r + odd * tiles])
                out_ref[0:rows, tile_slice(r % half)] = from_sums(window, w, total)

    by_parity(body)


def outer_rows_kernel(own_ref, near_ref, far_ref, places, outer_ref, pull, out_ref, high, low):
    rows, width = own_ref.shape[0] - 8, own_ref.shape[1]
    tiles = width // TILE_B
    half = tiles // 2
    high[...], low[...] = split(far_ref[...])
    own = dict(vec=own_ref.at[0:rows])
    near_refs = dict(vec=near_ref.at[0:rows], pos=places)
    far_refs = dict(vec=far_ref, pos=places, high=high, low=low)

    def body(odd):
        window = halo_tiles(own, near_refs, far_refs, odd)
        for r in range(odd * half, (1 + odd) * half):
            w = r + REACH
            far = [j for j in range(w - REACH, w + REACH + 1) if is_far(j, tiles, odd)]
            total = outer_ref[r % half] + sum_pulls(window, w, far, pull.at[r + odd * tiles])
            out_ref[:, tile_slice(r % half)] = from_sums(window, w, total)

    by_parity(body)


def beside_tiles(own_pos, places, vectors, side):
    tiles = own_pos.shape[1] // TILE_B
    beside = dict(vectors, pos=places[1 - side])

    def place(w):
        if REACH <= w < tiles + REACH:
            return dict(pos=own_pos), w - REACH
        return beside, w if side == 0 else w - tiles - REACH

    return Tiles(place)


def beside_rows(tiles, side):
    half = tiles // 2
    there = range(REACH) if side == 0 else range(tiles + REACH, tiles + 2 * REACH)
    for u in range(side * half, (1 + side) * half):
        yield u, [j for j in there if abs(j - u - REACH) <= REACH]


def places_of(ref):
    rows = ref.shape[0] - 16
    return ref.at[rows : rows + 8], ref.at[rows + 8 :]


def own_sums_kernel(own_ref, prod_ref, outer_ref, pull, part_ref, edge_ref, high, low, high_outer, low_outer):
    rows, width = own_ref.shape[0] - 8, own_ref.shape[1]
    tiles = width // TILE_B
    half = tiles // 2
    own_pos = own_ref.at[rows : rows + 8]
    high[...], low[...] = split(prod_ref[0:rows, :])
    high_outer[...], low_outer[...] = split(outer_ref[...])

    def body(odd):
        inner = dict(vec=prod_ref.at[0:rows], high=high, low=low)
        for u, total in inner_sums(own_pos, inner, odd, pull):
            part_ref[u] = total
        ours = dict(vec=outer_ref, high=high_outer, low=low_outer)
        window = beside_tiles(own_pos, places_of(prod_ref), ours, odd)
        for u, near in beside_rows(tiles, odd):
            edge_ref[u % half] = sum_pulls(window, u + REACH, near, pull.at[u + REACH])

    by_parity(body)


def inner_sums(own_pos, inner, side, pull):
    tiles = own_pos.shape[1] // TILE_B
    half = tiles // 2
    window = Tiles(lambda u: (dict(inner, pos=own_pos, pos_tile=u), u % half))
    for u in range(tiles):
        near = [j for j in range(side * half, (1 + side) * half) if abs(j - u) <= REACH]
        yield u, sum_pulls(window, u, near, pull.at[u + REACH])


def middle_kernel(own_ref, prod_ref, got_ref, ours_ref, edge_ref, pull_in, mid_ref, part_ref, pull, high, low, wide):
    rows, width = mid_ref.shape
    tiles = width // TILE_B
    half = tiles // 2
    edge = width // 2
    own_pos = own_ref.at[rows : rows + 8]
    high[...], low[...] = split(got_ref[0:rows, :])

    def body(odd):
        side = 1 - odd
        mid_ref[:, odd * edge : (1 + odd) * edge] = prod_ref[0:rows, :]
        mid_ref[:, side * edge : (1 + side) * edge] = got_ref[0:rows, :]
        window = beside_tiles(own_pos, places_of(got_ref), {}, side)
        first = side * (tiles + REACH)
        wide[...] = spread_places(window("pos", range(first, first + REACH)))
        for u, near in beside_rows(tiles, side):
            w = u + REACH
            for j in near:
                fill_pull(window("pos", [w]), window.bound(w, j), wide, (j - first) * TILE_B, pull, w, j - w + REACH)
        inner = dict(vec=got_ref.at[0:rows], high=high, low=low)
        for u, total in inner_sums(own_pos, inner, side, pull):
            total = ours_ref[u] + total
            part_ref[u] = total + edge_ref[u % half] if u // half == odd else total

    by_parity(body)


def second_kernel(own_ref, mid_ref, got_ref, outer_ref, pull, sums_in, out_ref, gram_ref, sums, high, low):
    rows, width = mid_ref.shape
    cols = rows // 3
    tiles = width // TILE_B
    own_pos = own_ref.at[rows : rows + 8]
    high[...], low[...] = split(outer_ref[...])

    def body(odd):
        theirs = dict(vec=outer_ref, high=high, low=low)
        window = beside_tiles(own_pos, places_of(got_ref), theirs, 1 - odd)
        for u, near in beside_rows(tiles, 1 - odd):
            sums[u] = sums[u] + sum_pulls(window, u + REACH, near, pull.at[u + REACH])

    by_parity(body)
    own = dict(vec=mid_ref, pos=own_pos)
    mine = Tiles(lambda u: (own, u))
    for u in range(tiles):
        out_ref[:, tile_slice(u)] = from_sums(mine, u, sums[u])
    bands = [slice(d * cols, (d + 1) * cols) for d in range(3)]
    joint = jnp.concatenate(
        [jnp.concatenate([own_ref[band, :], mid_ref[band, :], out_ref[band, :]], axis=0) for band in bands], axis=1
    )
    parts = split(joint)
    both = jnp.concatenate(parts, axis=0)
    by_high, by_low = [
        lax.dot_general(both, part, (((1,), (1,)), ((), ())), preferred_element_type=f32) for part in parts
    ]
    gram = by_high[0:rows] + (by_high[rows:] + by_low[0:rows] + by_low[rows:])
    gram_ref[...] = jnp.zeros(gram_ref.shape, f32)
    gram_ref[:, 0:rows] = gram[0:cols]
    gram_ref[:, rows : 2 * rows] = gram[cols : 2 * cols]
    gram_ref[:, 2 * rows : 2 * rows + cols] = gram[2 * cols :, 2 * cols :]


def eliminate(joint, n):
    row_of = lax.broadcasted_iota(jnp.int32, joint.shape, 0)
    col = [jnp.broadcast_to(joint[:, j : j + 1], joint.shape) for j in range(n)]
    for k in range(n):
        inverse = 1.0 / col[k][k : k + 1]
        here = row_of == k
        factor = jnp.where(here, -1.0, col[k])
        joint = jnp.where(here, 0.0, joint) - factor * (joint[k : k + 1] * inverse)
        for j in range(k + 1, n):
            col[j] = jnp.where(here, 0.0, col[j]) - factor * (col[j][k : k + 1] * inverse)
    return joint


def mul(a, b):
    return jnp.dot(a, b, precision=highest, preferred_element_type=f32)


def turned(high, both, vec_high, vec_low):
    n = high.shape[1]
    first = lax.dot_general(both, vec_high, (((0,), (0,)), ((), ())), preferred_element_type=f32)
    return first[0:n] + (first[n:] + lax.dot_general(high, vec_low, (((0,), (0,)), ((), ())), preferred_element_type=f32))


def last_kernel(
    bead_scale,
    own_ref,
    prod_ref,
    quad_ref,
    gram_ref,
    out_ref,
    ray_ref,
    corr_ref,
    norm_ref,
    out,
    ray,
    small,
    norm,
    sems,
):
    rows, width = prod_ref.shape
    cols = rows // 3
    row_of = lax.broadcasted_iota(jnp.int32, (cols, cols), 0)
    col_of = lax.broadcasted_iota(jnp.int32, (cols, cols), 1)
    eye = jnp.where(row_of == col_of, 1.0, 0.0).astype(f32)
    xx, xp = gram_ref[:, 0:cols], gram_ref[:, cols : 2 * cols]
    pp, pq = gram_ref[:, rows + cols : rows + 2 * cols], gram_ref[:, rows + 2 * cols : 2 * rows]
    qq = gram_ref[:, 2 * rows : 2 * rows + cols]
    joint = eliminate(jnp.concatenate([gram_ref[:, 0:rows], gram_ref[:, rows : 2 * rows]], axis=0), cols)
    shift = joint[0:cols, cols : 2 * cols]
    rest = joint[cols:, cols : 2 * cols]
    cross = joint[cols:, 2 * cols :]
    corr = xx + rest
    side = xp - 2.0 * rest + cross
    gram = side - mul(rest, shift)
    turn = eye + shift
    squares = turn * (mul(pp, turn) - 2.0 * pq) + eye * qq
    ray[...] = gram * (bead_scale / step_size)
    small[...] = corr * bead_scale
    copies = [
        pltpu.make_async_copy(ray, ray_ref, sems.at[0]),
        pltpu.make_async_copy(small, corr_ref, sems.at[1]),
        pltpu.make_async_copy(norm, norm_ref, sems.at[2]),
    ]
    shift_high, shift_low = split(shift)
    shift_both = jnp.concatenate([shift_high, shift_low], axis=1)
    bands = [slice(d * cols, (d + 1) * cols) for d in range(3)]
    right = []
    for band in bands:
        vec, prod = own_ref[band, :], prod_ref[band, :]
        moved = turned(shift_high, shift_both, *split(vec))
        out[band, :] = vec - 2.0 * prod + quad_ref[band, :]
        right.append(split(jnp.concatenate([vec - prod, moved], axis=0)))
    both = eliminate(jnp.concatenate([corr, side + xp], axis=1), cols)[:, cols:]
    second = both - shift
    norm[...] = jnp.sum(squares - gram * second, axis=0, keepdims=True) * (bead_scale / step_size**2)
    factor_high, factor_low = split(jnp.concatenate([both, second], axis=0))
    factor_both = jnp.concatenate([factor_high, factor_low], axis=1)
    for d, band in enumerate(bands):
        out[band, :] += turned(factor_high, factor_both, *right[d])
        copies.append(pltpu.make_async_copy(out.at[band], out_ref.at[band], sems.at[3 + d]))
        if d == 0:
            for copy in copies:
                copy.start()
        else:
            copies[-1].start()
    for copy in copies:
        copy.wait()


def per_device(positions, trial_block, pair_tiles, pair_count):
    comps, cols, width = trial_block.shape
    rows = comps * cols
    n_tile, n_col = lax.axis_size("tile"), lax.axis_size("col")
    tiles = width // TILE_B
    assert tiles == 2 * REACH and n_col % 2 == 0
    bead_scale = 1.0 / (3.0 * n_tile * width)
    vmem = pl.BlockSpec(memory_space=pltpu.VMEM)
    smem = pl.BlockSpec(memory_space=pltpu.SMEM)
    params = pltpu.CompilerParams(vmem_limit_bytes=24 * 2**20)

    def swapped(x):
        return lax.ppermute(x, "col", [(c, c ^ 1) for c in range(n_col)])

    def f32_array(*shape):
        return jax.ShapeDtypeStruct(shape, f32)

    def bf16_array(*shape):
        return jax.ShapeDtypeStruct(shape, bf16)

    hbm = pl.BlockSpec(memory_space=pltpu.HBM)
    vectors, *tables = [
        pltpu.with_memory_space_constraint(x, pltpu.HBM)
        for x in (trial_block.reshape(rows, width), positions, pair_tiles, pair_count)
    ]
    near, far = pl.pallas_call(
        pack_kernel,
        out_shape=(f32_array(rows + 16, width // 2), f32_array(rows, width // 2)),
        in_specs=[hbm] * 4,
        out_specs=(vmem,) * 2,
        scratch_shapes=[
            pltpu.SMEM(pair_tiles.shape, jnp.int32),
            pltpu.SMEM(pair_count.shape, jnp.int32),
            pltpu.VMEM(positions.shape, f32),
            pltpu.SemaphoreType.DMA((5,)),
        ],
        compiler_params=pltpu.CompilerParams(vmem_limit_bytes=4 * 2**20),
        name="pack",
    )(vectors, *tables)

    halo = []
    for t in range(n_tile):
        for c in range(n_col):
            source = t - 1 if (c + t + 1) % 2 == 0 else t + 1
            if not 0 <= source < n_tile:
                source = t
            halo.append((source * n_col + (c ^ 1), t * n_col + c))
    got_near = lax.ppermute(near, ("tile", "col"), halo)
    got_far = lax.ppermute(far, ("tile", "col"), halo)

    parts = [pltpu.VMEM((rows, width), bf16)] * 2
    sums = (rows + cols + 16, 3 * TILE_B)
    pulls = bf16_array(2 * tiles, (2 * REACH + 1) * TILE_B, 3 * TILE_B)
    hidden = pl.CostEstimate(flops=10**8, bytes_accessed=10**6, transcendentals=0)
    own, pull, wide, high, low, part = pl.pallas_call(
        own_kernel,
        out_shape=(
            f32_array(rows + 8, width),
            pulls,
            f32_array(width, 3 * TILE_B),
            bf16_array(rows, width),
            bf16_array(rows, width),
            f32_array(tiles // 2, *sums),
        ),
        in_specs=[hbm, vmem],
        out_specs=(vmem,) * 6,
        scratch_shapes=[pltpu.SemaphoreType.DMA(())],
        compiler_params=params,
        cost_estimate=hidden,
        name="own_pulls",
    )(vectors, near)
    pull, places = pl.pallas_call(
        outer_kernel,
        out_shape=(pulls, f32_array(8, width)),
        in_specs=[vmem] * 4,
        out_specs=(vmem,) * 2,
        input_output_aliases={3: 0},
        scratch_shapes=[pltpu.VMEM((width, 3 * TILE_B), f32)],
        compiler_params=params,
        cost_estimate=hidden,
        name="outer_pulls",
    )(own, got_near, wide, pull)
    half_parts = [pltpu.VMEM((rows, width // 2), bf16)] * 2
    prod, outer = pl.pallas_call(
        inner_kernel,
        out_shape=(f32_array(rows + 16, width // 2), f32_array(tiles // 2, *sums)),
        in_specs=[vmem] * 7,
        out_specs=(vmem,) * 2,
        scratch_shapes=half_parts,
        compiler_params=params,
        cost_estimate=hidden,
        name="inner",
    )(own, got_near, places, high, low, part, pull)
    prod_got = swapped(prod)
    outer = pl.pallas_call(
        outer_rows_kernel,
        out_shape=f32_array(rows, width // 2),
        in_specs=[vmem] * 6,
        out_specs=vmem,
        scratch_shapes=half_parts,
        compiler_params=params,
        name="outer_rows",
    )(own, got_near, got_far, places, outer, pull)
    outer_got = swapped(outer)
    part, edge = pl.pallas_call(
        own_sums_kernel,
        out_shape=(f32_array(tiles, *sums), f32_array(tiles // 2, *sums)),
        in_specs=[vmem] * 4,
        out_specs=(vmem,) * 2,
        scratch_shapes=half_parts * 2,
        compiler_params=params,
        cost_estimate=hidden,
        name="own_sums",
    )(own, prod, outer, pull)
    mid, part, pull = pl.pallas_call(
        middle_kernel,
        out_shape=(f32_array(rows, width), f32_array(tiles, *sums), pulls),
        in_specs=[vmem] * 6,
        out_specs=(vmem,) * 3,
        input_output_aliases={5: 2},
        scratch_shapes=half_parts + [pltpu.VMEM((REACH * TILE_B, 3 * TILE_B), f32)],
        compiler_params=params,
        cost_estimate=hidden,
        name="middle",
    )(own, prod, prod_got, part, edge, pull)
    quad, gram, _ = pl.pallas_call(
        second_kernel,
        out_shape=(f32_array(rows, width), f32_array(cols, 128), f32_array(tiles, *sums)),
        in_specs=[vmem] * 6,
        out_specs=(vmem,) * 3,
        input_output_aliases={5: 2},
        scratch_shapes=half_parts,
        compiler_params=params,
        name="second",
    )(own, mid, prod_got, outer_got, pull, part)

    def crossed(x, step):
        route = [
            (t * n_col + c, (t ^ step) * n_col + (c ^ 1)) for t in range(n_tile) for c in range(n_col)
        ]
        return lax.ppermute(x, ("tile", "col"), route)

    step = 1
    while step < n_tile:
        if 2 * step < n_tile:
            near, far, both = [crossed(gram, s) for s in (step, 2 * step, 3 * step)]
            gram = (gram + near) + (far + both)
        else:
            gram = gram + crossed(gram, step)
        step *= 4
    shapes = [(rows, width), (cols, cols), (cols, cols), (1, cols)]
    block, ray, corr, norms = pl.pallas_call(
        functools.partial(last_kernel, bead_scale),
        out_shape=tuple(jax.ShapeDtypeStruct(shape, f32) for shape in shapes),
        in_specs=[vmem] * 4,
        out_specs=(hbm,) * 4,
        scratch_shapes=[pltpu.VMEM(shape, f32) for shape in shapes] + [pltpu.SemaphoreType.DMA((6,))],
        compiler_params=params,
        name="last",
    )(own, mid, quad, gram)
    return block.reshape(comps, cols, width), ray, corr, norms.reshape(cols)


def solution(mesh):
    return jax.shard_map(
        per_device,
        mesh=mesh,
        in_specs=(
            P(None, "tile"),
            P(None, None, "tile"),
            P(None, "tile", None, None),
            P("tile", None),
        ),
        out_specs=(P(None, None, "tile"), P(), P(), P()),
        check_vma=False,
    )
```
